32 devices in a mesh: batch: 16 (over z, y, x), tensor: 2 (over core).
Axes of the slice: x: 2, y: 2, z: 4, core: 2. Of those that a mesh axis runs over, the one named last changes fastest.
Arguments:
- tokens: bfloat16 [32768, 768], P('batch'), may hold values from -6 to 6
- lengths: int32 [64], P('batch'), may hold values from 64 to 512, as said below
- q_weight: float32 [768, 768], P('batch', 'tensor'), may hold values from -0.21875 to 0.21875
- k_weight: float32 [768, 768], P('batch', 'tensor'), may hold values from -0.21875 to 0.21875
- v_weight: float32 [768, 768], P('batch', 'tensor'), may hold values from -0.21875 to 0.21875
- output_weight: float32 [768, 768], P('tensor', 'batch'), may hold values from -0.875 to 0.875
- up_weight: float32 [768, 3072], P('batch', 'tensor'), may hold values from -0.21875 to 0.21875
- down_projection_weight: float32 [3072, 768], P('tensor', 'batch'), may hold values from -0.109375 to 0.109375
- q_bias: float32 [768], P('tensor'), may hold values from -3 to 3
- v_bias: float32 [768], P('tensor'), may hold values from -3 to 3
- o_bias: float32 [768], replicated, may hold values from -3 to 3
- up_bias: float32 [3072], P('tensor'), may hold values from -3 to 3
- down_bias: float32 [768], replicated, may hold values from -3 to 3
- gain_first: float32 [768], replicated, may hold values from 0.1 to 1.9
- shift_first: float32 [768], replicated, may hold values from -3 to 3
- gain_second: float32 [768], replicated, may hold values from 0.1 to 1.9
- shift_second: float32 [768], replicated, may hold values from -3 to 3
- out_grad: bfloat16 [32768, 768], P('batch'), may hold values from -6 to 6
Outputs:
- layer_out: bfloat16 [32768, 768], P('batch')
- tokens_grad: bfloat16 [32768, 768], P('batch')
- q_weight_grad: float32 [768, 768], P('batch', 'tensor')
- k_weight_grad: float32 [768, 768], P('batch', 'tensor')
- v_weight_grad: float32 [768, 768], P('batch', 'tensor')
- o_weight_grad: float32 [768, 768], P('tensor', 'batch')
- up_weight_grad: float32 [768, 3072], P('batch', 'tensor')
- down_weight_grad: float32 [3072, 768], P('tensor', 'batch')
- q_bias_grad: float32 [768], P('tensor')
- v_bias_grad: float32 [768], P('tensor')
- o_bias_grad: float32 [768], replicated
- up_bias_grad: float32 [3072], P('tensor')
- down_bias_grad: float32 [768], replicated
- gain_first_grad: float32 [768], replicated
- shift_first_grad: float32 [768], replicated
- gain_second_grad: float32 [768], replicated
- shift_second_grad: float32 [768], replicated
The draws below stay inside these ranges and needn't reach their ends.
Inputs may be any that keep to these rules, and one draw needn't show every extreme that they name: lengths[s] is the number of real tokens of sequence s, which stand first; some sequence has exactly 512.
All inputs are finite; a program needn't handle non-finite values.
Results may differ from the reference program's by a relative error of at most 0.019.
Values may be sent and summed in bfloat16 or wider, within the bound.
No kernel may reach another device: no remote copies, remote signals or barrier semaphores. Data moves between devices by JAX's collectives and lax.ppermute only.
A program may use at most 128 MiB of HBM per device.

```python
import math
import jax
import jax.numpy as jnp
from jax import lax

D = 768
HEAD_DIM = 64
FF = 3072
LEN = 512
SEQS = 64
TOKENS = 32768
N_TENSOR = 2


def draw_lengths(key, part):
    first, second = jax.random.split(jax.random.fold_in(key, 17))
    drawn = jax.random.randint(first, (SEQS,), max(1, LEN // 8), LEN + 1)
    longest = jax.random.randint(second, (), 0, SEQS)
    return jnp.where(jnp.arange(SEQS) == longest, LEN, drawn).astype(jnp.int32)


def strengthened(values, stream_key, source, target, blocks, factor):
    owner, partner = [(jnp.arange(values.shape[axis_at]) // (values.shape[axis_at] // blocks)).reshape([-1 if axis == axis_at else 1 for axis in range(values.ndim)]) for axis_at in (source, target)]
    chosen = jax.random.permutation(stream_key, blocks)[partner]
    strong = (owner == chosen) | (owner == (partner + blocks // 2) % blocks)
    return jnp.where(strong, factor * values, values)


def block_scale(rng, extent, pieces, least, top_value):
    level = 1.0
    for position, blocks in pieces:
        heights = jax.random.uniform(jax.random.fold_in(jax.random.fold_in(rng, 6), position), (blocks,), jnp.float32, least / len(pieces), top_value / len(pieces))
        level = level * jnp.repeat(jnp.exp(heights), extent[position] // blocks).reshape((-1,) + (1,) * (len(extent) - 1 - position))
    return level


def normal_values(rng, extent, scale, limit, cuts=(), held_as=jnp.bfloat16):
    values = jax.random.normal(rng, extent, jnp.float32) * scale
    if len(cuts) > 0:
        values = block_scale(rng, extent, cuts, -0.22, 0.18) * values
    return jnp.clip(values, min=-limit, max=limit).astype(held_as)


def bell_draw_with(key, shape, scale, reach, cuts, heavy, kind=jnp.bfloat16):
    values = scale * jax.random.normal(key, shape, jnp.float32)
    if cuts:
        values = values * block_scale(key, shape, cuts, -0.22, 0.18)
    return jnp.clip(strengthened(values, jax.random.fold_in(key, 3), *heavy), -reach, reach).astype(kind)


def setup_inputs(seed: int = 0) -> dict:
    streams_of = jax.random.split(jax.random.key(seed), 19)
    return {
        "tokens": bell_draw_with(streams_of[0], (TOKENS, D), 1.0, 6.0, ((0, 16),), (0, 1, 16, 2.0)),
        "lengths": draw_lengths(jax.random.fold_in(streams_of[18], 71), 0),
        "q_weight": normal_values(streams_of[2], (D, D), D ** -0.5, 0.21875, ((0, 16), (1, 2)), jnp.float32),
        "k_weight": normal_values(streams_of[3], (D, D), D ** -0.5, 0.21875, ((0, 16), (1, 2)), jnp.float32),
        "v_weight": normal_values(streams_of[4], (D, D), D ** -0.5, 0.21875, ((0, 16), (1, 2)), jnp.float32),
        "output_weight": normal_values(streams_of[5], (D, D), (D // 16) ** -0.5, 0.875, ((0, 2), (1, 16)), jnp.float32),
        "up_weight": normal_values(streams_of[6], (D, FF), D ** -0.5, 0.21875, ((0, 16), (1, 2)), jnp.float32),
        "down_projection_weight": normal_values(streams_of[7], (FF, D), FF ** -0.5, 0.109375, ((0, 2), (1, 16)), jnp.float32),
        "q_bias": normal_values(streams_of[8], (D,), 0.5, 3.0, ((0, 2),), jnp.float32),
        "v_bias": normal_values(streams_of[9], (D,), 0.5, 3.0, ((0, 2),), jnp.float32),
        "o_bias": normal_values(streams_of[10], (D,), 0.5, 3.0, (), jnp.float32),
        "up_bias": normal_values(streams_of[11], (FF,), 0.5, 3.0, ((0, 2),), jnp.float32),
        "down_bias": normal_values(streams_of[12], (D,), 0.5, 3.0, (), jnp.float32),
        "gain_first": jnp.clip(1.0 + 0.18 * jax.random.normal(streams_of[13], (D,), jnp.float32), 0.1, 1.9),
        "shift_first": normal_values(streams_of[14], (D,), 0.5, 3.0, (), jnp.float32),
        "gain_second": jnp.clip(1.0 + 0.18 * jax.random.normal(streams_of[15], (D,), jnp.float32), 0.1, 1.9),
        "shift_second": normal_values(streams_of[16], (D,), 0.5, 3.0, (), jnp.float32),
        "out_grad": bell_draw_with(streams_of[17], (TOKENS, D), 1.0, 6.0, ((0, 16),), (0, 1, 16, 2.0)),
    }


EPSILON = 1e-12
NEGATIVE = -1000000000.0
TOP_PRECISION = lax.Precision.HIGHEST

@jax.custom_vjp
def lowered_forward(v):
    return lax.optimization_barrier(v.astype(jnp.bfloat16)).astype(jnp.float32)

@jax.custom_vjp
def lowered_backward(v):
    return v

def low_keep(v):
    return (lowered_forward(v), None)

def low_pass(kept, grad):
    return (grad,)

def back_keep(v):
    return (v, None)

def back_low(kept, grad):
    return (lowered_forward(grad),)
lowered_forward.defvjp(low_keep, low_pass)
lowered_backward.defvjp(back_keep, back_low)

def layer_norm(values, gain, shift):
    center = values - lax.optimization_barrier(jnp.mean(values, -1, keepdims=True))
    inverse = lax.rsqrt(lax.optimization_barrier(jnp.mean(center * center, -1, keepdims=True)) + EPSILON)
    return center * inverse * gain + shift

def heads_of(flat, groups):
    rows, width = flat.shape
    return flat.reshape(groups, rows // groups, width // HEAD_DIM, HEAD_DIM).transpose(0, 2, 1, 3)

def split_columns(matrix):
    return matrix.reshape(matrix.shape[0], N_TENSOR, -1).transpose(1, 0, 2)

def divide_rows(matrix):
    return matrix.reshape(N_TENSOR, -1, matrix.shape[1])

def merge_columns(parts):
    return parts.transpose(1, 0, 2).reshape(parts.shape[1], -1)

def project(copies, matrix, bias):
    return jnp.einsum('trd,tde->tre', copies, split_columns(lowered_forward(matrix)), precision=TOP_PRECISION) + bias

def layer(params, inputs, valid):
    q_weight, k_weight, v_weight, output_weight, up_weight, down_projection_weight, q_bias, v_bias, o_bias, up_bias, down_bias, gain_first, shift_first, gain_second, shift_second = params
    groups = valid.shape[0]
    rows = inputs.shape[0]
    copies = lowered_backward(jnp.broadcast_to(inputs, (N_TENSOR,) + inputs.shape))
    query = lowered_forward(lowered_backward(project(copies, q_weight, q_bias.reshape(N_TENSOR, 1, -1))))
    keys = lowered_forward(lowered_backward(project(copies, k_weight, 0.0)))
    values = lowered_forward(lowered_backward(project(copies, v_weight, v_bias.reshape(N_TENSOR, 1, -1))))
    scores = jnp.einsum('ghqd,ghkd->ghqk', heads_of(merge_columns(query), groups), heads_of(merge_columns(keys), groups), precision=TOP_PRECISION) * HEAD_DIM ** (-0.5)
    scores = jnp.where(valid[:, None, None, :], lowered_backward(scores), NEGATIVE)
    probs = lowered_forward(jax.nn.softmax(scores, axis=-1))
    mixed = jnp.einsum('ghqk,ghkd->ghqd', probs, heads_of(merge_columns(values), groups), precision=TOP_PRECISION)
    mixed = lowered_forward(lowered_backward(mixed.transpose(0, 2, 1, 3).reshape(rows, -1)))
    mixed_pieces = mixed.reshape(rows, N_TENSOR, -1).transpose(1, 0, 2)
    attention_block = lax.optimization_barrier(jnp.sum(lowered_forward(lowered_backward(jnp.einsum('dxp,dpl->dxl', mixed_pieces, divide_rows(lowered_forward(output_weight)), precision=TOP_PRECISION))), 0))
    normed_first = layer_norm(inputs + attention_block + o_bias, gain_first, shift_first)
    spread = lowered_backward(jnp.broadcast_to(lowered_forward(normed_first), (N_TENSOR,) + normed_first.shape))
    upper = lowered_backward(project(spread, up_weight, up_bias.reshape(N_TENSOR, 1, -1)))
    active_rows = lowered_forward(jax.nn.gelu(upper, approximate=False))
    residual_branch = lax.optimization_barrier(jnp.sum(lowered_forward(lowered_backward(jnp.einsum('qji,qiw->qjw', active_rows, divide_rows(lowered_forward(down_projection_weight)), precision=TOP_PRECISION))), 0))
    return layer_norm(normed_first + residual_branch + down_bias, gain_second, shift_second)

def reference(tokens, lengths, q_weight, k_weight, v_weight, output_weight, up_weight, down_projection_weight, q_bias, v_bias, o_bias, up_bias, down_bias, gain_first, shift_first, gain_second, shift_second, out_grad):
    params = (q_weight, k_weight, v_weight, output_weight, up_weight, down_projection_weight, q_bias, v_bias, o_bias, up_bias, down_bias, gain_first, shift_first, gain_second, shift_second)
    seq_total = lengths.shape[0]
    span = tokens.shape[0] // seq_total
    bundle = math.gcd(seq_total, 8)
    rounds = seq_total // bundle
    width = tokens.shape[1]
    inputs = tokens.astype(jnp.float32).reshape(rounds, bundle * span, width)
    cotangents = out_grad.astype(jnp.float32).reshape(rounds, bundle * span, width)
    valid = (jnp.arange(span, dtype=jnp.int32)[None, :] < lengths[:, None]).reshape(rounds, bundle, span)

    def advance(total, item):
        block, cotangent, mask = item

        def forward(weights, rows_in):
            return layer(weights, rows_in, mask)
        output, pull = jax.vjp(forward, params, block)
        param_grads, input_grad = pull(cotangent)
        total = jax.tree.map(jnp.add, total, param_grads)
        return (total, (output.astype(jnp.bfloat16), input_grad.astype(jnp.bfloat16)))
    start = jax.tree.map(jnp.zeros_like, params)
    total, (outputs, input_grads) = lax.scan(advance, start, (inputs, cotangents, valid))
    g_query, g_key, g_value, g_out, g_up, g_down, g_qbias, g_vbias, g_obias, g_upbias, g_downbias, g_gain_first, g_shift_first, g_gain_second, g_shift_second = total
    return (outputs.reshape(-1, width), input_grads.reshape(-1, width), g_query, g_key, g_value, g_out, g_up, g_down, g_qbias, g_vbias, g_obias, g_upbias, g_downbias, g_gain_first, g_shift_first, g_gain_second, g_shift_second)
```

```python
import functools
import math

import jax
import jax.numpy as jnp
from jax import lax
from jax.experimental import pallas as pl
from jax.experimental.pallas import tpu as pltpu
from jax.sharding import PartitionSpec as P

HEAD_DIM = 64
LANES = 128
EPSILON = 1e-12
NEGATIVE = -1000000000.0
HALF = jnp.bfloat16
SINGLE = jnp.float32
SWAP = ((0, 1), (1, 0))


def matmul(left, right):
    return jnp.dot(left, right, preferred_element_type=SINGLE)


def inner_rows(left, right):
    return lax.dot_general(left, right, (((0,), (0,)), ((), ())), preferred_element_type=SINGLE)


def outer_cols(left, right):
    return lax.dot_general(left, right, (((1,), (1,)), ((), ())), preferred_element_type=SINGLE)


def layer_norm(values, gain, shift):
    center = values - jnp.mean(values, -1, keepdims=True)
    inverse = lax.rsqrt(jnp.mean(center * center, -1, keepdims=True) + EPSILON)
    normal = center * inverse
    return (normal * gain + shift, normal, inverse)


def norm_back(grad, normal, inverse, gain):
    scaled = grad * gain
    inner = (
        scaled
        - jnp.mean(scaled, -1, keepdims=True)
        - normal * jnp.mean(scaled * normal, -1, keepdims=True)
    )
    return inner * inverse


def gelu_parts(upper):
    cdf = 0.5 * (1.0 + lax.erf(upper * (1.0 / math.sqrt(2.0))))
    density = jnp.exp(-0.5 * upper * upper) * (1.0 / math.sqrt(2.0 * math.pi))
    return (upper * cdf, cdf + upper * density)


def head_sides():
    lane = lax.broadcasted_iota(jnp.int32, (1, LANES), 1)
    first = (lane < HEAD_DIM).astype(SINGLE)
    return (first.astype(HALF), (1.0 - first).astype(HALF))


def attend_kernel(len_ref, tok_ref, w_ref, b_ref, qkv_ref, mixed_ref, lse_ref):
    span = tok_ref.shape[0]
    width = mixed_ref.shape[1]
    length = len_ref[pl.program_id(0)]
    qkv_ref[...] = (matmul(tok_ref[...], w_ref[...]) + b_ref[...]).astype(HALF)
    sides = head_sides()
    keep = lax.broadcasted_iota(jnp.int32, (span, span), 0) < length
    for pair in range(width // LANES):
        at = LANES * pair
        query = qkv_ref[:, pl.ds(at, LANES)] * HALF(HEAD_DIM**-0.5)
        keys = qkv_ref[:, pl.ds(width + at, LANES)]
        values = qkv_ref[:, pl.ds(2 * width + at, LANES)]
        mixed = 0.0
        for h in range(2):
            scores = jnp.where(keep, outer_cols(keys * sides[h], query), NEGATIVE)
            top = jnp.max(scores, 0, keepdims=True)
            expo = jnp.exp(scores - top)
            total = jnp.sum(expo, 0, keepdims=True)
            lse_ref[0, 2 * pair + h : 2 * pair + h + 1, :] = top + jnp.log(total)
            mixed += inner_rows(values * sides[h], expo.astype(HALF)) * (1.0 / total)
        mixed_ref[:, pl.ds(at, LANES)] = mixed.T.astype(HALF)


def attend(lengths, tokens, weight, bias):
    rows, depth = tokens.shape
    seqs = lengths.shape[0]
    span = rows // seqs
    width = weight.shape[1] // 3
    heads = width // HEAD_DIM
    return pl.pallas_call(
        attend_kernel,
        grid_spec=pltpu.PrefetchScalarGridSpec(
            num_scalar_prefetch=1,
            grid=(seqs,),
            in_specs=[
                pl.BlockSpec((span, depth), lambda i, n: (i, 0)),
                pl.BlockSpec((depth, 3 * width), lambda i, n: (0, 0)),
                pl.BlockSpec((1, 3 * width), lambda i, n: (0, 0)),
            ],
            out_specs=[
                pl.BlockSpec((span, 3 * width), lambda i, n: (i, 0)),
                pl.BlockSpec((span, width), lambda i, n: (i, 0)),
                pl.BlockSpec((1, heads, span), lambda i, n: (i, 0, 0)),
            ],
        ),
        out_shape=[
            jax.ShapeDtypeStruct((rows, 3 * width), HALF),
            jax.ShapeDtypeStruct((rows, width), HALF),
            jax.ShapeDtypeStruct((seqs, heads, span), SINGLE),
        ],
        compiler_params=pltpu.CompilerParams(vmem_limit_bytes=40 << 20),
        cost_estimate=pl.CostEstimate(
            flops=30_000_000_000, bytes_accessed=8_000_000, transcendentals=0
        ),
        name="attend",
    )(lengths, tokens, weight, bias)


def attend_back_kernel(len_ref, qkv_ref, lse_ref, grad_ref, out_ref, bias_ref):
    span, width = grad_ref.shape
    step = pl.program_id(0)
    length = len_ref[step]
    sides = head_sides()
    keep = lax.broadcasted_iota(jnp.int32, (span, span), 0) < length

    @pl.when(step == 0)
    def _():
        bias_ref[...] = jnp.zeros_like(bias_ref)

    for pair in range(width // LANES):
        at = LANES * pair
        query = qkv_ref[:, pl.ds(at, LANES)] * HALF(HEAD_DIM**-0.5)
        keys = qkv_ref[:, pl.ds(width + at, LANES)]
        values = qkv_ref[:, pl.ds(2 * width + at, LANES)]
        grad = grad_ref[:, pl.ds(at, LANES)]
        query_grad = key_grad = value_grad = 0.0
        for h in range(2):
            side_keys = keys * sides[h]
            scores = jnp.where(keep, outer_cols(side_keys, query), NEGATIVE)
            probs = jnp.exp(scores - lse_ref[0, 2 * pair + h : 2 * pair + h + 1, :])
            value_grad += matmul(probs.astype(HALF), grad * sides[h])
            prob_grad = outer_cols(values * sides[h], grad)
            delta = jnp.sum(probs * prob_grad, 0, keepdims=True)
            score_grad = (probs * (prob_grad - delta)).astype(HALF)
            key_grad += matmul(score_grad, query * sides[h])
            query_grad += inner_rows(side_keys, score_grad)
        query_grad = (query_grad * HEAD_DIM**-0.5).T
        for j, grads in enumerate((query_grad, key_grad, value_grad)):
            out_ref[:, pl.ds(j * width + at, LANES)] = grads.astype(HALF)
            if j != 1:
                bias_ref[:, pl.ds(j * width + at, LANES)] += jnp.sum(grads, 0, keepdims=True)


def attend_back(lengths, qkv, lse, grad):
    rows, width = grad.shape
    seqs = lengths.shape[0]
    span = rows // seqs
    heads = width // HEAD_DIM
    return pl.pallas_call(
        attend_back_kernel,
        grid_spec=pltpu.PrefetchScalarGridSpec(
            num_scalar_prefetch=1,
            grid=(seqs,),
            in_specs=[
                pl.BlockSpec((span, 3 * width), lambda i, n: (i, 0)),
                pl.BlockSpec((1, heads, span), lambda i, n: (i, 0, 0)),
                pl.BlockSpec((span, width), lambda i, n: (i, 0)),
            ],
            out_specs=[
                pl.BlockSpec((span, 3 * width), lambda i, n: (i, 0)),
                pl.BlockSpec((1, 3 * width), lambda i, n: (0, 0)),
            ],
        ),
        out_shape=[
            jax.ShapeDtypeStruct((rows, 3 * width), HALF),
            jax.ShapeDtypeStruct((1, 3 * width), SINGLE),
        ],
        compiler_params=pltpu.CompilerParams(vmem_limit_bytes=40 << 20),
        cost_estimate=pl.CostEstimate(
            flops=32_000_000_000, bytes_accessed=8_000_000, transcendentals=0
        ),
        name="attend_back",
    )(lengths, qkv, lse, grad)


def middle_kernel(
    chunk,
    mix_a,
    mix_b,
    tok_ref,
    cot_ref,
    o_a,
    o_b,
    up_a,
    up_b,
    down_a,
    down_b,
    up_bias,
    vec_ref,
    out_ref,
    act_a,
    act_b,
    ugrad_a,
    ugrad_b,
    normed_ref,
    second_ref,
    first_ref,
    first_half_ref,
    mgrad_a,
    mgrad_b,
    vec_grad,
    up_bias_grad,
    slope_ref,
):
    @pl.when(pl.program_id(0) == 0)
    def _():
        vec_grad[...] = jnp.zeros_like(vec_grad)
        up_bias_grad[...] = jnp.zeros_like(up_bias_grad)

    o_bias, down_bias, gain_1, shift_1, gain_2, shift_2 = (
        vec_ref[j : j + 1, :] for j in range(6)
    )
    attention = outer_cols(mix_a[...], o_a[...]) + outer_cols(mix_b[...], o_b[...])
    normed, normal_1, inverse_1 = layer_norm(
        tok_ref[...].astype(SINGLE) + attention + o_bias, gain_1, shift_1
    )
    normed_half = normed.astype(HALF)
    normed_ref[...] = normed_half
    units = up_a.shape[1]
    branch = 0.0
    for half, (up, down, act) in enumerate(((up_a, down_a, act_a), (up_b, down_b, act_b))):
        for c in range(units // chunk):
            here = pl.ds(c * chunk, chunk)
            there = pl.ds(half * units + c * chunk, chunk)
            active, slope = gelu_parts(matmul(normed_half, up[:, here]) + up_bias[:, there])
            active = active.astype(HALF)
            act[:, here] = active
            slope_ref[:, there] = slope
            branch += outer_cols(active, down[:, here])
    output, normal_2, inverse_2 = layer_norm(normed + branch + down_bias, gain_2, shift_2)
    out_ref[...] = output.astype(HALF)
    cot = cot_ref[...].astype(SINGLE)
    second = norm_back(cot, normal_2, inverse_2, gain_2)
    second_half = second.astype(HALF)
    second_ref[...] = second_half
    normed_grad = second
    for half, (up, down, ugrad) in enumerate(((up_a, down_a, ugrad_a), (up_b, down_b, ugrad_b))):
        for c in range(units // chunk):
            here = pl.ds(c * chunk, chunk)
            there = pl.ds(half * units + c * chunk, chunk)
            upper_grad = matmul(second_half, down[:, here]) * slope_ref[:, there]
            up_bias_grad[:, there] += jnp.sum(upper_grad, 0, keepdims=True)
            upper_grad = upper_grad.astype(HALF)
            ugrad[:, here] = upper_grad
            normed_grad += outer_cols(upper_grad, up[:, here])
    first = norm_back(normed_grad, normal_1, inverse_1, gain_1)
    first_ref[...] = first
    first_half = first.astype(HALF)
    first_half_ref[...] = first_half
    mgrad_a[...] = matmul(first_half, o_a[...]).astype(HALF)
    mgrad_b[...] = matmul(first_half, o_b[...]).astype(HALF)
    sums = (first, second, normed_grad * normal_1, normed_grad, cot * normal_2, cot)
    for j, rows in enumerate(sums):
        vec_grad[j : j + 1, :] += jnp.sum(rows, 0, keepdims=True)


def middle(mixes, tokens, cotangent, o_halves, up_halves, down_halves, up_bias, vectors):
    rows, depth = tokens.shape
    width = mixes[0].shape[1]
    units = up_halves[0].shape[1]
    block = math.gcd(rows, 256)
    chunk = math.gcd(units, 768)
    wide = lambda columns: pl.BlockSpec((block, columns), lambda i: (i, 0))
    held = lambda a: pl.BlockSpec(a.shape, lambda i: (0, 0), pipeline_mode=pl.Buffered(1))
    kept = (*o_halves, *up_halves, *down_halves, up_bias, vectors)
    shape = jax.ShapeDtypeStruct
    return pl.pallas_call(
        functools.partial(middle_kernel, chunk),
        grid=(rows // block,),
        in_specs=[wide(width), wide(width), wide(depth), wide(depth)] + [held(a) for a in kept],
        out_specs=[wide(depth)]
        + [wide(units)] * 4
        + [wide(depth)] * 4
        + [wide(width)] * 2
        + [
            pl.BlockSpec((8, depth), lambda i: (0, 0)),
            pl.BlockSpec((1, 2 * units), lambda i: (0, 0)),
        ],
        out_shape=[shape((rows, depth), HALF)]
        + [shape((rows, units), HALF)] * 4
        + [shape((rows, depth), HALF)] * 2
        + [shape((rows, depth), SINGLE), shape((rows, depth), HALF)]
        + [shape((rows, width), HALF)] * 2
        + [shape((8, depth), SINGLE), shape((1, 2 * units), SINGLE)],
        scratch_shapes=[pltpu.VMEM((block, 2 * units), SINGLE)],
        compiler_params=pltpu.CompilerParams(vmem_limit_bytes=58 << 20),
        cost_estimate=pl.CostEstimate(
            flops=60_000_000_000, bytes_accessed=40_000_000, transcendentals=0
        ),
        name="middle",
    )(*mixes, tokens, cotangent, *kept)


def swap(array):
    return lax.ppermute(array, "tensor", SWAP)


def hop(array, distance, size):
    return lax.ppermute(array, "batch", [(i, i ^ distance) for i in range(size)])


def place_kernel(distances, me_ref, *refs):
    count = len(distances)
    blocks, outs, sems = refs[:count], refs[count:-1], refs[-1]
    rows = blocks[0].shape[0]
    copies = []
    for j, distance in enumerate(distances):
        at = pl.multiple_of((me_ref[0] ^ distance) * rows, rows)
        left = 0
        for n, out in enumerate(outs):
            columns = out.shape[1]
            copies.append(
                pltpu.make_async_copy(
                    blocks[j].at[:, pl.ds(left, columns)],
                    out.at[pl.ds(at, rows), :],
                    sems.at[j, n],
                )
            )
            left += columns
    for copy in copies:
        copy.start()
    for copy in copies:
        copy.wait()


def place(me, blocks, widths):
    distances = sorted(blocks)
    rows = blocks[0].shape[0]
    return pl.pallas_call(
        functools.partial(place_kernel, distances),
        grid_spec=pltpu.PrefetchScalarGridSpec(
            num_scalar_prefetch=1,
            grid=(1,),
            in_specs=[pl.BlockSpec(memory_space=pl.ANY)] * len(distances),
            out_specs=[pl.BlockSpec(memory_space=pl.ANY)] * len(widths),
            scratch_shapes=[pltpu.SemaphoreType.DMA((len(distances), len(widths)))],
        ),
        out_shape=[
            jax.ShapeDtypeStruct((len(distances) * rows, columns), HALF) for columns in widths
        ],
        compiler_params=pltpu.CompilerParams(vmem_limit_bytes=4 << 20),
        name="place",
    )(me.reshape(1), *[blocks[d] for d in distances])


def gather(me, size, part, widths):
    if size != 16:
        whole = lax.all_gather(part, "batch", axis=0, tiled=True)
        edges = [sum(widths[:n]) for n in range(1, len(widths))]
        return jnp.split(whole, edges, axis=1)
    blocks = {0: part}
    for z in (4, 8, 12):
        blocks[z] = hop(part, z, size)
    for z in (0, 4, 8, 12):
        blocks[z + 1] = hop(blocks[z], 1, size)
        blocks[z + 2] = hop(blocks[z], 2, size)
    for z in (0, 4):
        blocks[z + 3] = hop(blocks[z + 2], 1, size)
    for z in (8, 12):
        blocks[z + 3] = hop(blocks[z + 1], 2, size)
    return place(me, blocks, widths)


def scatter(me, size, whole):
    if size != 16:
        return lax.psum_scatter(whole.astype(SINGLE), "batch", scatter_dimension=0, tiled=True)
    x, y, z = me & 1, (me >> 1) & 1, me >> 2
    rows, columns = whole.shape
    whole = whole.reshape(4, 2, 2, rows // 16, columns)
    pick = lambda array, at, axis: lax.dynamic_index_in_dim(array, at, axis, keepdims=False)
    low, high = whole[:2], whole[2:]
    low_in = hop(pick(low, 1 - x, 2), 1, size)
    high_in = hop(pick(high, 1 - y, 1), 2, size)
    low = pick(low, x, 2) + low_in
    high = pick(high, y, 1) + high_in
    low_in = hop(pick(low, 1 - y, 1), 2, size)
    high_in = hop(pick(high, 1 - x, 1), 1, size)
    column = jnp.concatenate([pick(low, y, 1) + low_in, pick(high, x, 1) + high_in])
    total = pick(column, z, 0).astype(SINGLE)
    for d in (1, 2, 3):
        total += hop(pick(column, z ^ d, 0), 4 * d, size).astype(SINGLE)
    return total


def total_over_batch(size, vector):
    if size != 16:
        return lax.psum(vector, "batch")
    for d in (1, 2, 4, 8):
        vector = vector + hop(vector, d, size)
    return vector


def weight_grad(left, right_own, right_other):
    received = swap(inner_rows(left, right_other).astype(HALF))
    return (inner_rows(left, right_own) + received.astype(SINGLE)).astype(HALF)


def per_device(
    size,
    tokens,
    lengths,
    q_weight,
    k_weight,
    v_weight,
    output_weight,
    up_weight,
    down_projection_weight,
    q_bias,
    v_bias,
    o_bias,
    up_bias,
    down_bias,
    gain_first,
    shift_first,
    gain_second,
    shift_second,
    out_grad,
):
    me = lax.axis_index("batch")
    core = lax.axis_index("tensor")
    depth = tokens.shape[1]
    width = q_weight.shape[1]
    units = up_weight.shape[1]
    rows = tokens.shape[0] // 2
    seqs = lengths.shape[0] // 2

    qkv_part = jnp.concatenate([w.astype(HALF) for w in (q_weight, k_weight, v_weight)], 1)
    up_part = jnp.concatenate([output_weight.astype(HALF).T, up_weight.astype(HALF)], 1)
    down_part = down_projection_weight.astype(HALF).T
    tokens = lax.dynamic_slice_in_dim(tokens, core * rows, rows)
    cotangent = lax.dynamic_slice_in_dim(out_grad, core * rows, rows)
    lengths = lax.dynamic_slice_in_dim(lengths, core * seqs, seqs)
    biases = jnp.concatenate([q_bias, jnp.zeros_like(q_bias), v_bias, up_bias])
    other_biases = swap(biases)
    qkv_bias = [b[: 3 * width].reshape(1, -1) for b in (biases, other_biases)]
    up_biases = jnp.concatenate([b[3 * width :] for b in (biases, other_biases)]).reshape(1, -1)
    blank = jnp.zeros_like(o_bias)
    vectors = jnp.stack(
        [o_bias, down_bias, gain_first, shift_first, gain_second, shift_second, blank, blank]
    )

    (qkv_own,) = gather(me, size, qkv_part, (3 * width,))
    o_own, up_own = gather(me, size, up_part, (width, units))
    (down_own,) = gather(me, size, down_part, (units,))
    qkv_w = (qkv_own, swap(qkv_own))
    o_w = (o_own, swap(o_own))
    up_w = (up_own, swap(up_own))
    down_w = (down_own, swap(down_own))

    fronts = [attend(lengths, tokens, w, b) for w, b in zip(qkv_w, qkv_bias)]
    mixes = [front[1] for front in fronts]
    (
        output,
        act_own,
        act_other,
        ugrad_own,
        ugrad_other,
        normed,
        second,
        first,
        first_half,
        mgrad_own,
        mgrad_other,
        vec_grad,
        up_bias_grad,
    ) = middle(mixes, tokens, cotangent, o_w, up_w, down_w, up_biases, vectors)

    down_grad = weight_grad(second, act_own, act_other)
    up_grad = weight_grad(normed, ugrad_own, ugrad_other)
    o_grad = weight_grad(first_half, mixes[0], mixes[1])
    down_sum = scatter(me, size, down_grad)
    up_sum = scatter(me, size, up_grad)
    o_sum = scatter(me, size, o_grad)

    back_other, bias_other = attend_back(lengths, fronts[1][0], fronts[1][2], mgrad_other)
    back_own, bias_own = attend_back(lengths, fronts[0][0], fronts[0][2], mgrad_own)
    qkv_grad = weight_grad(tokens, back_own, back_other)
    qkv_sum = scatter(me, size, qkv_grad)

    shared = vec_grad[:6].reshape(-1)
    mine = jnp.concatenate([bias_own[0], up_bias_grad[0, :units], shared])
    theirs = jnp.concatenate([bias_other[0], up_bias_grad[0, units:], shared])
    small = total_over_batch(size, mine + swap(theirs))

    tokens_grad = (
        first + outer_cols(back_own, qkv_w[0]) + outer_cols(back_other, qkv_w[1])
    ).astype(HALF)

    def both(part):
        other = swap(part)
        low = jnp.where(core == 0, part, other)
        high = jnp.where(core == 0, other, part)
        return jnp.concatenate([low, high])

    edge = 3 * width + units
    o_bias_grad, down_bias_grad, gain_1, shift_1, gain_2, shift_2 = jnp.split(small[edge:], 6)
    return (
        both(output),
        both(tokens_grad),
        qkv_sum[:, :width],
        qkv_sum[:, width : 2 * width],
        qkv_sum[:, 2 * width :],
        o_sum.T,
        up_sum,
        down_sum.T,
        small[:width],
        small[2 * width : 3 * width],
        o_bias_grad,
        small[3 * width : edge],
        down_bias_grad,
        gain_1,
        shift_1,
        gain_2,
        shift_2,
    )


def solution(mesh):
    in_specs = (
        P("batch", None),
        P("batch"),
        P("batch", "tensor"),
        P("batch", "tensor"),
        P("batch", "tensor"),
        P("tensor", "batch"),
        P("batch", "tensor"),
        P("tensor", "batch"),
        P("tensor"),
        P("tensor"),
        P(),
        P("tensor"),
        P(),
        P(),
        P(),
        P(),
        P(),
        P("batch", None),
    )
    out_specs = (
        P("batch", None),
        P("batch", None),
        P("batch", "tensor"),
        P("batch", "tensor"),
        P("batch", "tensor"),
        P("tensor", "batch"),
        P("batch", "tensor"),
        P("tensor", "batch"),
        P("tensor"),
        P("tensor"),
        P(),
        P("tensor"),
        P(),
        P(),
        P(),
        P(),
        P(),
    )
    return jax.shard_map(
        functools.partial(per_device, mesh.shape["batch"]),
        mesh=mesh,
        in_specs=in_specs,
        out_specs=out_specs,
        check_vma=False,
    )
```

```python
import functools
import math

import jax
import jax.numpy as jnp
from jax import lax
from jax.experimental import pallas as pl
from jax.experimental.pallas import tpu as pltpu
from jax.sharding import PartitionSpec as P

HEAD_DIM = 64
LANES = 128
BLOCK = 256
CHUNK = 768
EPSILON = 1e-12
NEGATIVE = -1000000000.0
HALF = jnp.bfloat16
SINGLE = jnp.float32
SWAP = ((0, 1), (1, 0))


def matmul(left, right):
    return jnp.dot(left, right, preferred_element_type=SINGLE)


def inner_rows(left, right):
    return lax.dot_general(left, right, (((0,), (0,)), ((), ())), preferred_element_type=SINGLE)


def outer_cols(left, right):
    return lax.dot_general(left, right, (((1,), (1,)), ((), ())), preferred_element_type=SINGLE)


def layer_norm(values, gain, shift):
    center = values - jnp.mean(values, -1, keepdims=True)
    inverse = lax.rsqrt(jnp.mean(center * center, -1, keepdims=True) + EPSILON)
    normal = center * inverse
    return (normal * gain + shift, normal, inverse)


def norm_back(grad, normal, inverse, gain):
    scaled = grad * gain
    inner = (
        scaled
        - jnp.mean(scaled, -1, keepdims=True)
        - normal * jnp.mean(scaled * normal, -1, keepdims=True)
    )
    return inner * inverse


def gelu_parts(upper):
    cdf = 0.5 * (1.0 + lax.erf(upper * (1.0 / math.sqrt(2.0))))
    density = jnp.exp(-0.5 * upper * upper) * (1.0 / math.sqrt(2.0 * math.pi))
    return (upper * cdf, cdf + upper * density)


def clear_at_start(*refs):
    @pl.when(pl.program_id(0) == 0)
    def _():
        for ref in refs:
            ref[...] = jnp.zeros_like(ref)


SHORT = pl.CostEstimate(flops=1000, bytes_accessed=1000, transcendentals=0)


def owner(where_ref, z, first, second):
    core = where_ref[1]
    return where_ref[0] ^ (4 * z) ^ (first * (1 + core)) ^ (second * (2 - core))


def head_sides():
    lane = lax.broadcasted_iota(jnp.int32, (1, LANES), 1)
    first = (lane < HEAD_DIM).astype(SINGLE)
    return (first.astype(HALF), (1.0 - first).astype(HALF))


def attend_kernel(len_ref, tok_ref, w_ref, b_ref, qkv_ref, mixed_ref, lse_ref):
    span = tok_ref.shape[0]
    width = mixed_ref.shape[1]
    length = len_ref[pl.program_id(0)]
    qkv_ref[...] = (matmul(tok_ref[...], w_ref[...]) + b_ref[...]).astype(HALF)
    sides = head_sides()
    keep = lax.broadcasted_iota(jnp.int32, (span, span), 0) < length
    for pair in range(width // LANES):
        at = LANES * pair
        query = qkv_ref[:, pl.ds(at, LANES)] * HALF(HEAD_DIM**-0.5)
        keys = qkv_ref[:, pl.ds(width + at, LANES)]
        values = qkv_ref[:, pl.ds(2 * width + at, LANES)]
        mixed = 0.0
        for h in range(2):
            scores = jnp.where(keep, outer_cols(keys * sides[h], query), NEGATIVE)
            top = jnp.max(scores, 0, keepdims=True)
            expo = jnp.exp(scores - top)
            total = jnp.sum(expo, 0, keepdims=True)
            lse_ref[0, 2 * pair + h : 2 * pair + h + 1, :] = top + jnp.log(total)
            mixed += inner_rows(values * sides[h], expo.astype(HALF)) * (1.0 / total)
        mixed_ref[:, pl.ds(at, LANES)] = mixed.T.astype(HALF)


def attend(lengths, tokens, weight, bias):
    rows, depth = tokens.shape
    seqs = lengths.shape[0]
    span = rows // seqs
    width = weight.shape[1] // 3
    heads = width // HEAD_DIM
    return pl.pallas_call(
        attend_kernel,
        grid_spec=pltpu.PrefetchScalarGridSpec(
            num_scalar_prefetch=1,
            grid=(seqs,),
            in_specs=[
                pl.BlockSpec((span, depth), lambda i, n: (i, 0)),
                pl.BlockSpec((depth, 3 * width), lambda i, n: (0, 0)),
                pl.BlockSpec((1, 3 * width), lambda i, n: (0, 0)),
            ],
            out_specs=[
                pl.BlockSpec((span, 3 * width), lambda i, n: (i, 0)),
                pl.BlockSpec((span, width), lambda i, n: (i, 0)),
                pl.BlockSpec((1, heads, span), lambda i, n: (i, 0, 0)),
            ],
        ),
        out_shape=[
            jax.ShapeDtypeStruct((rows, 3 * width), HALF),
            jax.ShapeDtypeStruct((rows, width), HALF),
            jax.ShapeDtypeStruct((seqs, heads, span), SINGLE),
        ],
        compiler_params=pltpu.CompilerParams(vmem_limit_bytes=60 << 20),
        cost_estimate=SHORT,
        name="attend",
    )(lengths, tokens, weight, bias)


def attend_back_kernel(len_ref, qkv_ref, lse_ref, grad_ref, out_ref, bias_ref):
    span, width = grad_ref.shape
    step = pl.program_id(0)
    length = len_ref[step]
    sides = head_sides()
    keep = lax.broadcasted_iota(jnp.int32, (span, span), 0) < length

    @pl.when(step == 0)
    def _():
        bias_ref[...] = jnp.zeros_like(bias_ref)

    for pair in range(width // LANES):
        at = LANES * pair
        query = qkv_ref[:, pl.ds(at, LANES)] * HALF(HEAD_DIM**-0.5)
        keys = qkv_ref[:, pl.ds(width + at, LANES)]
        values = qkv_ref[:, pl.ds(2 * width + at, LANES)]
        grad = grad_ref[:, pl.ds(at, LANES)]
        query_grad = key_grad = value_grad = 0.0
        for h in range(2):
            side_keys = keys * sides[h]
            scores = jnp.where(keep, outer_cols(side_keys, query), NEGATIVE)
            probs = jnp.exp(scores - lse_ref[0, 2 * pair + h : 2 * pair + h + 1, :])
            value_grad += matmul(probs.astype(HALF), grad * sides[h])
            prob_grad = outer_cols(values * sides[h], grad)
            delta = jnp.sum(probs * prob_grad, 0, keepdims=True)
            score_grad = (probs * (prob_grad - delta)).astype(HALF)
            key_grad += matmul(score_grad, query * sides[h])
            query_grad += inner_rows(side_keys, score_grad)
        query_grad = (query_grad * HEAD_DIM**-0.5).T
        for j, grads in enumerate((query_grad, key_grad, value_grad)):
            out_ref[:, pl.ds(j * width + at, LANES)] = grads.astype(HALF)
            if j != 1:
                bias_ref[:, pl.ds(j * width + at, LANES)] += jnp.sum(grads, 0, keepdims=True)


def attend_back(lengths, qkv, lse, grad):
    rows, width = grad.shape
    seqs = lengths.shape[0]
    span = rows // seqs
    heads = width // HEAD_DIM
    return pl.pallas_call(
        attend_back_kernel,
        grid_spec=pltpu.PrefetchScalarGridSpec(
            num_scalar_prefetch=1,
            grid=(seqs,),
            in_specs=[
                pl.BlockSpec((span, 3 * width), lambda i, n: (i, 0)),
                pl.BlockSpec((1, heads, span), lambda i, n: (i, 0, 0)),
                pl.BlockSpec((span, width), lambda i, n: (i, 0)),
            ],
            out_specs=[
                pl.BlockSpec((span, 3 * width), lambda i, n: (i, 0)),
                pl.BlockSpec((1, 3 * width), lambda i, n: (0, 0)),
            ],
        ),
        out_shape=[
            jax.ShapeDtypeStruct((rows, 3 * width), HALF),
            jax.ShapeDtypeStruct((1, 3 * width), SINGLE),
        ],
        compiler_params=pltpu.CompilerParams(vmem_limit_bytes=60 << 20),
        cost_estimate=SHORT,
        name="attend_back",
    )(lengths, qkv, lse, grad)


def middle_kernel(
    chunk,
    mix_a,
    mix_b,
    tok_ref,
    cot_ref,
    ou_a,
    ou_b,
    down_a,
    down_b,
    up_bias,
    vec_ref,
    out_ref,
    act_a,
    act_b,
    ugrad_a,
    ugrad_b,
    normed_ref,
    second_ref,
    first_ref,
    mgrad_a,
    mgrad_b,
    vec_grad,
    up_bias_grad,
    slope_ref,
):
    clear_at_start(vec_grad, up_bias_grad)
    width = mix_a.shape[1]
    o_bias, down_bias, gain_1, shift_1, gain_2, shift_2 = (
        vec_ref[j : j + 1, :] for j in range(6)
    )
    attention = outer_cols(mix_a[...], ou_a[:, :width])
    attention += outer_cols(mix_b[...], ou_b[:, :width])
    normed, normal_1, inverse_1 = layer_norm(
        tok_ref[...].astype(SINGLE) + attention + o_bias, gain_1, shift_1
    )
    normed_half = normed.astype(HALF)
    normed_ref[...] = normed_half
    units = down_a.shape[1]
    branch = 0.0
    for half, (ou, down, act) in enumerate(((ou_a, down_a, act_a), (ou_b, down_b, act_b))):
        for c in range(units // chunk):
            here = pl.ds(c * chunk, chunk)
            there = pl.ds(half * units + c * chunk, chunk)
            upper = matmul(normed_half, ou[:, pl.ds(width + c * chunk, chunk)])
            active, slope = gelu_parts(upper + up_bias[:, there])
            active = active.astype(HALF)
            act[:, here] = active
            slope_ref[:, there] = slope
            branch += outer_cols(active, down[:, here])
    output, normal_2, inverse_2 = layer_norm(normed + branch + down_bias, gain_2, shift_2)
    out_ref[...] = output.astype(HALF)
    cot = cot_ref[...].astype(SINGLE)
    second = norm_back(cot, normal_2, inverse_2, gain_2)
    second_half = second.astype(HALF)
    second_ref[...] = second_half
    normed_grad = second
    for half, (ou, down, ugrad) in enumerate(((ou_a, down_a, ugrad_a), (ou_b, down_b, ugrad_b))):
        for c in range(units // chunk):
            here = pl.ds(c * chunk, chunk)
            there = pl.ds(half * units + c * chunk, chunk)
            upper_grad = matmul(second_half, down[:, here]) * slope_ref[:, there]
            up_bias_grad[:, there] += jnp.sum(upper_grad, 0, keepdims=True)
            upper_grad = upper_grad.astype(HALF)
            ugrad[:, here] = upper_grad
            normed_grad += outer_cols(upper_grad, ou[:, pl.ds(width + c * chunk, chunk)])
    first = norm_back(normed_grad, normal_1, inverse_1, gain_1)
    first_half = first.astype(HALF)
    first_ref[...] = first_half
    mgrad_a[...] = matmul(first_half, ou_a[:, :width]).astype(HALF)
    mgrad_b[...] = matmul(first_half, ou_b[:, :width]).astype(HALF)
    sums = (first, second, normed_grad * normal_1, normed_grad, cot * normal_2, cot)
    for j, rows in enumerate(sums):
        vec_grad[j : j + 1, :] += jnp.sum(rows, 0, keepdims=True)


def close_kernel(first, grad_a, grad_b, qkv_a, qkv_b, out):
    total = first[...].astype(SINGLE) + outer_cols(grad_a[...], qkv_a[...])
    out[...] = (total + outer_cols(grad_b[...], qkv_b[...])).astype(HALF)


def by_rows(kernel, name, streamed, held, outs, totals=(), scratch=()):
    rows = streamed[0].shape[0]
    block = math.gcd(rows, BLOCK)
    stream = lambda columns: pl.BlockSpec((block, columns), lambda i: (i, 0))
    shape = jax.ShapeDtypeStruct
    return pl.pallas_call(
        kernel,
        grid=(rows // block,),
        in_specs=[stream(a.shape[1]) for a in streamed]
        + [
            pl.BlockSpec(a.shape, lambda i: (0, 0), pipeline_mode=pl.Buffered(1)) for a in held
        ],
        out_specs=[stream(columns) for columns in outs]
        + [pl.BlockSpec(size, lambda i: (0, 0)) for size in totals],
        out_shape=[shape((rows, columns), HALF) for columns in outs]
        + [shape(size, SINGLE) for size in totals],
        scratch_shapes=[pltpu.VMEM((block, columns), SINGLE) for columns in scratch],
        compiler_params=pltpu.CompilerParams(vmem_limit_bytes=60 << 20),
        cost_estimate=SHORT,
        name=name,
    )(*streamed, *held)


def middle(mixes, tokens, cotangent, ou_halves, down_halves, up_bias, vectors):
    depth = tokens.shape[1]
    width = mixes[0].shape[1]
    units = down_halves[0].shape[1]
    return by_rows(
        functools.partial(middle_kernel, math.gcd(units, CHUNK)),
        "middle",
        (*mixes, tokens, cotangent),
        (*ou_halves, *down_halves, up_bias, vectors),
        [depth] + [units] * 4 + [depth] * 3 + [width] * 2,
        [(8, depth), (1, 2 * units)],
        [2 * units],
    )


def close(first, grads, qkv_halves):
    return by_rows(close_kernel, "close", (first, *grads), qkv_halves, [first.shape[1]])[0]


def swap(array):
    return lax.ppermute(array, "tensor", SWAP)


def hop(array, distance, size):
    return lax.ppermute(array, "batch", [(i, i ^ distance) for i in range(size)])


def pack_first_kernel(*refs):
    out = refs[-1]
    width = refs[0].shape[1]
    for j, ref in enumerate(refs[:-1]):
        out[:, j * width : (j + 1) * width] = ref[...].astype(HALF)


def pack_rest_kernel(o_ref, up_ref, down_ref, ou, down, pack):
    width = o_ref.shape[1]
    ou[:, :width] = o_ref[...].astype(HALF)
    ou[:, width:] = up_ref[...].astype(HALF)
    down[...] = down_ref[...].astype(HALF)
    pack[:, : ou.shape[1]] = ou[...]
    pack[:, ou.shape[1] :] = down[...]


def packed(size, qkv, o_turned, up_weight, down_turned):
    if size != 16:
        first = jnp.concatenate(qkv, 1).astype(HALF)
        ou = jnp.concatenate([o_turned, up_weight], 1).astype(HALF)
        return first, ou, down_turned.astype(HALF), None
    rows, units = up_weight.shape
    width = o_turned.shape[1]
    shape = lambda columns: jax.ShapeDtypeStruct((rows, columns), HALF)
    params = pltpu.CompilerParams(vmem_limit_bytes=60 << 20)
    first = pl.pallas_call(
        pack_first_kernel,
        out_shape=shape(3 * width),
        compiler_params=params,
        cost_estimate=SHORT,
        name="pack_first",
    )(*qkv)
    rest = pl.pallas_call(
        pack_rest_kernel,
        out_shape=[shape(width + units), shape(units), shape(width + 2 * units)],
        compiler_params=params,
        cost_estimate=SHORT,
        name="pack_rest",
    )(o_turned, up_weight, down_turned)
    return first, *rest


def place_kernel(moves, where_ref, *refs):
    blocks, out, sems = refs[:-2], refs[-2], refs[-1]
    rows = out.shape[0] // 16
    copies = []
    for j, (source, index, column, relative) in enumerate(moves):
        block = blocks[source].at[index] if len(blocks[source].shape) == 3 else blocks[source]
        at = pl.multiple_of(owner(where_ref, *relative) * rows, rows)
        copies.append(
            pltpu.make_async_copy(
                block.at[:, pl.ds(column, out.shape[1])], out.at[pl.ds(at, rows), :], sems.at[j]
            )
        )
    for copy in copies:
        copy.start()
    for copy in copies:
        copy.wait()


def place(where, blocks, moves, rows, columns):
    return pl.pallas_call(
        functools.partial(place_kernel, moves),
        grid_spec=pltpu.PrefetchScalarGridSpec(
            num_scalar_prefetch=1,
            grid=(1,),
            in_specs=[pl.BlockSpec(memory_space=pl.ANY)] * len(blocks),
            out_specs=pl.BlockSpec((16 * rows, columns), lambda i, n: (0, 0)),
            scratch_shapes=[pltpu.SemaphoreType.DMA((len(moves),))],
        ),
        out_shape=jax.ShapeDtypeStruct((16 * rows, columns), HALF),
        compiler_params=pltpu.CompilerParams(vmem_limit_bytes=60 << 20),
        cost_estimate=SHORT,
        name="place",
    )(where, *blocks)


def join_kernel(where_ref, mine, theirs, out):
    is_mine = pl.program_id(0) * 2 // pl.num_programs(0) == where_ref[1]

    @pl.when(is_mine)
    def _():
        out[...] = mine[...]

    @pl.when(jnp.logical_not(is_mine))
    def _():
        out[...] = theirs[...]


def join(where, mine, theirs):
    rows, columns = mine.shape
    block = math.gcd(rows, 512)
    steps = rows // block

    def spec(other):
        first = lambda w: (w[1] ^ other) * steps
        return pl.BlockSpec(
            (block, columns), lambda i, w: (jnp.clip(i - first(w), 0, steps - 1), 0)
        )

    return pl.pallas_call(
        join_kernel,
        grid_spec=pltpu.PrefetchScalarGridSpec(
            num_scalar_prefetch=1,
            grid=(2 * steps,),
            in_specs=[spec(0), spec(1)],
            out_specs=pl.BlockSpec((block, columns), lambda i, w: (i, 0)),
        ),
        out_shape=jax.ShapeDtypeStruct((2 * rows, columns), HALF),
        compiler_params=pltpu.CompilerParams(vmem_limit_bytes=60 << 20),
        cost_estimate=SHORT,
        name="join",
    )(where, mine, theirs)


def after(array, *others):
    return lax.optimization_barrier((array, *others))[0]


def meet(*arrays):
    return lax.optimization_barrier(arrays)


def cross(array, turn, size):
    pairs = [(2 * i + c, 2 * (i ^ (1 + (c ^ turn))) + c) for i in range(size) for c in (0, 1)]
    return lax.ppermute(array, ("batch", "tensor"), pairs)


class Quad:
    def __init__(self, size, part):
        self.size, self.part = size, part
        self.one = self.two = None

    def first(self):
        if self.size == 16:
            self.one = cross(self.part, 0, self.size)

    def second(self):
        if self.size == 16:
            self.two = cross(jnp.stack([self.part, self.one]), 1, self.size)

    def moves(self, source, left):
        pieces = [self.part, self.one, self.two]
        places = ((0, None, (0, 0, 0)), (1, None, (0, 1, 0)), (2, 0, (0, 0, 1)), (2, 1, (0, 1, 1)))
        return pieces, [(source + n, index, left, place) for n, index, place in places]


class Gather:
    def __init__(self, where, size, part, quad=None, left=0):
        self.where, self.size, self.part = where, size, part
        self.quad, self.left = quad, left
        self.came = []

    def over_z(self, *steps):
        if self.size == 16:
            self.came = [*self.came, *(hop(self.part, 4 * z, self.size) for z in steps)]

    def first(self):
        if self.size != 16:
            return self.part
        self.column = jnp.stack(self.came if self.quad else [self.part, *self.came])
        self.came = cross(self.column, 0, self.size)
        return self.column

    def second(self):
        if self.size != 16:
            return self.part
        self.pair = jnp.concatenate([self.column, self.came])
        self.came = cross(self.pair, 1, self.size)
        return self.pair

    def whole(self):
        if self.size != 16:
            return lax.all_gather(self.part, "batch", axis=0, tiled=True)
        pieces = [self.pair, self.came]
        count = self.column.shape[0]
        moves = [
            (n, count * f + j, 0, (j + 4 - count, f, n))
            for n in (0, 1)
            for f in (0, 1)
            for j in range(count)
        ]
        if self.quad:
            more, others = self.quad.moves(2, self.left)
            pieces, moves = pieces + more, moves + others
        return place(self.where, pieces, moves, *self.part.shape)


def own_grad_kernel(counts, where_ref, *refs):
    n = len(counts)
    lefts, rights, received, outs, summed = (
        refs[:n],
        refs[n : 2 * n],
        refs[2 * n : 3 * n],
        refs[3 * n : -1],
        refs[-1],
    )
    step = pl.program_id(0)
    start = 0
    for left, right, got, count in zip(lefts, rights, received, counts):

        @pl.when((step >= start) & (step < start + count))
        def _(left=left, right=right, got=got):
            grads = inner_rows(left[...], right[...]) + got[...].astype(SINGLE)
            summed[...] = grads.astype(HALF)

        start += count
    rows = outs[0].shape[1]
    for j in range(16):
        at = pl.multiple_of(owner(where_ref, j % 4, j // 8, j // 4 % 2) * rows, rows)
        outs[1 - j // 8][j % 8] = summed[pl.ds(at, rows), :]


def own_grad(where, pairs, received):
    rows, depth = pairs[0][0].shape
    widths = [right.shape[1] for _, right in pairs]
    chunk = math.gcd(*widths, 768) if len(widths) == 1 else math.gcd(*widths)
    counts = [width // chunk for width in widths]
    starts = [sum(counts[:j]) for j in range(len(counts))]

    def spec(height, j):
        last = counts[j] - 1
        return pl.BlockSpec(
            (height, chunk), lambda c, m: (0, jnp.clip(c - starts[j], 0, last))
        )

    block = depth // 16
    return pl.pallas_call(
        functools.partial(own_grad_kernel, counts),
        grid_spec=pltpu.PrefetchScalarGridSpec(
            num_scalar_prefetch=1,
            grid=(sum(counts),),
            in_specs=[
                pl.BlockSpec((rows, depth), lambda c, m: (0, 0), pipeline_mode=pl.Buffered(1))
                for _ in pairs
            ]
            + [spec(rows, j) for j in range(len(pairs))]
            + [spec(depth, j) for j in range(len(pairs))],
            out_specs=[pl.BlockSpec((8, block, chunk), lambda c, m: (0, 0, c))] * 2,
            scratch_shapes=[pltpu.VMEM((depth, chunk), HALF)],
        ),
        out_shape=[jax.ShapeDtypeStruct((8, block, sum(widths)), HALF)] * 2,
        compiler_params=pltpu.CompilerParams(vmem_limit_bytes=60 << 20),
        cost_estimate=SHORT,
        name="own_grad",
    )(where, *[left for left, _ in pairs], *[right for _, right in pairs], *received)


class Scatter:
    def __init__(self, where, size, others):
        self.where, self.size = where, size
        self.sent = [inner_rows(left, right).astype(HALF) for left, right in others]
        self.came = [swap(grads) for grads in self.sent]

    def first(self, pairs):
        if self.size != 16:
            parts = [
                inner_rows(*pair) + part.astype(SINGLE) for pair, part in zip(pairs, self.came)
            ]
            self.kept = jnp.concatenate(parts, 1)
            return self.kept
        sent, self.kept = own_grad(self.where, pairs, self.came)
        self.came = cross(sent, 0, self.size)
        return sent

    def second(self):
        if self.size != 16:
            return self.kept
        half = self.kept.shape[0] // 2
        sent = self.kept[half:] + self.came[half:]
        self.kept = self.kept[:half] + self.came[:half]
        self.came = cross(sent, 1, self.size)
        return sent

    def third(self):
        if self.size != 16:
            return self.kept
        total = self.kept + self.came
        self.kept = total[0]
        self.came = [hop(total[z], 4 * z, self.size) for z in (1, 2, 3)]
        return total

    def result(self):
        if self.size != 16:
            return lax.psum_scatter(self.kept, "batch", scatter_dimension=0, tiled=True)
        return sum((a.astype(SINGLE) for a in self.came), self.kept.astype(SINGLE))


class Total:
    def __init__(self, size, mine, theirs):
        self.size, self.sum, self.came = size, mine, swap(theirs)

    def over(self, distance):
        if self.size == 16:
            self.sum = self.sum + self.came
            self.came = hop(self.sum, distance, self.size)

    def over_z(self):
        if self.size == 16:
            self.sum = self.sum + self.came
            self.came = [hop(self.sum, 4 * z, self.size) for z in (1, 2, 3)]

    def result(self):
        if self.size != 16:
            return lax.psum(self.sum + self.came, "batch")
        one, two, three = self.came
        return (self.sum + one) + (two + three)


def per_device(
    size,
    tokens,
    lengths,
    q_weight,
    k_weight,
    v_weight,
    output_weight,
    up_weight,
    down_projection_weight,
    q_bias,
    v_bias,
    o_bias,
    up_bias,
    down_bias,
    gain_first,
    shift_first,
    gain_second,
    shift_second,
    out_grad,
):
    me = lax.axis_index("batch")
    core = lax.axis_index("tensor")
    depth = tokens.shape[1]
    width = q_weight.shape[1]
    units = up_weight.shape[1]
    rows = tokens.shape[0] // 2
    seqs = lengths.shape[0] // 2

    qkv_part, ou_part, down_part, pack = packed(
        size, (q_weight, k_weight, v_weight), output_weight.T, up_weight, down_projection_weight.T
    )
    tokens = lax.dynamic_slice_in_dim(tokens, core * rows, rows)
    cotangent = lax.dynamic_slice_in_dim(out_grad, core * rows, rows)
    lengths = lax.dynamic_slice_in_dim(lengths, core * seqs, seqs)
    biases = jnp.concatenate([q_bias, jnp.zeros_like(q_bias), v_bias, up_bias])
    other_biases = swap(biases)
    qkv_bias = [b[: 3 * width].reshape(1, -1) for b in (biases, other_biases)]
    up_biases = jnp.concatenate([b[3 * width :] for b in (biases, other_biases)]).reshape(1, -1)
    blank = jnp.zeros_like(o_bias)
    vectors = jnp.stack(
        [o_bias, down_bias, gain_first, shift_first, gain_second, shift_second, blank, blank]
    )

    where = jnp.stack([me, core]).astype(jnp.int32)

    quad = Quad(size, pack)
    qkv = Gather(where, size, qkv_part)
    ou = Gather(where, size, ou_part, quad, 0)
    down = Gather(where, size, down_part, quad, ou_part.shape[1])
    qkv.over_z(1, 2, 3)
    quad.first()
    qkv.came, quad.one, ou.part, down.part = meet(qkv.came, quad.one, ou.part, down.part)
    ou.over_z(1, 2)
    qkv.first()
    quad.second()
    qkv.came, quad.two, ou.came, ou.part = meet(qkv.came, quad.two, ou.came, ou.part)
    ou.over_z(3)
    qkv.second()
    qkv.came, ou.came, down.part, *sliced = meet(
        qkv.came, ou.came, down.part, tokens, cotangent, vectors, qkv_bias, up_biases
    )
    tokens, cotangent, vectors, qkv_bias, up_biases = sliced
    qkv_own = qkv.whole()
    column = ou.first()
    down.over_z(1, 2, 3)
    qkv_w = (qkv_own, swap(qkv_own))
    front_own = attend(lengths, tokens, after(qkv_own, column), qkv_bias[0])
    front_own, ou.came, down.came, qkv_other = meet(front_own, ou.came, down.came, qkv_w[1])
    pair = ou.second()
    column = down.first()
    front_other = attend(lengths, tokens, after(qkv_other, pair, column), qkv_bias[1])
    front_other, ou.came, down.came = meet(front_other, ou.came, down.came)
    pair = down.second()
    ou.came = after(ou.came, pair)
    ou_own = ou.whole()
    ou_own, down.came = meet(ou_own, down.came)
    ou_w = (ou_own, swap(ou_own))
    mixes = (front_own[1], front_other[1])
    down_own = down.whole()
    down_w = (down_own, swap(down_own))
    (
        output,
        *acts,
        ugrad_own,
        ugrad_other,
        normed,
        second,
        first,
        mgrad_own,
        mgrad_other,
        vec_sums,
        unit_sums,
    ) = middle(mixes, tokens, cotangent, ou_w, down_w, up_biases, vectors)
    output_came = swap(output)
    down = Scatter(where, size, [(second, acts[1])])
    first = after(first, *down.sent)
    ou = Scatter(where, size, [(first, mixes[1]), (normed, ugrad_other)])
    down.came = after(down.came, *ou.sent)
    sent = down.first([(second, acts[0])])
    back_other, bias_other = attend_back(
        lengths, front_other[0], front_other[2], after(mgrad_other, sent)
    )
    qkv = Scatter(where, size, [(tokens, back_other)])
    down.came, qkv.sent = meet(down.came, qkv.sent)
    sent = down.second()
    ou.came = after(ou.came, sent)
    sent = ou.first([(first, mixes[0]), (normed, ugrad_own)])
    down.came, sent = meet(down.came, sent)
    total = down.third()
    back_own, bias_own = attend_back(
        lengths, front_own[0], front_own[2], after(mgrad_own, sent, total)
    )
    shared = vec_sums[:6].reshape(-1)
    small = Total(
        size,
        jnp.concatenate([bias_own[0], unit_sums[0, :units], shared]),
        jnp.concatenate([bias_other[0], unit_sums[0, units:], shared]),
    )
    back_own, qkv.came, down.came = meet(back_own, qkv.came, down.came)
    sent = qkv.first([(tokens, back_own)])
    small.came, ou.came = meet(after(small.came, sent), ou.came)
    small.over(1)
    sent = ou.second()
    tokens_grad = close(after(first, sent, small.sum), (back_own, back_other), qkv_w)
    down_sum = down.result()
    tokens_grad, qkv.came, small.came = meet(tokens_grad, qkv.came, small.came)
    small.over(2)
    sent = qkv.second()
    ou.came = after(ou.came, sent)
    total = ou.third()
    tokens_grad_came = swap(tokens_grad)
    output = join(where, output, after(output_came, total))
    output, qkv.came, small.came = meet(output, qkv.came, small.came)
    small.over_z()
    total = qkv.third()
    tokens_grad = join(where, after(tokens_grad, total), tokens_grad_came)
    tokens_grad, ou.came = meet(tokens_grad, ou.came)
    ou_sum = ou.result()
    qkv.came = after(qkv.came, ou_sum)
    qkv_sum, small = qkv.result(), small.result()

    edge = 3 * width + units
    o_bias_grad, down_bias_grad, gain_1, shift_1, gain_2, shift_2 = jnp.split(small[edge:], 6)
    return (
        output,
        tokens_grad,
        qkv_sum[:, :width],
        qkv_sum[:, width : 2 * width],
        qkv_sum[:, 2 * width :],
        ou_sum[:, :width].T,
        ou_sum[:, width:],
        down_sum.T,
        small[:width],
        small[2 * width : 3 * width],
        o_bias_grad,
        small[3 * width : edge],
        down_bias_grad,
        gain_1,
        shift_1,
        gain_2,
        shift_2,
    )


def solution(mesh):
    in_specs = (
        P("batch", None),
        P("batch"),
        P("batch", "tensor"),
        P("batch", "tensor"),
        P("batch", "tensor"),
        P("tensor", "batch"),
        P("batch", "tensor"),
        P("tensor", "batch"),
        P("tensor"),
        P("tensor"),
        P(),
        P("tensor"),
        P(),
        P(),
        P(),
        P(),
        P(),
        P("batch", None),
    )
    out_specs = (
        P("batch", None),
        P("batch", None),
        P("batch", "tensor"),
        P("batch", "tensor"),
        P("batch", "tensor"),
        P("tensor", "batch"),
        P("batch", "tensor"),
        P("tensor", "batch"),
        P("tensor"),
        P("tensor"),
        P(),
        P("tensor"),
        P(),
        P(),
        P(),
        P(),
        P(),
    )
    return jax.shard_map(
        functools.partial(per_device, mesh.shape["batch"]),
        mesh=mesh,
        in_specs=in_specs,
        out_specs=out_specs,
        check_vma=False,
    )
```

```python
import functools
import math

import jax
import jax.numpy as jnp
from jax import lax
from jax.experimental import pallas as pl
from jax.experimental.pallas import tpu as pltpu
from jax.sharding import PartitionSpec as P

HEAD_DIM = 64
LANES = 128
BLOCK = 256
CHUNK = 768
EPSILON = 1e-12
NEGATIVE = -1000000000.0
HALF = jnp.bfloat16
SINGLE = jnp.float32
SWAP = ((0, 1), (1, 0))


def matmul(left, right):
    return jnp.dot(left, right, preferred_element_type=SINGLE)


def inner_rows(left, right):
    return lax.dot_general(left, right, (((0,), (0,)), ((), ())), preferred_element_type=SINGLE)


def outer_cols(left, right):
    return lax.dot_general(left, right, (((1,), (1,)), ((), ())), preferred_element_type=SINGLE)


def layer_norm(values, gain, shift):
    center = values - jnp.mean(values, -1, keepdims=True)
    inverse = lax.rsqrt(jnp.mean(center * center, -1, keepdims=True) + EPSILON)
    normal = center * inverse
    return (normal * gain + shift, normal, inverse)


def norm_back(grad, normal, inverse, gain):
    scaled = grad * gain
    inner = (
        scaled
        - jnp.mean(scaled, -1, keepdims=True)
        - normal * jnp.mean(scaled * normal, -1, keepdims=True)
    )
    return inner * inverse


def gelu_parts(upper):
    cdf = 0.5 * (1.0 + lax.erf(upper * (1.0 / math.sqrt(2.0))))
    density = jnp.exp(-0.5 * upper * upper) * (1.0 / math.sqrt(2.0 * math.pi))
    return (upper * cdf, cdf + upper * density)


def clear_at_start(*refs):
    @pl.when(pl.program_id(0) == 0)
    def _():
        for ref in refs:
            ref[...] = jnp.zeros_like(ref)


SHORT = pl.CostEstimate(flops=1000, bytes_accessed=1000, transcendentals=0)


def owner(where_ref, z, first, second):
    core = where_ref[1]
    return where_ref[0] ^ (4 * z) ^ (first * (1 + core)) ^ (second * (2 - core))


def head_sides():
    lane = lax.broadcasted_iota(jnp.int32, (1, LANES), 1)
    first = (lane < HEAD_DIM).astype(SINGLE)
    return (first.astype(HALF), (1.0 - first).astype(HALF))


def attend_kernel(len_ref, tok_ref, w_ref, b_ref, qkv_ref, mixed_ref, lse_ref):
    span = tok_ref.shape[0]
    width = mixed_ref.shape[1]
    length = len_ref[pl.program_id(0)]
    qkv_ref[...] = (matmul(tok_ref[...], w_ref[...]) + b_ref[...]).astype(HALF)
    sides = head_sides()
    keep = lax.broadcasted_iota(jnp.int32, (span, span), 0) < length
    for pair in range(width // LANES):
        at = LANES * pair
        query = qkv_ref[:, pl.ds(at, LANES)] * HALF(HEAD_DIM**-0.5)
        keys = qkv_ref[:, pl.ds(width + at, LANES)]
        values = qkv_ref[:, pl.ds(2 * width + at, LANES)]
        mixed = 0.0
        for h in range(2):
            scores = jnp.where(keep, outer_cols(keys * sides[h], query), NEGATIVE)
            top = jnp.max(scores, 0, keepdims=True)
            expo = jnp.exp(scores - top)
            total = jnp.sum(expo, 0, keepdims=True)
            lse_ref[0, 2 * pair + h : 2 * pair + h + 1, :] = top + jnp.log(total)
            mixed += inner_rows(values * sides[h], expo.astype(HALF)) * (1.0 / total)
        mixed_ref[:, pl.ds(at, LANES)] = mixed.T.astype(HALF)


def attend(lengths, tokens, weight, bias):
    rows, depth = tokens.shape
    seqs = lengths.shape[0]
    span = rows // seqs
    width = weight.shape[1] // 3
    heads = width // HEAD_DIM
    return pl.pallas_call(
        attend_kernel,
        grid_spec=pltpu.PrefetchScalarGridSpec(
            num_scalar_prefetch=1,
            grid=(seqs,),
            in_specs=[
                pl.BlockSpec((span, depth), lambda i, n: (i, 0)),
                pl.BlockSpec((depth, 3 * width), lambda i, n: (0, 0)),
                pl.BlockSpec((1, 3 * width), lambda i, n: (0, 0)),
            ],
            out_specs=[
                pl.BlockSpec((span, 3 * width), lambda i, n: (i, 0)),
                pl.BlockSpec((span, width), lambda i, n: (i, 0)),
                pl.BlockSpec((1, heads, span), lambda i, n: (i, 0, 0)),
            ],
        ),
        out_shape=[
            jax.ShapeDtypeStruct((rows, 3 * width), HALF),
            jax.ShapeDtypeStruct((rows, width), HALF),
            jax.ShapeDtypeStruct((seqs, heads, span), SINGLE),
        ],
        compiler_params=pltpu.CompilerParams(vmem_limit_bytes=60 << 20),
        cost_estimate=SHORT,
        name="attend",
    )(lengths, tokens, weight, bias)


def attend_back_kernel(len_ref, qkv_ref, lse_ref, grad_ref, out_ref, bias_ref):
    span, width = grad_ref.shape
    step = pl.program_id(0)
    length = len_ref[step]
    sides = head_sides()
    keep = lax.broadcasted_iota(jnp.int32, (span, span), 0) < length

    @pl.when(step == 0)
    def _():
        bias_ref[...] = jnp.zeros_like(bias_ref)

    for pair in range(width // LANES):
        at = LANES * pair
        query = qkv_ref[:, pl.ds(at, LANES)] * HALF(HEAD_DIM**-0.5)
        keys = qkv_ref[:, pl.ds(width + at, LANES)]
        values = qkv_ref[:, pl.ds(2 * width + at, LANES)]
        grad = grad_ref[:, pl.ds(at, LANES)]
        query_grad = key_grad = value_grad = 0.0
        for h in range(2):
            side_keys = keys * sides[h]
            scores = jnp.where(keep, outer_cols(side_keys, query), NEGATIVE)
            probs = jnp.exp(scores - lse_ref[0, 2 * pair + h : 2 * pair + h + 1, :])
            value_grad += matmul(probs.astype(HALF), grad * sides[h])
            prob_grad = outer_cols(values * sides[h], grad)
            delta = jnp.sum(probs * prob_grad, 0, keepdims=True)
            score_grad = (probs * (prob_grad - delta)).astype(HALF)
            key_grad += matmul(score_grad, query * sides[h])
            query_grad += inner_rows(side_keys, score_grad)
        query_grad = (query_grad * HEAD_DIM**-0.5).T
        for j, grads in enumerate((query_grad, key_grad, value_grad)):
            out_ref[:, pl.ds(j * width + at, LANES)] = grads.astype(HALF)
            if j != 1:
                bias_ref[:, pl.ds(j * width + at, LANES)] += jnp.sum(grads, 0, keepdims=True)


def attend_back(lengths, qkv, lse, grad):
    rows, width = grad.shape
    seqs = lengths.shape[0]
    span = rows // seqs
    heads = width // HEAD_DIM
    return pl.pallas_call(
        attend_back_kernel,
        grid_spec=pltpu.PrefetchScalarGridSpec(
            num_scalar_prefetch=1,
            grid=(seqs,),
            in_specs=[
                pl.BlockSpec((span, 3 * width), lambda i, n: (i, 0)),
                pl.BlockSpec((1, heads, span), lambda i, n: (i, 0, 0)),
                pl.BlockSpec((span, width), lambda i, n: (i, 0)),
            ],
            out_specs=[
                pl.BlockSpec((span, 3 * width), lambda i, n: (i, 0)),
                pl.BlockSpec((1, 3 * width), lambda i, n: (0, 0)),
            ],
        ),
        out_shape=[
            jax.ShapeDtypeStruct((rows, 3 * width), HALF),
            jax.ShapeDtypeStruct((1, 3 * width), SINGLE),
        ],
        compiler_params=pltpu.CompilerParams(vmem_limit_bytes=60 << 20),
        cost_estimate=SHORT,
        name="attend_back",
    )(lengths, qkv, lse, grad)


def middle_kernel(
    chunk,
    mix_a,
    mix_b,
    tok_ref,
    cot_ref,
    ou_a,
    ou_b,
    down_a,
    down_b,
    up_bias,
    vec_ref,
    out_ref,
    act_a,
    act_b,
    ugrad_a,
    ugrad_b,
    normed_ref,
    second_ref,
    first_ref,
    mgrad_a,
    mgrad_b,
    vec_grad,
    up_bias_grad,
    slope_ref,
):
    clear_at_start(vec_grad, up_bias_grad)
    width = mix_a.shape[1]
    o_bias, down_bias, gain_1, shift_1, gain_2, shift_2 = (
        vec_ref[j : j + 1, :] for j in range(6)
    )
    attention = outer_cols(mix_a[...], ou_a[:, :width])
    attention += outer_cols(mix_b[...], ou_b[:, :width])
    normed, normal_1, inverse_1 = layer_norm(
        tok_ref[...].astype(SINGLE) + attention + o_bias, gain_1, shift_1
    )
    normed_half = normed.astype(HALF)
    normed_ref[...] = normed_half
    units = down_a.shape[1]
    branch = 0.0
    for half, (ou, down, act) in enumerate(((ou_a, down_a, act_a), (ou_b, down_b, act_b))):
        for c in range(units // chunk):
            here = pl.ds(c * chunk, chunk)
            there = pl.ds(half * units + c * chunk, chunk)
            upper = matmul(normed_half, ou[:, pl.ds(width + c * chunk, chunk)])
            active, slope = gelu_parts(upper + up_bias[:, there])
            active = active.astype(HALF)
            act[:, here] = active
            slope_ref[:, there] = slope
            branch += outer_cols(active, down[:, here])
    output, normal_2, inverse_2 = layer_norm(normed + branch + down_bias, gain_2, shift_2)
    out_ref[...] = output.astype(HALF)
    cot = cot_ref[...].astype(SINGLE)
    second = norm_back(cot, normal_2, inverse_2, gain_2)
    second_half = second.astype(HALF)
    second_ref[...] = second_half
    normed_grad = second
    for half, (ou, down, ugrad) in enumerate(((ou_a, down_a, ugrad_a), (ou_b, down_b, ugrad_b))):
        for c in range(units // chunk):
            here = pl.ds(c * chunk, chunk)
            there = pl.ds(half * units + c * chunk, chunk)
            upper_grad = matmul(second_half, down[:, here]) * slope_ref[:, there]
            up_bias_grad[:, there] += jnp.sum(upper_grad, 0, keepdims=True)
            upper_grad = upper_grad.astype(HALF)
            ugrad[:, here] = upper_grad
            normed_grad += outer_cols(upper_grad, ou[:, pl.ds(width + c * chunk, chunk)])
    first = norm_back(normed_grad, normal_1, inverse_1, gain_1)
    first_half = first.astype(HALF)
    first_ref[...] = first_half
    mgrad_a[...] = matmul(first_half, ou_a[:, :width]).astype(HALF)
    mgrad_b[...] = matmul(first_half, ou_b[:, :width]).astype(HALF)
    sums = (first, second, normed_grad * normal_1, normed_grad, cot * normal_2, cot)
    for j, rows in enumerate(sums):
        vec_grad[j : j + 1, :] += jnp.sum(rows, 0, keepdims=True)


def close_kernel(first, grad_a, grad_b, qkv_a, qkv_b, out):
    total = first[...].astype(SINGLE) + outer_cols(grad_a[...], qkv_a[...])
    out[...] = (total + outer_cols(grad_b[...], qkv_b[...])).astype(HALF)


def by_rows(kernel, name, streamed, held, outs, totals=(), scratch=()):
    rows = streamed[0].shape[0]
    block = math.gcd(rows, BLOCK)
    stream = lambda columns: pl.BlockSpec((block, columns), lambda i: (i, 0))
    shape = jax.ShapeDtypeStruct
    return pl.pallas_call(
        kernel,
        grid=(rows // block,),
        in_specs=[stream(a.shape[1]) for a in streamed]
        + [
            pl.BlockSpec(a.shape, lambda i: (0, 0), pipeline_mode=pl.Buffered(1)) for a in held
        ],
        out_specs=[stream(columns) for columns in outs]
        + [pl.BlockSpec(size, lambda i: (0, 0)) for size in totals],
        out_shape=[shape((rows, columns), HALF) for columns in outs]
        + [shape(size, SINGLE) for size in totals],
        scratch_shapes=[pltpu.VMEM((block, columns), SINGLE) for columns in scratch],
        compiler_params=pltpu.CompilerParams(vmem_limit_bytes=60 << 20),
        cost_estimate=SHORT,
        name=name,
    )(*streamed, *held)


def middle(mixes, tokens, cotangent, ou_halves, down_halves, up_bias, vectors):
    depth = tokens.shape[1]
    width = mixes[0].shape[1]
    units = down_halves[0].shape[1]
    return by_rows(
        functools.partial(middle_kernel, math.gcd(units, CHUNK)),
        "middle",
        (*mixes, tokens, cotangent),
        (*ou_halves, *down_halves, up_bias, vectors),
        [depth] + [units] * 4 + [depth] * 3 + [width] * 2,
        [(8, depth), (1, 2 * units)],
        [2 * units],
    )


def close(first, grads, qkv_halves):
    return by_rows(close_kernel, "close", (first, *grads), qkv_halves, [first.shape[1]])[0]


def swap(array):
    return lax.ppermute(array, "tensor", SWAP)


def hop(array, distance, size):
    return lax.ppermute(array, "batch", [(i, i ^ distance) for i in range(size)])


def pack_first_kernel(*refs):
    out = refs[-1]
    width = refs[0].shape[1]
    for j, ref in enumerate(refs[:-1]):
        out[:, j * width : (j + 1) * width] = ref[...].astype(HALF)


def pack_rest_kernel(o_ref, up_ref, down_ref, ou, down, pack):
    width = o_ref.shape[1]
    ou[:, :width] = o_ref[...].astype(HALF)
    ou[:, width:] = up_ref[...].astype(HALF)
    down[...] = down_ref[...].astype(HALF)
    pack[:, : ou.shape[1]] = ou[...]
    pack[:, ou.shape[1] :] = down[...]


def packed(size, qkv, o_turned, up_weight, down_turned):
    if size != 16:
        first = jnp.concatenate(qkv, 1).astype(HALF)
        ou = jnp.concatenate([o_turned, up_weight], 1).astype(HALF)
        return first, ou, down_turned.astype(HALF), None
    rows, units = up_weight.shape
    width = o_turned.shape[1]
    shape = lambda columns: jax.ShapeDtypeStruct((rows, columns), HALF)
    params = pltpu.CompilerParams(vmem_limit_bytes=60 << 20)
    first = pl.pallas_call(
        pack_first_kernel,
        out_shape=shape(3 * width),
        compiler_params=params,
        cost_estimate=SHORT,
        name="pack_first",
    )(*qkv)
    rest = pl.pallas_call(
        pack_rest_kernel,
        out_shape=[shape(width + units), shape(units), shape(width + 2 * units)],
        compiler_params=params,
        cost_estimate=SHORT,
        name="pack_rest",
    )(o_turned, up_weight, down_turned)
    return first, *rest


def place_kernel(moves, where_ref, *refs):
    blocks, out, sems = refs[:-2], refs[-2], refs[-1]
    rows = out.shape[0] // 16
    copies = []
    for j, (source, index, column, relative) in enumerate(moves):
        block = blocks[source].at[index] if len(blocks[source].shape) == 3 else blocks[source]
        at = pl.multiple_of(owner(where_ref, *relative) * rows, rows)
        copies.append(
            pltpu.make_async_copy(
                block.at[:, pl.ds(column, out.shape[1])], out.at[pl.ds(at, rows), :], sems.at[j]
            )
        )
    for copy in copies:
        copy.start()
    for copy in copies:
        copy.wait()


def place(where, blocks, moves, rows, columns):
    return pl.pallas_call(
        functools.partial(place_kernel, moves),
        grid_spec=pltpu.PrefetchScalarGridSpec(
            num_scalar_prefetch=1,
            grid=(1,),
            in_specs=[pl.BlockSpec(memory_space=pl.ANY)] * len(blocks),
            out_specs=pl.BlockSpec((16 * rows, columns), lambda i, n: (0, 0)),
            scratch_shapes=[pltpu.SemaphoreType.DMA((len(moves),))],
        ),
        out_shape=jax.ShapeDtypeStruct((16 * rows, columns), HALF),
        compiler_params=pltpu.CompilerParams(vmem_limit_bytes=60 << 20),
        cost_estimate=SHORT,
        name="place",
    )(where, *blocks)


def join_kernel(where_ref, mine, theirs, out):
    is_mine = pl.program_id(0) * 2 // pl.num_programs(0) == where_ref[1]

    @pl.when(is_mine)
    def _():
        out[...] = mine[...]

    @pl.when(jnp.logical_not(is_mine))
    def _():
        out[...] = theirs[...]


def join(where, mine, theirs):
    rows, columns = mine.shape
    block = math.gcd(rows, 512)
    steps = rows // block

    def spec(other):
        first = lambda w: (w[1] ^ other) * steps
        return pl.BlockSpec(
            (block, columns), lambda i, w: (jnp.clip(i - first(w), 0, steps - 1), 0)
        )

    return pl.pallas_call(
        join_kernel,
        grid_spec=pltpu.PrefetchScalarGridSpec(
            num_scalar_prefetch=1,
            grid=(2 * steps,),
            in_specs=[spec(0), spec(1)],
            out_specs=pl.BlockSpec((block, columns), lambda i, w: (i, 0)),
        ),
        out_shape=jax.ShapeDtypeStruct((2 * rows, columns), HALF),
        compiler_params=pltpu.CompilerParams(vmem_limit_bytes=60 << 20),
        cost_estimate=SHORT,
        name="join",
    )(where, mine, theirs)


def after(array, *others):
    return lax.optimization_barrier((array, *others))[0]


def meet(*arrays):
    return lax.optimization_barrier(arrays)


def cross(array, turn, size):
    pairs = [(2 * i + c, 2 * (i ^ (1 + (c ^ turn))) + c) for i in range(size) for c in (0, 1)]
    return lax.ppermute(array, ("batch", "tensor"), pairs)


class Quad:
    def __init__(self, size, part):
        self.size, self.part = size, part
        self.one = self.two = None

    def first(self):
        if self.size == 16:
            self.one = cross(self.part, 0, self.size)

    def second(self):
        if self.size == 16:
            self.two = cross(jnp.stack([self.part, self.one]), 1, self.size)

    def moves(self, source, left):
        pieces = [self.part, self.one, self.two]
        places = ((0, None, (0, 0, 0)), (1, None, (0, 1, 0)), (2, 0, (0, 0, 1)), (2, 1, (0, 1, 1)))
        return pieces, [(source + n, index, left, place) for n, index, place in places]


class Gather:
    def __init__(self, where, size, part, quad=None, left=0):
        self.where, self.size, self.part = where, size, part
        self.quad, self.left = quad, left
        self.came = []

    def over_z(self, *steps):
        if self.size == 16:
            self.came = [*self.came, *(hop(self.part, 4 * z, self.size) for z in steps)]

    def first(self):
        if self.size != 16:
            return self.part
        self.column = jnp.stack(self.came if self.quad else [self.part, *self.came])
        self.came = cross(self.column, 0, self.size)
        return self.column

    def second(self):
        if self.size != 16:
            return self.part
        self.pair = jnp.concatenate([self.column, self.came])
        self.came = cross(self.pair, 1, self.size)
        return self.pair

    def whole(self):
        if self.size != 16:
            return lax.all_gather(self.part, "batch", axis=0, tiled=True)
        pieces = [self.pair, self.came]
        count = self.column.shape[0]
        moves = [
            (n, count * f + j, 0, (j + 4 - count, f, n))
            for n in (0, 1)
            for f in (0, 1)
            for j in range(count)
        ]
        if self.quad:
            more, others = self.quad.moves(2, self.left)
            pieces, moves = pieces + more, moves + others
        return place(self.where, pieces, moves, *self.part.shape)


def own_grad_kernel(counts, where_ref, *refs):
    n = len(counts)
    lefts, rights, received, outs, summed = (
        refs[:n],
        refs[n : 2 * n],
        refs[2 * n : 3 * n],
        refs[3 * n : -1],
        refs[-1],
    )
    step = pl.program_id(0)
    start = 0
    for left, right, got, count in zip(lefts, rights, received, counts):

        @pl.when((step >= start) & (step < start + count))
        def _(left=left, right=right, got=got):
            grads = inner_rows(left[...], right[...]) + got[...].astype(SINGLE)
            summed[...] = grads.astype(HALF)

        start += count
    rows = outs[0].shape[1]
    for j in range(16):
        at = pl.multiple_of(owner(where_ref, j % 4, j // 8, j // 4 % 2) * rows, rows)
        outs[1 - j // 8][j % 8] = summed[pl.ds(at, rows), :]


def own_grad(where, pairs, received):
    rows, depth = pairs[0][0].shape
    widths = [right.shape[1] for _, right in pairs]
    chunk = math.gcd(*widths, 768) if len(widths) == 1 else math.gcd(*widths)
    counts = [width // chunk for width in widths]
    starts = [sum(counts[:j]) for j in range(len(counts))]

    def spec(height, j):
        last = counts[j] - 1
        return pl.BlockSpec(
            (height, chunk), lambda c, m: (0, jnp.clip(c - starts[j], 0, last))
        )

    block = depth // 16
    return pl.pallas_call(
        functools.partial(own_grad_kernel, counts),
        grid_spec=pltpu.PrefetchScalarGridSpec(
            num_scalar_prefetch=1,
            grid=(sum(counts),),
            in_specs=[
                pl.BlockSpec((rows, depth), lambda c, m: (0, 0), pipeline_mode=pl.Buffered(1))
                for _ in pairs
            ]
            + [spec(rows, j) for j in range(len(pairs))]
            + [spec(depth, j) for j in range(len(pairs))],
            out_specs=[pl.BlockSpec((8, block, chunk), lambda c, m: (0, 0, c))] * 2,
            scratch_shapes=[pltpu.VMEM((depth, chunk), HALF)],
        ),
        out_shape=[jax.ShapeDtypeStruct((8, block, sum(widths)), HALF)] * 2,
        compiler_params=pltpu.CompilerParams(vmem_limit_bytes=60 << 20),
        cost_estimate=SHORT,
        name="own_grad",
    )(where, *[left for left, _ in pairs], *[right for _, right in pairs], *received)


class Scatter:
    def __init__(self, where, size, others):
        self.where, self.size = where, size
        self.sent = [inner_rows(left, right).astype(HALF) for left, right in others]
        self.came = [swap(grads) for grads in self.sent]

    def make(self, pairs):
        if self.size != 16:
            parts = [
                inner_rows(*pair) + part.astype(SINGLE) for pair, part in zip(pairs, self.came)
            ]
            self.made = [jnp.concatenate(parts, 1)]
        else:
            self.made = own_grad(self.where, pairs, self.came)
        return self.made

    def first(self):
        self.kept = self.made[-1]
        if self.size == 16:
            self.came = cross(self.made[0], 0, self.size)

    def second(self):
        if self.size != 16:
            return self.kept
        half = self.kept.shape[0] // 2
        sent = self.kept[half:] + self.came[half:]
        self.kept = self.kept[:half] + self.came[:half]
        self.came = cross(sent, 1, self.size)
        return sent

    def third(self):
        if self.size != 16:
            return self.kept
        total = self.kept + self.came
        self.kept = total[0]
        self.came = [hop(total[z], 4 * z, self.size) for z in (1, 2, 3)]
        return total

    def near_z(self):
        if self.size != 16:
            return self.kept
        sent = self.kept[1::2] + self.came[1::2]
        self.kept = self.kept[::2] + self.came[::2]
        self.came = hop(sent, 4, self.size)
        return sent

    def far_z(self):
        if self.size != 16:
            return self.kept
        sent = self.kept[1] + self.came[1]
        self.kept = self.kept[0] + self.came[0]
        self.came = [hop(sent, 8, self.size)]
        return sent

    def result(self):
        if self.size != 16:
            return lax.psum_scatter(self.kept, "batch", scatter_dimension=0, tiled=True)
        return sum((a.astype(SINGLE) for a in self.came), self.kept.astype(SINGLE))


class Total:
    def __init__(self, size, mine, theirs):
        self.size, self.sum, self.came = size, mine, swap(theirs)

    def over(self, distance):
        if self.size == 16:
            self.sum = self.sum + self.came
            self.came = hop(self.sum, distance, self.size)

    def over_z(self):
        if self.size == 16:
            self.sum = self.sum + self.came
            self.came = [hop(self.sum, 4 * z, self.size) for z in (1, 2, 3)]

    def result(self):
        if self.size != 16:
            return lax.psum(self.sum + self.came, "batch")
        one, two, three = self.came
        return (self.sum + one) + (two + three)


def per_device(
    size,
    tokens,
    lengths,
    q_weight,
    k_weight,
    v_weight,
    output_weight,
    up_weight,
    down_projection_weight,
    q_bias,
    v_bias,
    o_bias,
    up_bias,
    down_bias,
    gain_first,
    shift_first,
    gain_second,
    shift_second,
    out_grad,
):
    me = lax.axis_index("batch")
    core = lax.axis_index("tensor")
    depth = tokens.shape[1]
    width = q_weight.shape[1]
    units = up_weight.shape[1]
    rows = tokens.shape[0] // 2
    seqs = lengths.shape[0] // 2

    qkv_part, ou_part, down_part, pack = packed(
        size, (q_weight, k_weight, v_weight), output_weight.T, up_weight, down_projection_weight.T
    )
    tokens = lax.dynamic_slice_in_dim(tokens, core * rows, rows)
    cotangent = lax.dynamic_slice_in_dim(out_grad, core * rows, rows)
    lengths = lax.dynamic_slice_in_dim(lengths, core * seqs, seqs)
    biases = jnp.concatenate([q_bias, jnp.zeros_like(q_bias), v_bias, up_bias])
    other_biases = swap(biases)
    qkv_bias = [b[: 3 * width].reshape(1, -1) for b in (biases, other_biases)]
    up_biases = jnp.concatenate([b[3 * width :] for b in (biases, other_biases)]).reshape(1, -1)
    blank = jnp.zeros_like(o_bias)
    vectors = jnp.stack(
        [o_bias, down_bias, gain_first, shift_first, gain_second, shift_second, blank, blank]
    )

    where = jnp.stack([me, core]).astype(jnp.int32)

    quad = Quad(size, pack)
    qkv = Gather(where, size, qkv_part)
    ou = Gather(where, size, ou_part, quad, 0)
    down = Gather(where, size, down_part, quad, ou_part.shape[1])
    qkv.over_z(1, 2, 3)
    quad.first()
    qkv.came, quad.one, ou.part, down.part = meet(qkv.came, quad.one, ou.part, down.part)
    ou.over_z(1, 2, 3)
    qkv.first()
    quad.second()
    qkv.came, quad.two, ou.came, down.part, *sliced = meet(
        qkv.came,
        quad.two,
        ou.came,
        down.part,
        tokens,
        cotangent,
        vectors,
        qkv_bias,
        up_biases,
        where,
    )
    tokens, cotangent, vectors, qkv_bias, up_biases, where = sliced
    down.over_z(1, 2, 3)
    pair = qkv.second()
    ou.came = after(ou.came, pair)
    ou.first()
    qkv.came, ou.came, down.came = meet(qkv.came, ou.came, down.came)
    qkv_own = qkv.whole()
    qkv_w = (qkv_own, swap(qkv_own))
    pair = ou.second()
    column = down.first()
    front_own = attend(lengths, tokens, after(qkv_own, pair, column), qkv_bias[0])
    front_own, down.came, qkv_other = meet(front_own, down.came, qkv_w[1])
    pair = down.second()
    front_other = attend(lengths, tokens, after(qkv_other, pair), qkv_bias[1])
    front_other, ou.came = meet(front_other, ou.came)
    ou_own, down.came = meet(ou.whole(), down.came)
    ou_w = (ou_own, swap(ou_own))
    mixes = (front_own[1], front_other[1])
    down_own = down.whole()
    down_w = (down_own, swap(down_own))
    (
        output,
        *acts,
        ugrad_own,
        ugrad_other,
        normed,
        second,
        first,
        mgrad_own,
        mgrad_other,
        vec_sums,
        unit_sums,
    ) = middle(mixes, tokens, cotangent, ou_w, down_w, up_biases, vectors)
    output_came = swap(output)
    down = Scatter(where, size, [(second, acts[1])])
    first = after(first, *down.sent)
    ou = Scatter(where, size, [(first, mixes[1]), (normed, ugrad_other)])
    down.came = after(down.came, *ou.sent)
    made = down.make([(second, acts[0])])
    down.first()
    back_other, bias_other = attend_back(
        lengths, front_other[0], front_other[2], after(mgrad_other, *made)
    )
    qkv = Scatter(where, size, [(tokens, back_other)])
    down.came, qkv.sent = meet(down.came, qkv.sent)
    sent = down.second()
    ou.came = after(ou.came, sent)
    ou.make([(first, mixes[0]), (normed, ugrad_own)])
    down.came, ou.made = meet(down.came, ou.made)
    ou.first()
    sent = down.near_z()
    back_own, bias_own = attend_back(
        lengths, front_own[0], front_own[2], after(mgrad_own, sent, *ou.made)
    )
    shared = vec_sums[:6].reshape(-1)
    small = Total(
        size,
        jnp.concatenate([bias_own[0], unit_sums[0, :units], shared]),
        jnp.concatenate([bias_other[0], unit_sums[0, units:], shared]),
    )
    back_own, qkv.came, down.came = meet(back_own, qkv.came, down.came)
    qkv.make([(tokens, back_own)])
    qkv.made, ou.came, small.came = meet(qkv.made, ou.came, small.came)
    qkv.first()
    small.over(1)
    ou_sent = ou.second()
    down_sent = down.far_z()
    tokens_grad = close(
        after(first, ou_sent, down_sent, small.sum), (back_own, back_other), qkv_w
    )
    tokens_grad_came = swap(tokens_grad)
    output = join(where, output, after(output_came, tokens_grad))
    output, qkv.came, ou.came, small.came = meet(output, qkv.came, ou.came, small.came)
    sent = qkv.second()
    small.came, ou.came = after((small.came, ou.came), sent)
    small.over(2)
    sent = ou.near_z()
    down.came = after(down.came, sent)
    down_sum = down.result()
    qkv.came, small.came, down_sum = meet(qkv.came, small.came, down_sum)
    total = qkv.third()
    small.came, ou.came = after((small.came, ou.came), total)
    small.over_z()
    sent = ou.far_z()
    tokens_grad = after(tokens_grad, sent, small.sum)
    tokens_grad = join(where, tokens_grad, tokens_grad_came)
    tokens_grad, ou.came, small.came = meet(tokens_grad, ou.came, small.came)
    ou_sum, small = ou.result(), small.result()
    qkv.came = after(qkv.came, ou_sum, small)
    qkv_sum = qkv.result()

    edge = 3 * width + units
    o_bias_grad, down_bias_grad, gain_1, shift_1, gain_2, shift_2 = jnp.split(small[edge:], 6)
    return (
        output,
        tokens_grad,
        qkv_sum[:, :width],
        qkv_sum[:, width : 2 * width],
        qkv_sum[:, 2 * width :],
        ou_sum[:, :width].T,
        ou_sum[:, width:],
        down_sum.T,
        small[:width],
        small[2 * width : 3 * width],
        o_bias_grad,
        small[3 * width : edge],
        down_bias_grad,
        gain_1,
        shift_1,
        gain_2,
        shift_2,
    )


def solution(mesh):
    in_specs = (
        P("batch", None),
        P("batch"),
        P("batch", "tensor"),
        P("batch", "tensor"),
        P("batch", "tensor"),
        P("tensor", "batch"),
        P("batch", "tensor"),
        P("tensor", "batch"),
        P("tensor"),
        P("tensor"),
        P(),
        P("tensor"),
        P(),
        P(),
        P(),
        P(),
        P(),
        P("batch", None),
    )
    out_specs = (
        P("batch", None),
        P("batch", None),
        P("batch", "tensor"),
        P("batch", "tensor"),
        P("batch", "tensor"),
        P("tensor", "batch"),
        P("batch", "tensor"),
        P("tensor", "batch"),
        P("tensor"),
        P("tensor"),
        P(),
        P("tensor"),
        P(),
        P(),
        P(),
        P(),
        P(),
    )
    return jax.shard_map(
        functools.partial(per_device, mesh.shape["batch"]),
        mesh=mesh,
        in_specs=in_specs,
        out_specs=out_specs,
        check_vma=False,
    )
```

```python
import functools
import math

import jax
import jax.numpy as jnp
from jax import lax
from jax.experimental import pallas as pl
from jax.experimental.pallas import tpu as pltpu
from jax.sharding import PartitionSpec as P

HEAD_DIM = 64
LANES = 128
BLOCK = 256
CHUNK = 768
EPSILON = 1e-12
NEGATIVE = -1000000000.0
HALF = jnp.bfloat16
SINGLE = jnp.float32
SWAP = ((0, 1), (1, 0))


def matmul(left, right):
    return jnp.dot(left, right, preferred_element_type=SINGLE)


def inner_rows(left, right):
    return lax.dot_general(left, right, (((0,), (0,)), ((), ())), preferred_element_type=SINGLE)


def outer_cols(left, right):
    return lax.dot_general(left, right, (((1,), (1,)), ((), ())), preferred_element_type=SINGLE)


def layer_norm(values, gain, shift):
    center = values - jnp.mean(values, -1, keepdims=True)
    inverse = lax.rsqrt(jnp.mean(center * center, -1, keepdims=True) + EPSILON)
    normal = center * inverse
    return (normal * gain + shift, normal, inverse)


def norm_back(grad, normal, inverse, gain):
    scaled = grad * gain
    inner = (
        scaled
        - jnp.mean(scaled, -1, keepdims=True)
        - normal * jnp.mean(scaled * normal, -1, keepdims=True)
    )
    return inner * inverse


def gelu_parts(upper):
    cdf = 0.5 * (1.0 + lax.erf(upper * (1.0 / math.sqrt(2.0))))
    density = jnp.exp(-0.5 * upper * upper) * (1.0 / math.sqrt(2.0 * math.pi))
    return (upper * cdf, cdf + upper * density)


def clear_at_start(*refs):
    @pl.when(pl.program_id(0) == 0)
    def _():
        for ref in refs:
            ref[...] = jnp.zeros_like(ref)


SHORT = pl.CostEstimate(flops=1000, bytes_accessed=1000, transcendentals=0)


def owner(where_ref, z, first, second, other=0):
    core = where_ref[1] ^ other
    return where_ref[0] ^ (4 * z) ^ (first * (1 + core)) ^ (second * (2 - core))


def bring(where_ref, moves, pieces, out, sems, other):
    rows = out.shape[0] // 16
    copies = []
    for j, (source, index, column, relative) in enumerate(moves):
        piece = pieces[source] if index is None else pieces[source].at[index]
        target = out
        if relative is not None:
            piece = piece.at[:, pl.ds(column, out.shape[1])]
            at = pl.multiple_of(owner(where_ref, *relative, other) * rows, rows)
            target = out.at[pl.ds(at, rows), :]
        copies.append(pltpu.make_async_copy(piece, target, sems.at[j]))
    return copies


def head_sides():
    lane = lax.broadcasted_iota(jnp.int32, (1, LANES), 1)
    first = (lane < HEAD_DIM).astype(SINGLE)
    return (first.astype(HALF), (1.0 - first).astype(HALF))


def attend_kernel(moves, other, len_ref, where_ref, tok_ref, b_ref, *refs):
    pieces, (qkv_ref, mixed_ref, lse_ref, w_ref, sems) = refs[:-5], refs[-5:]

    @pl.when(pl.program_id(0) == 0)
    def _():
        copies = bring(where_ref, moves, pieces, w_ref, sems, other)
        for copy in copies:
            copy.start()
        for copy in copies:
            copy.wait()

    span = tok_ref.shape[0]
    width = mixed_ref.shape[1]
    length = len_ref[pl.program_id(0)]
    qkv_ref[...] = (matmul(tok_ref[...], w_ref[...]) + b_ref[...]).astype(HALF)
    sides = head_sides()
    keep = lax.broadcasted_iota(jnp.int32, (span, span), 0) < length
    upper = lax.broadcasted_iota(jnp.int32, (LANES, 1), 0) < HEAD_DIM
    for pair in range(width // LANES):
        at = LANES * pair
        query = qkv_ref[:, pl.ds(at, LANES)] * HALF(HEAD_DIM**-0.5)
        keys = qkv_ref[:, pl.ds(width + at, LANES)]
        values = qkv_ref[:, pl.ds(2 * width + at, LANES)]
        both = outer_cols(jnp.concatenate([keys * side for side in sides]), query)
        expos, totals = [], []
        for h in range(2):
            scores = jnp.where(keep, both[h * span : (h + 1) * span], NEGATIVE)
            top = jnp.max(scores, 0, keepdims=True)
            expo = jnp.exp(scores - top)
            total = jnp.sum(expo, 0, keepdims=True)
            lse_ref[0, 2 * pair + h : 2 * pair + h + 1, :] = top + jnp.log(total)
            expos.append(expo.astype(HALF))
            totals.append(1.0 / total)
        mixed = inner_rows(
            jnp.concatenate([values * side for side in sides]), jnp.concatenate(expos)
        )
        mixed *= jnp.where(upper, totals[0], totals[1])
        mixed_ref[:, pl.ds(at, LANES)] = mixed.T.astype(HALF)


def attend(lengths, where, tokens, gathered, bias, other):
    pieces, moves = gathered
    rows, depth = tokens.shape
    seqs = lengths.shape[0]
    span = rows // seqs
    width = bias.shape[1] // 3
    heads = width // HEAD_DIM
    return pl.pallas_call(
        functools.partial(attend_kernel, moves, other),
        grid_spec=pltpu.PrefetchScalarGridSpec(
            num_scalar_prefetch=2,
            grid=(seqs,),
            in_specs=[
                pl.BlockSpec((span, depth), lambda i, *_: (i, 0)),
                pl.BlockSpec((1, 3 * width), lambda i, *_: (0, 0)),
            ]
            + [pl.BlockSpec(memory_space=pl.ANY)] * len(pieces),
            out_specs=[
                pl.BlockSpec((span, 3 * width), lambda i, *_: (i, 0)),
                pl.BlockSpec((span, width), lambda i, *_: (i, 0)),
                pl.BlockSpec((1, heads, span), lambda i, *_: (i, 0, 0)),
                pl.BlockSpec((depth, 3 * width), lambda i, *_: (0, 0)),
            ],
            scratch_shapes=[pltpu.SemaphoreType.DMA((len(moves),))],
        ),
        out_shape=[
            jax.ShapeDtypeStruct((rows, 3 * width), HALF),
            jax.ShapeDtypeStruct((rows, width), HALF),
            jax.ShapeDtypeStruct((seqs, heads, span), SINGLE),
            jax.ShapeDtypeStruct((depth, 3 * width), HALF),
        ],
        compiler_params=pltpu.CompilerParams(vmem_limit_bytes=60 << 20),
        cost_estimate=SHORT,
        name="attend",
    )(lengths, where, tokens, bias, *pieces)


def attend_back_kernel(len_ref, qkv_ref, lse_ref, grad_ref, out_ref, bias_ref):
    span, width = grad_ref.shape
    step = pl.program_id(0)
    length = len_ref[step]
    sides = head_sides()
    keep = lax.broadcasted_iota(jnp.int32, (span, span), 0) < length

    @pl.when(step == 0)
    def _():
        bias_ref[...] = jnp.zeros_like(bias_ref)

    for pair in range(width // LANES):
        at = LANES * pair
        query = qkv_ref[:, pl.ds(at, LANES)] * HALF(HEAD_DIM**-0.5)
        keys = qkv_ref[:, pl.ds(width + at, LANES)]
        values = qkv_ref[:, pl.ds(2 * width + at, LANES)]
        grad = grad_ref[:, pl.ds(at, LANES)]
        side_keys = jnp.concatenate([keys * side for side in sides])
        both = outer_cols(side_keys, query)
        both_grads = outer_cols(jnp.concatenate([values * side for side in sides]), grad)
        key_grad = value_grad = 0.0
        score_grads = []
        for h in range(2):
            here = slice(h * span, (h + 1) * span)
            scores = jnp.where(keep, both[here], NEGATIVE)
            probs = jnp.exp(scores - lse_ref[0, 2 * pair + h : 2 * pair + h + 1, :])
            value_grad += matmul(probs.astype(HALF), grad * sides[h])
            prob_grad = both_grads[here]
            delta = jnp.sum(probs * prob_grad, 0, keepdims=True)
            score_grad = (probs * (prob_grad - delta)).astype(HALF)
            key_grad += matmul(score_grad, query * sides[h])
            score_grads.append(score_grad)
        query_grad = inner_rows(side_keys, jnp.concatenate(score_grads))
        query_grad = (query_grad * HEAD_DIM**-0.5).T
        for j, grads in enumerate((query_grad, key_grad, value_grad)):
            out_ref[:, pl.ds(j * width + at, LANES)] = grads.astype(HALF)
            if j != 1:
                bias_ref[:, pl.ds(j * width + at, LANES)] += jnp.sum(grads, 0, keepdims=True)


def attend_back(lengths, qkv, lse, grad):
    rows, width = grad.shape
    seqs = lengths.shape[0]
    span = rows // seqs
    heads = width // HEAD_DIM
    return pl.pallas_call(
        attend_back_kernel,
        grid_spec=pltpu.PrefetchScalarGridSpec(
            num_scalar_prefetch=1,
            grid=(seqs,),
            in_specs=[
                pl.BlockSpec((span, 3 * width), lambda i, n: (i, 0)),
                pl.BlockSpec((1, heads, span), lambda i, n: (i, 0, 0)),
                pl.BlockSpec((span, width), lambda i, n: (i, 0)),
            ],
            out_specs=[
                pl.BlockSpec((span, 3 * width), lambda i, n: (i, 0)),
                pl.BlockSpec((1, 3 * width), lambda i, n: (0, 0)),
            ],
        ),
        out_shape=[
            jax.ShapeDtypeStruct((rows, 3 * width), HALF),
            jax.ShapeDtypeStruct((1, 3 * width), SINGLE),
        ],
        compiler_params=pltpu.CompilerParams(vmem_limit_bytes=60 << 20),
        cost_estimate=SHORT,
        name="attend_back",
    )(lengths, qkv, lse, grad)


def middle_kernel(chunk, plans, count, where_ref, mix_a, mix_b, tok_ref, cot_ref, up_bias, vec_ref, *refs):
    pieces, outs, scratch = refs[:count], refs[count:-6], refs[-6:]
    out_ref, act_a, act_b, ugrad_a, ugrad_b, normed_ref, second_ref = outs[:7]
    first_ref, mgrad_a, mgrad_b, vec_grad, up_bias_grad = outs[7:]
    slope_ref, *weights, sems = scratch
    ou_a, ou_b, down_a, down_b = weights
    step = pl.program_id(0)

    def copies(n):
        names, moves, other = plans[n]
        chosen = [pieces[j] for j in names]
        return bring(where_ref, moves, chosen, weights[n], sems.at[n], other)

    def wait_for(*which):
        @pl.when(step == 0)
        def _():
            for n in which:
                for copy in copies(n):
                    copy.wait()

    def start(*which):
        @pl.when(step == 0)
        def _():
            for n in which:
                for copy in copies(n):
                    copy.start()

    start(0, 1)
    clear_at_start(vec_grad, up_bias_grad)
    width = mix_a.shape[1]
    o_bias, down_bias, gain_1, shift_1, gain_2, shift_2 = (
        vec_ref[j : j + 1, :] for j in range(6)
    )
    start(2, 3)
    wait_for(0, 1, 2, 3)
    attention = outer_cols(mix_a[...], ou_a[:, :width])
    attention += outer_cols(mix_b[...], ou_b[:, :width])
    normed, normal_1, inverse_1 = layer_norm(
        tok_ref[...].astype(SINGLE) + attention + o_bias, gain_1, shift_1
    )
    normed_half = normed.astype(HALF)
    normed_ref[...] = normed_half
    units = down_a.shape[1]
    branch = 0.0
    for half, (ou, down, act) in enumerate(((ou_a, down_a, act_a), (ou_b, down_b, act_b))):
        for c in range(units // chunk):
            here = pl.ds(c * chunk, chunk)
            there = pl.ds(half * units + c * chunk, chunk)
            upper = matmul(normed_half, ou[:, pl.ds(width + c * chunk, chunk)])
            active, slope = gelu_parts(upper + up_bias[:, there])
            active = active.astype(HALF)
            act[:, here] = active
            slope_ref[:, there] = slope
            branch += outer_cols(active, down[:, here])
    output, normal_2, inverse_2 = layer_norm(normed + branch + down_bias, gain_2, shift_2)
    out_ref[...] = output.astype(HALF)
    cot = cot_ref[...].astype(SINGLE)
    second = norm_back(cot, normal_2, inverse_2, gain_2)
    second_half = second.astype(HALF)
    second_ref[...] = second_half
    normed_grad = second
    for half, (ou, down, ugrad) in enumerate(((ou_a, down_a, ugrad_a), (ou_b, down_b, ugrad_b))):
        for c in range(units // chunk):
            here = pl.ds(c * chunk, chunk)
            there = pl.ds(half * units + c * chunk, chunk)
            upper_grad = matmul(second_half, down[:, here]) * slope_ref[:, there]
            up_bias_grad[:, there] += jnp.sum(upper_grad, 0, keepdims=True)
            upper_grad = upper_grad.astype(HALF)
            ugrad[:, here] = upper_grad
            normed_grad += outer_cols(upper_grad, ou[:, pl.ds(width + c * chunk, chunk)])
    first = norm_back(normed_grad, normal_1, inverse_1, gain_1)
    first_half = first.astype(HALF)
    first_ref[...] = first_half
    mgrad_a[...] = matmul(first_half, ou_a[:, :width]).astype(HALF)
    mgrad_b[...] = matmul(first_half, ou_b[:, :width]).astype(HALF)
    sums = (first, second, normed_grad * normal_1, normed_grad, cot * normal_2, cot)
    for j, rows in enumerate(sums):
        vec_grad[j : j + 1, :] += jnp.sum(rows, 0, keepdims=True)


def close_kernel(first, grad_a, grad_b, qkv_a, qkv_b, out):
    total = first[...].astype(SINGLE) + outer_cols(grad_a[...], qkv_a[...])
    out[...] = (total + outer_cols(grad_b[...], qkv_b[...])).astype(HALF)


def by_rows(kernel, name, streamed, held, outs, totals=(), pieces=(), scratch=(), where=None):
    rows = streamed[0].shape[0]
    block = math.gcd(rows, BLOCK)
    stream = lambda columns: pl.BlockSpec((block, columns), lambda i, *_: (i, 0))
    shape = jax.ShapeDtypeStruct
    scalars = () if where is None else (where,)
    return pl.pallas_call(
        kernel,
        grid_spec=pltpu.PrefetchScalarGridSpec(
            num_scalar_prefetch=len(scalars),
            grid=(rows // block,),
            in_specs=[stream(a.shape[1]) for a in streamed]
            + [
                pl.BlockSpec(a.shape, lambda i, *_: (0, 0), pipeline_mode=pl.Buffered(1))
                for a in held
            ]
            + [pl.BlockSpec(memory_space=pl.ANY)] * len(pieces),
            out_specs=[stream(columns) for columns in outs]
            + [pl.BlockSpec(size, lambda i, *_: (0, 0)) for size in totals],
            scratch_shapes=scratch,
        ),
        out_shape=[shape((rows, columns), HALF) for columns in outs]
        + [shape(size, SINGLE) for size in totals],
        compiler_params=pltpu.CompilerParams(vmem_limit_bytes=60 << 20),
        cost_estimate=SHORT,
        name=name,
    )(*scalars, *streamed, *held, *pieces)


def middle(where, mixes, tokens, cotangent, gathered, up_bias, vectors):
    depth = tokens.shape[1]
    width = mixes[0].shape[1]
    units = up_bias.shape[1] // 2
    block = math.gcd(tokens.shape[0], BLOCK)
    pieces, plans = [], []
    for n, (parts, moves) in enumerate(gathered):
        names = []
        for part in parts:
            known = [j for j, piece in enumerate(pieces) if piece is part]
            names.append(known[0] if known else len(pieces))
            if not known:
                pieces.append(part)
        plans.append((names, moves, n % 2))
    most = max(len(moves) for _, moves in gathered)
    held = [pltpu.VMEM((depth, columns), HALF) for columns in (width + units, units) for _ in (0, 1)]
    return by_rows(
        functools.partial(middle_kernel, math.gcd(units, CHUNK), plans, len(pieces)),
        "middle",
        (*mixes, tokens, cotangent),
        (up_bias, vectors),
        [depth] + [units] * 4 + [depth] * 3 + [width] * 2,
        [(8, depth), (1, 2 * units)],
        pieces,
        [pltpu.VMEM((block, 2 * units), SINGLE), *held, pltpu.SemaphoreType.DMA((4, most))],
        where,
    )


def close(first, grads, qkv_halves):
    return by_rows(close_kernel, "close", (first, *grads), qkv_halves, [first.shape[1]])[0]


def swap(array):
    return lax.ppermute(array, "tensor", SWAP)


def hop(array, distance, size):
    return lax.ppermute(array, "batch", [(i, i ^ distance) for i in range(size)])


def pack_first_kernel(*refs):
    out = refs[-1]
    width = refs[0].shape[1]
    for j, ref in enumerate(refs[:-1]):
        out[:, j * width : (j + 1) * width] = ref[...].astype(HALF)


def pack_rest_kernel(o_ref, up_ref, down_ref, ou, down, pack):
    width = o_ref.shape[1]
    ou[:, :width] = o_ref[...].astype(HALF)
    ou[:, width:] = up_ref[...].astype(HALF)
    down[...] = down_ref[...].astype(HALF)
    pack[:, : ou.shape[1]] = ou[...]
    pack[:, ou.shape[1] :] = down[...]


def packed(size, qkv, o_turned, up_weight, down_turned):
    if size != 16:
        first = jnp.concatenate(qkv, 1).astype(HALF)
        ou = jnp.concatenate([o_turned, up_weight], 1).astype(HALF)
        return first, ou, down_turned.astype(HALF), None
    rows, units = up_weight.shape
    width = o_turned.shape[1]
    shape = lambda columns: jax.ShapeDtypeStruct((rows, columns), HALF)
    params = pltpu.CompilerParams(vmem_limit_bytes=60 << 20)
    first = pl.pallas_call(
        pack_first_kernel,
        out_shape=shape(3 * width),
        compiler_params=params,
        cost_estimate=SHORT,
        name="pack_first",
    )(*qkv)
    rest = pl.pallas_call(
        pack_rest_kernel,
        out_shape=[shape(width + units), shape(units), shape(width + 2 * units)],
        compiler_params=params,
        cost_estimate=SHORT,
        name="pack_rest",
    )(o_turned, up_weight, down_turned)
    return first, *rest


def join_kernel(where_ref, mine, theirs, out):
    is_mine = pl.program_id(0) * 2 // pl.num_programs(0) == where_ref[1]

    @pl.when(is_mine)
    def _():
        out[...] = mine[...]

    @pl.when(jnp.logical_not(is_mine))
    def _():
        out[...] = theirs[...]


def join(where, mine, theirs):
    rows, columns = mine.shape
    block = rows
    steps = 1

    def spec(other):
        first = lambda w: (w[1] ^ other) * steps
        return pl.BlockSpec(
            (block, columns), lambda i, w: (jnp.clip(i - first(w), 0, steps - 1), 0)
        )

    return pl.pallas_call(
        join_kernel,
        grid_spec=pltpu.PrefetchScalarGridSpec(
            num_scalar_prefetch=1,
            grid=(2 * steps,),
            in_specs=[spec(0), spec(1)],
            out_specs=pl.BlockSpec((block, columns), lambda i, w: (i, 0)),
        ),
        out_shape=jax.ShapeDtypeStruct((2 * rows, columns), HALF),
        compiler_params=pltpu.CompilerParams(vmem_limit_bytes=60 << 20),
        cost_estimate=SHORT,
        name="join",
    )(where, mine, theirs)


def after(array, *others):
    return lax.optimization_barrier((array, *others))[0]


def meet(*arrays):
    return lax.optimization_barrier(arrays)


def cross(array, turn, size):
    pairs = [(2 * i + c, 2 * (i ^ (1 + (c ^ turn))) + c) for i in range(size) for c in (0, 1)]
    return lax.ppermute(array, ("batch", "tensor"), pairs)


class Quad:
    def __init__(self, size, part):
        self.size, self.part = size, part
        self.one = self.two = None

    def first(self):
        if self.size == 16:
            self.one = cross(self.part, 0, self.size)

    def second(self):
        if self.size == 16:
            self.two = cross(jnp.stack([self.part, self.one]), 1, self.size)

    def pieces(self):
        return [self.part, self.one, self.two]

    def moves(self, source, left):
        places = ((0, None, (0, 0, 0)), (1, None, (0, 1, 0)), (2, 0, (0, 0, 1)), (2, 1, (0, 1, 1)))
        return [(source + n, index, left, place) for n, index, place in places]


class Gather:
    def __init__(self, where, size, part, quad=None, left=0):
        self.where, self.size, self.part = where, size, part
        self.quad, self.left = quad, left
        self.came = []

    def over_z(self, *steps):
        if self.size == 16:
            self.came = [*self.came, *(hop(self.part, 4 * z, self.size) for z in steps)]

    def first(self):
        if self.size != 16:
            return self.part
        self.column = jnp.stack(self.came if self.quad else [self.part, *self.came])
        self.came = cross(self.column, 0, self.size)
        return self.column

    def second(self):
        if self.size != 16:
            return self.part
        self.pair = jnp.concatenate([self.column, self.came])
        self.came = cross(self.pair, 1, self.size)
        return self.pair

    def pieces(self):
        if self.size != 16:
            return [lax.all_gather(self.part, "batch", axis=0, tiled=True)]
        return [self.pair, self.came]

    def moves(self):
        if self.size != 16:
            return [(0, None, 0, None)]
        count = self.column.shape[0]
        moves = [
            (n, count * f + j, 0, (j + 4 - count, f, n))
            for n in (0, 1)
            for f in (0, 1)
            for j in range(count)
        ]
        return moves + (self.quad.moves(2, self.left) if self.quad else [])


def own_grad_kernel(counts, where_ref, *refs):
    n = len(counts)
    lefts, rights, received, outs, summed = (
        refs[:n],
        refs[n : 2 * n],
        refs[2 * n : 3 * n],
        refs[3 * n : -1],
        refs[-1],
    )
    step = pl.program_id(0)
    start = 0
    for left, right, got, count in zip(lefts, rights, received, counts):

        @pl.when((step >= start) & (step < start + count))
        def _(left=left, right=right, got=got):
            grads = inner_rows(left[...], right[...]) + got[...].astype(SINGLE)
            summed[...] = grads.astype(HALF)

        start += count
    rows = outs[0].shape[1]
    for j in range(16):
        at = pl.multiple_of(owner(where_ref, j % 4, j // 8, j // 4 % 2) * rows, rows)
        outs[1 - j // 8][j % 8] = summed[pl.ds(at, rows), :]


def own_grad(where, pairs, received):
    rows, depth = pairs[0][0].shape
    widths = [right.shape[1] for _, right in pairs]
    chunk = math.gcd(*widths, 768) if len(widths) == 1 else math.gcd(*widths)
    counts = [width // chunk for width in widths]
    starts = [sum(counts[:j]) for j in range(len(counts))]

    def spec(height, j):
        last = counts[j] - 1
        return pl.BlockSpec(
            (height, chunk), lambda c, m: (0, jnp.clip(c - starts[j], 0, last))
        )

    block = depth // 16
    return pl.pallas_call(
        functools.partial(own_grad_kernel, counts),
        grid_spec=pltpu.PrefetchScalarGridSpec(
            num_scalar_prefetch=1,
            grid=(sum(counts),),
            in_specs=[
                pl.BlockSpec((rows, depth), lambda c, m: (0, 0), pipeline_mode=pl.Buffered(1))
                for _ in pairs
            ]
            + [spec(rows, j) for j in range(len(pairs))]
            + [spec(depth, j) for j in range(len(pairs))],
            out_specs=[pl.BlockSpec((8, block, chunk), lambda c, m: (0, 0, c))] * 2,
            scratch_shapes=[pltpu.VMEM((depth, chunk), HALF)],
        ),
        out_shape=[jax.ShapeDtypeStruct((8, block, sum(widths)), HALF)] * 2,
        compiler_params=pltpu.CompilerParams(vmem_limit_bytes=60 << 20),
        cost_estimate=SHORT,
        name="own_grad",
    )(where, *[left for left, _ in pairs], *[right for _, right in pairs], *received)


class Scatter:
    def __init__(self, where, size, others):
        self.where, self.size = where, size
        self.sent = [inner_rows(left, right).astype(HALF) for left, right in others]
        self.came = [swap(grads) for grads in self.sent]

    def make(self, pairs):
        if self.size != 16:
            parts = [
                inner_rows(*pair) + part.astype(SINGLE) for pair, part in zip(pairs, self.came)
            ]
            self.made = [jnp.concatenate(parts, 1)]
        else:
            self.made = own_grad(self.where, pairs, self.came)
        return self.made

    def first(self):
        self.kept = self.made[-1]
        if self.size == 16:
            self.came = cross(self.made[0], 0, self.size)

    def second(self):
        if self.size != 16:
            return self.kept
        half = self.kept.shape[0] // 2
        sent = self.kept[half:] + self.came[half:]
        self.kept = self.kept[:half] + self.came[:half]
        self.came = cross(sent, 1, self.size)
        return sent

    def third(self):
        if self.size != 16:
            return self.kept
        total = self.kept + self.came
        self.kept = total[0]
        self.came = [hop(total[z], 4 * z, self.size) for z in (1, 2, 3)]
        return total

    def near_z(self):
        if self.size != 16:
            return self.kept
        sent = self.kept[1::2] + self.came[1::2]
        self.kept = self.kept[::2] + self.came[::2]
        self.came = hop(sent, 4, self.size)
        return sent

    def far_z(self):
        if self.size != 16:
            return self.kept
        sent = self.kept[1] + self.came[1]
        self.kept = self.kept[0] + self.came[0]
        self.came = [hop(sent, 8, self.size)]
        return sent

    def result(self):
        if self.size != 16:
            return lax.psum_scatter(self.kept, "batch", scatter_dimension=0, tiled=True)
        return sum((a.astype(SINGLE) for a in self.came), self.kept.astype(SINGLE))


class Total:
    def __init__(self, size, mine, theirs):
        self.size, self.sum, self.came = size, mine, swap(theirs)

    def over(self, distance):
        if self.size == 16:
            self.sum = self.sum + self.came
            self.came = hop(self.sum, distance, self.size)

    def over_z(self):
        if self.size == 16:
            self.sum = self.sum + self.came
            self.came = [hop(self.sum, 4 * z, self.size) for z in (1, 2, 3)]

    def result(self):
        if self.size != 16:
            return lax.psum(self.sum + self.came, "batch")
        one, two, three = self.came
        return (self.sum + one) + (two + three)


def per_device(
    size,
    tokens,
    lengths,
    q_weight,
    k_weight,
    v_weight,
    output_weight,
    up_weight,
    down_projection_weight,
    q_bias,
    v_bias,
    o_bias,
    up_bias,
    down_bias,
    gain_first,
    shift_first,
    gain_second,
    shift_second,
    out_grad,
):
    me = lax.axis_index("batch")
    core = lax.axis_index("tensor")
    depth = tokens.shape[1]
    width = q_weight.shape[1]
    units = up_weight.shape[1]
    rows = tokens.shape[0] // 2
    seqs = lengths.shape[0] // 2

    qkv_part, ou_part, down_part, pack = packed(
        size, (q_weight, k_weight, v_weight), output_weight.T, up_weight, down_projection_weight.T
    )
    tokens = lax.dynamic_slice_in_dim(tokens, core * rows, rows)
    cotangent = lax.dynamic_slice_in_dim(out_grad, core * rows, rows)
    lengths = lax.dynamic_slice_in_dim(lengths, core * seqs, seqs)
    biases = jnp.concatenate([q_bias, jnp.zeros_like(q_bias), v_bias, up_bias])
    other_biases = swap(biases)
    qkv_bias = [b[: 3 * width].reshape(1, -1) for b in (biases, other_biases)]
    up_biases = jnp.concatenate([b[3 * width :] for b in (biases, other_biases)]).reshape(1, -1)
    blank = jnp.zeros_like(o_bias)
    vectors = jnp.stack(
        [o_bias, down_bias, gain_first, shift_first, gain_second, shift_second, blank, blank]
    )

    where = jnp.stack([me, core]).astype(jnp.int32)

    quad = Quad(size, pack)
    qkv = Gather(where, size, qkv_part)
    ou = Gather(where, size, ou_part, quad, 0)
    down = Gather(where, size, down_part, quad, ou_part.shape[1])
    qkv.over_z(1, 2, 3)
    quad.first()
    qkv.came, quad.one, ou.part, down.part = meet(qkv.came, quad.one, ou.part, down.part)
    column = qkv.first()
    ou.part, quad.one = after((ou.part, quad.one), column)
    ou.over_z(1, 2, 3)
    quad.second()
    qkv.came, quad.two, ou.came, down.part, tokens, cotangent = meet(
        qkv.came, quad.two, ou.came, down.part, tokens, cotangent
    )
    down.over_z(1, 2, 3)
    pair = qkv.second()
    ou.came = after(ou.came, pair)
    ou.first()
    qkv.came, ou.came, down.came, *rest = meet(
        qkv.came, ou.came, down.came, vectors, qkv_bias, up_biases, where
    )
    vectors, qkv_bias, up_biases, where = rest
    swapped = lambda arrays: [swap(array) for array in arrays]
    qkv_own = qkv.pieces()
    qkv_other = swapped(qkv_own)
    shared = quad.pieces() if size == 16 else []
    shared_other = swapped(shared)
    pair = ou.second()
    column = down.first()
    front_own = attend(
        lengths, where, after(tokens, pair, column), (qkv_own, qkv.moves()), qkv_bias[0], 0
    )
    front_own, ou.came, down.came, qkv_other, shared_other = meet(
        front_own, ou.came, down.came, qkv_other, shared_other
    )
    pair = down.second()
    early = (ou.pair, down.pair) if size == 16 else ()
    early_other = swapped(early)
    front_other = attend(
        lengths, where, after(tokens, pair), (qkv_other, qkv.moves()), qkv_bias[1], 1
    )
    ou_late = [ou.came, swap(ou.came)] if size == 16 else []
    front_other, ou_late, down.came, early_other = meet(
        front_other, ou_late, down.came, early_other
    )
    if size == 16:
        down_late = [down.came, swap(down.came)]
        gathered = [
            ([pair, late, *pieces], moves)
            for lates, moves, pairs in (
                (ou_late, ou.moves(), (ou.pair, early_other[0])),
                (down_late, down.moves(), (down.pair, early_other[1])),
            )
            for pair, late, pieces in zip(pairs, lates, (shared, shared_other))
        ]
    else:
        gathered = []
        for weight in (ou, down):
            own = weight.pieces()
            gathered += [(own, weight.moves()), (swapped(own), weight.moves())]
    qkv_w = (front_own[3], front_other[3])
    mixes = (front_own[1], front_other[1])
    (
        output,
        *acts,
        ugrad_own,
        ugrad_other,
        normed,
        second,
        first,
        mgrad_own,
        mgrad_other,
        vec_sums,
        unit_sums,
    ) = middle(where, mixes, tokens, cotangent, gathered, up_biases, vectors)
    output_came = swap(output)
    down = Scatter(where, size, [(second, acts[1])])
    first = after(first, *down.sent)
    ou = Scatter(where, size, [(first, mixes[1]), (normed, ugrad_other)])
    down.came = after(down.came, *ou.sent)
    made = down.make([(second, acts[0])])
    down.first()
    back_other, bias_other = attend_back(
        lengths, front_other[0], front_other[2], after(mgrad_other, *made)
    )
    qkv = Scatter(where, size, [(tokens, back_other)])
    down.came, qkv.sent = meet(down.came, qkv.sent)
    sent = down.second()
    ou.came = after(ou.came, sent)
    ou.make([(first, mixes[0]), (normed, ugrad_own)])
    down.came, ou.made = meet(down.came, ou.made)
    ou.first()
    sent = down.near_z()
    back_own, bias_own = attend_back(
        lengths, front_own[0], front_own[2], after(mgrad_own, sent, *ou.made)
    )
    shared = vec_sums[:6].reshape(-1)
    small = Total(
        size,
        jnp.concatenate([bias_own[0], unit_sums[0, :units], shared]),
        jnp.concatenate([bias_other[0], unit_sums[0, units:], shared]),
    )
    back_own, qkv.came, down.came = meet(back_own, qkv.came, down.came)
    qkv.make([(tokens, back_own)])
    qkv.made, ou.came, small.came = meet(qkv.made, ou.came, small.came)
    qkv.first()
    small.over(1)
    ou_sent = ou.second()
    down_sent = down.far_z()
    tokens_grad = close(
        after(first, ou_sent, down_sent, small.sum), (back_own, back_other), qkv_w
    )
    tokens_grad_came = swap(tokens_grad)
    output = join(where, output, after(output_came, tokens_grad))
    output, qkv.came, ou.came, small.came = meet(output, qkv.came, ou.came, small.came)
    sent = qkv.second()
    small.came, ou.came = after((small.came, ou.came), sent)
    small.over(2)
    sent = ou.near_z()
    down.came = after(down.came, sent)
    down_sum = down.result()
    tokens_grad = after(tokens_grad, sent, small.sum)
    tokens_grad = join(where, tokens_grad, tokens_grad_came)
    qkv.came, down_sum, tokens_grad = meet(qkv.came, down_sum, tokens_grad)
    total = qkv.third()
    small.came, ou.came = after((small.came, ou.came), total)
    sent = ou.far_z()
    small.came = after(small.came, sent)
    small.over_z()
    small = small.result()
    ou.came = after(ou.came, small)
    ou_sum = ou.result()
    edge = 3 * width + units
    ready = (
        output,
        tokens_grad,
        ou_sum[:, :width].T,
        ou_sum[:, width:],
        down_sum.T,
        small[:width],
        small[2 * width : 3 * width],
        small[3 * width : edge],
        *jnp.split(small[edge:], 6),
    )
    qkv.came, ready = meet(qkv.came, ready)
    qkv_sum = qkv.result()
    output, tokens_grad, o_sum, up_sum, down_sum, q_bias_grad, v_bias_grad, up_bias_grad = ready[:8]
    o_bias_grad, down_bias_grad, gain_1, shift_1, gain_2, shift_2 = ready[8:]
    return (
        output,
        tokens_grad,
        qkv_sum[:, :width],
        qkv_sum[:, width : 2 * width],
        qkv_sum[:, 2 * width :],
        o_sum,
        up_sum,
        down_sum,
        q_bias_grad,
        v_bias_grad,
        o_bias_grad,
        up_bias_grad,
        down_bias_grad,
        gain_1,
        shift_1,
        gain_2,
        shift_2,
    )


def solution(mesh):
    in_specs = (
        P("batch", None),
        P("batch"),
        P("batch", "tensor"),
        P("batch", "tensor"),
        P("batch", "tensor"),
        P("tensor", "batch"),
        P("batch", "tensor"),
        P("tensor", "batch"),
        P("tensor"),
        P("tensor"),
        P(),
        P("tensor"),
        P(),
        P(),
        P(),
        P(),
        P(),
        P("batch", None),
    )
    out_specs = (
        P("batch", None),
        P("batch", None),
        P("batch", "tensor"),
        P("batch", "tensor"),
        P("batch", "tensor"),
        P("tensor", "batch"),
        P("batch", "tensor"),
        P("tensor", "batch"),
        P("tensor"),
        P("tensor"),
        P(),
        P("tensor"),
        P(),
        P(),
        P(),
        P(),
        P(),
    )
    return jax.shard_map(
        functools.partial(per_device, mesh.shape["batch"]),
        mesh=mesh,
        in_specs=in_specs,
        out_specs=out_specs,
        check_vma=False,
    )
```

```python
import functools
import math

import jax
import jax.numpy as jnp
from jax import lax
from jax.experimental import pallas as pl
from jax.experimental.pallas import tpu as pltpu
from jax.sharding import PartitionSpec as P

HEAD_DIM = 64
LANES = 128
BLOCK = 256
CHUNK = 768
EPSILON = 1e-12
NEGATIVE = -1000000000.0
HALF = jnp.bfloat16
SINGLE = jnp.float32
SWAP = ((0, 1), (1, 0))


def matmul(left, right):
    return jnp.dot(left, right, preferred_element_type=SINGLE)


def inner_rows(left, right):
    return lax.dot_general(left, right, (((0,), (0,)), ((), ())), preferred_element_type=SINGLE)


def outer_cols(left, right):
    return lax.dot_general(left, right, (((1,), (1,)), ((), ())), preferred_element_type=SINGLE)


def layer_norm(values, gain, shift):
    center = values - jnp.mean(values, -1, keepdims=True)
    inverse = lax.rsqrt(jnp.mean(center * center, -1, keepdims=True) + EPSILON)
    normal = center * inverse
    return (normal * gain + shift, normal, inverse)


def norm_back(grad, normal, inverse, gain):
    scaled = grad * gain
    inner = (
        scaled
        - jnp.mean(scaled, -1, keepdims=True)
        - normal * jnp.mean(scaled * normal, -1, keepdims=True)
    )
    return inner * inverse


def gelu_parts(upper):
    cdf = 0.5 * (1.0 + lax.erf(upper * (1.0 / math.sqrt(2.0))))
    density = jnp.exp(-0.5 * upper * upper) * (1.0 / math.sqrt(2.0 * math.pi))
    return (upper * cdf, cdf + upper * density)


def clear_at_start(*refs):
    @pl.when(pl.program_id(0) == 0)
    def _():
        for ref in refs:
            ref[...] = jnp.zeros_like(ref)


SHORT = pl.CostEstimate(flops=1000, bytes_accessed=1000, transcendentals=0)


def owner(where_ref, z, first, second, other=0):
    core = where_ref[1] ^ other
    return where_ref[0] ^ (4 * z) ^ (first * (1 + core)) ^ (second * (2 - core))


def bring(where_ref, moves, pieces, out, sems, other):
    rows = out.shape[0] // 16
    copies = []
    for j, (source, index, column, relative) in enumerate(moves):
        piece = pieces[source] if index is None else pieces[source].at[index]
        target = out
        if relative is not None:
            piece = piece.at[:, pl.ds(column, out.shape[1])]
            at = pl.multiple_of(owner(where_ref, *relative, other) * rows, rows)
            target = out.at[pl.ds(at, rows), :]
        copies.append(pltpu.make_async_copy(piece, target, sems.at[j]))
    return copies


def head_sides():
    lane = lax.broadcasted_iota(jnp.int32, (1, LANES), 1)
    first = (lane < HEAD_DIM).astype(SINGLE)
    return (first.astype(HALF), (1.0 - first).astype(HALF))


def attend_kernel(moves, other, len_ref, where_ref, tok_ref, b_ref, *refs):
    pieces, (qkv_ref, mixed_ref, lse_ref, w_ref, sems) = refs[:-5], refs[-5:]

    @pl.when(pl.program_id(0) == 0)
    def _():
        copies = bring(where_ref, moves, pieces, w_ref, sems, other)
        for copy in copies:
            copy.start()
        for copy in copies:
            copy.wait()

    span = tok_ref.shape[0]
    width = mixed_ref.shape[1]
    length = len_ref[pl.program_id(0)]
    qkv_ref[...] = (matmul(tok_ref[...], w_ref[...]) + b_ref[...]).astype(HALF)
    sides = head_sides()
    keep = lax.broadcasted_iota(jnp.int32, (span, span), 0) < length
    upper = lax.broadcasted_iota(jnp.int32, (LANES, 1), 0) < HEAD_DIM
    for pair in range(width // LANES):
        at = LANES * pair
        query = qkv_ref[:, pl.ds(at, LANES)] * HALF(HEAD_DIM**-0.5)
        keys = qkv_ref[:, pl.ds(width + at, LANES)]
        values = qkv_ref[:, pl.ds(2 * width + at, LANES)]
        both = outer_cols(jnp.concatenate([keys * side for side in sides]), query)
        expos, totals = [], []
        for h in range(2):
            scores = jnp.where(keep, both[h * span : (h + 1) * span], NEGATIVE)
            top = jnp.max(scores, 0, keepdims=True)
            expo = jnp.exp(scores - top)
            total = jnp.sum(expo, 0, keepdims=True)
            lse_ref[0, 2 * pair + h : 2 * pair + h + 1, :] = top + jnp.log(total)
            expos.append(expo.astype(HALF))
            totals.append(1.0 / total)
        mixed = inner_rows(
            jnp.concatenate([values * side for side in sides]), jnp.concatenate(expos)
        )
        mixed *= jnp.where(upper, totals[0], totals[1])
        mixed_ref[:, pl.ds(at, LANES)] = mixed.T.astype(HALF)


def attend(lengths, where, tokens, gathered, bias, other):
    pieces, moves = gathered
    rows, depth = tokens.shape
    seqs = lengths.shape[0]
    span = rows // seqs
    width = bias.shape[1] // 3
    heads = width // HEAD_DIM
    return pl.pallas_call(
        functools.partial(attend_kernel, moves, other),
        grid_spec=pltpu.PrefetchScalarGridSpec(
            num_scalar_prefetch=2,
            grid=(seqs,),
            in_specs=[
                pl.BlockSpec((span, depth), lambda i, *_: (i, 0)),
                pl.BlockSpec((1, 3 * width), lambda i, *_: (0, 0)),
            ]
            + [pl.BlockSpec(memory_space=pl.ANY)] * len(pieces),
            out_specs=[
                pl.BlockSpec((span, 3 * width), lambda i, *_: (i, 0)),
                pl.BlockSpec((span, width), lambda i, *_: (i, 0)),
                pl.BlockSpec((1, heads, span), lambda i, *_: (i, 0, 0)),
                pl.BlockSpec((depth, 3 * width), lambda i, *_: (0, 0)),
            ],
            scratch_shapes=[pltpu.SemaphoreType.DMA((len(moves),))],
        ),
        out_shape=[
            jax.ShapeDtypeStruct((rows, 3 * width), HALF),
            jax.ShapeDtypeStruct((rows, width), HALF),
            jax.ShapeDtypeStruct((seqs, heads, span), SINGLE),
            jax.ShapeDtypeStruct((depth, 3 * width), HALF),
        ],
        compiler_params=pltpu.CompilerParams(vmem_limit_bytes=60 << 20),
        cost_estimate=SHORT,
        name="attend",
    )(lengths, where, tokens, bias, *pieces)


WHOLE, BLOCKS = 0, 1


def attend_back_kernel(kind, len_ref, where_ref, qkv_ref, lse_ref, grad_ref, tok_ref, *refs):
    if kind == BLOCKS:
        got_ref, out_ref, bias_ref, sent_ref, kept_ref, summed = refs
    else:
        out_ref, bias_ref, whole_ref, summed = refs
    span, width = grad_ref.shape
    step = pl.program_id(0)
    length = len_ref[step]
    sides = head_sides()
    keep = lax.broadcasted_iota(jnp.int32, (span, span), 0) < length

    clear_at_start(bias_ref, summed)
    for pair in range(width // LANES):
        at = LANES * pair
        query = qkv_ref[:, pl.ds(at, LANES)] * HALF(HEAD_DIM**-0.5)
        keys = qkv_ref[:, pl.ds(width + at, LANES)]
        values = qkv_ref[:, pl.ds(2 * width + at, LANES)]
        grad = grad_ref[:, pl.ds(at, LANES)]
        side_keys = jnp.concatenate([keys * side for side in sides])
        both = outer_cols(side_keys, query)
        both_grads = outer_cols(jnp.concatenate([values * side for side in sides]), grad)
        key_grad = value_grad = 0.0
        score_grads = []
        for h in range(2):
            here = slice(h * span, (h + 1) * span)
            scores = jnp.where(keep, both[here], NEGATIVE)
            probs = jnp.exp(scores - lse_ref[0, 2 * pair + h : 2 * pair + h + 1, :])
            value_grad += matmul(probs.astype(HALF), grad * sides[h])
            prob_grad = both_grads[here]
            delta = jnp.sum(probs * prob_grad, 0, keepdims=True)
            score_grad = (probs * (prob_grad - delta)).astype(HALF)
            key_grad += matmul(score_grad, query * sides[h])
            score_grads.append(score_grad)
        query_grad = inner_rows(side_keys, jnp.concatenate(score_grads))
        query_grad = (query_grad * HEAD_DIM**-0.5).T
        for j, grads in enumerate((query_grad, key_grad, value_grad)):
            out_ref[:, pl.ds(j * width + at, LANES)] = grads.astype(HALF)
            if j != 1:
                bias_ref[:, pl.ds(j * width + at, LANES)] += jnp.sum(grads, 0, keepdims=True)
    for j in range(3):
        here = pl.ds(j * width, width)
        summed[:, here] += inner_rows(tok_ref[...], out_ref[:, here])

    @pl.when(step == pl.num_programs(0) - 1)
    def _():
        if kind == WHOLE:
            whole_ref[...] = summed[...].astype(HALF)
        else:
            summed[...] += got_ref[...].astype(SINGLE)
            rows = sent_ref.shape[1]
            for j in range(16):
                at = pl.multiple_of(owner(where_ref, j % 4, j // 8, j // 4 % 2) * rows, rows)
                target = sent_ref if j >= 8 else kept_ref
                target[j % 8] = summed[pl.ds(at, rows), :].astype(HALF)


def attend_back(lengths, where, qkv, lse, grad, tokens, got=None):
    rows, width = grad.shape
    depth = tokens.shape[1]
    seqs = lengths.shape[0]
    span = rows // seqs
    heads = width // HEAD_DIM
    stay = lambda size: pl.BlockSpec(size, lambda i, *_: (0,) * len(size))
    whole = (depth, 3 * width)
    blocks = (8, depth // 16, 3 * width)
    kind = WHOLE if got is None else BLOCKS
    shapes = [whole] if got is None else [blocks] * 2
    more = () if got is None else (got,)
    return pl.pallas_call(
        functools.partial(attend_back_kernel, kind),
        grid_spec=pltpu.PrefetchScalarGridSpec(
            num_scalar_prefetch=2,
            grid=(seqs,),
            in_specs=[
                pl.BlockSpec((span, 3 * width), lambda i, *_: (i, 0)),
                pl.BlockSpec((1, heads, span), lambda i, *_: (i, 0, 0)),
                pl.BlockSpec((span, width), lambda i, *_: (i, 0)),
                pl.BlockSpec((span, depth), lambda i, *_: (i, 0)),
            ]
            + [stay(whole) for _ in more],
            out_specs=[
                pl.BlockSpec((span, 3 * width), lambda i, *_: (i, 0)),
                stay((1, 3 * width)),
            ]
            + [stay(size) for size in shapes],
            scratch_shapes=[pltpu.VMEM(whole, SINGLE)],
        ),
        out_shape=[
            jax.ShapeDtypeStruct((rows, 3 * width), HALF),
            jax.ShapeDtypeStruct((1, 3 * width), SINGLE),
        ]
        + [jax.ShapeDtypeStruct(size, HALF) for size in shapes],
        compiler_params=pltpu.CompilerParams(vmem_limit_bytes=60 << 20),
        cost_estimate=SHORT,
        name="attend_back",
    )(lengths, where, qkv, lse, grad, tokens, *more)


def middle_kernel(chunk, plans, count, where_ref, mix_a, mix_b, tok_ref, cot_ref, up_bias, vec_ref, *refs):
    pieces, outs, scratch = refs[:count], refs[count:-6], refs[-6:]
    out_ref, act_a, act_b, ugrad_a, ugrad_b, normed_ref, second_ref = outs[:7]
    first_ref, mgrad_a, mgrad_b, vec_grad, up_bias_grad = outs[7:]
    slope_ref, *weights, sems = scratch
    ou_a, ou_b, down_a, down_b = weights
    step = pl.program_id(0)

    def copies(n):
        names, moves, other = plans[n]
        chosen = [pieces[j] for j in names]
        return bring(where_ref, moves, chosen, weights[n], sems.at[n], other)

    def wait_for(*which):
        @pl.when(step == 0)
        def _():
            for n in which:
                for copy in copies(n):
                    copy.wait()

    def start(*which):
        @pl.when(step == 0)
        def _():
            for n in which:
                for copy in copies(n):
                    copy.start()

    start(0, 1)
    clear_at_start(vec_grad, up_bias_grad)
    width = mix_a.shape[1]
    o_bias, down_bias, gain_1, shift_1, gain_2, shift_2 = (
        vec_ref[j : j + 1, :] for j in range(6)
    )
    start(2, 3)
    wait_for(0, 1, 2, 3)
    attention = outer_cols(mix_a[...], ou_a[:, :width])
    attention += outer_cols(mix_b[...], ou_b[:, :width])
    normed, normal_1, inverse_1 = layer_norm(
        tok_ref[...].astype(SINGLE) + attention + o_bias, gain_1, shift_1
    )
    normed_half = normed.astype(HALF)
    normed_ref[...] = normed_half
    units = down_a.shape[1]
    branch = 0.0
    for half, (ou, down, act) in enumerate(((ou_a, down_a, act_a), (ou_b, down_b, act_b))):
        for c in range(units // chunk):
            here = pl.ds(c * chunk, chunk)
            there = pl.ds(half * units + c * chunk, chunk)
            upper = matmul(normed_half, ou[:, pl.ds(width + c * chunk, chunk)])
            active, slope = gelu_parts(upper + up_bias[:, there])
            active = active.astype(HALF)
            act[:, here] = active
            slope_ref[:, there] = slope
            branch += outer_cols(active, down[:, here])
    output, normal_2, inverse_2 = layer_norm(normed + branch + down_bias, gain_2, shift_2)
    out_ref[...] = output.astype(HALF)
    cot = cot_ref[...].astype(SINGLE)
    second = norm_back(cot, normal_2, inverse_2, gain_2)
    second_half = second.astype(HALF)
    second_ref[...] = second_half
    normed_grad = second
    for half, (ou, down, ugrad) in enumerate(((ou_a, down_a, ugrad_a), (ou_b, down_b, ugrad_b))):
        for c in range(units // chunk):
            here = pl.ds(c * chunk, chunk)
            there = pl.ds(half * units + c * chunk, chunk)
            upper_grad = matmul(second_half, down[:, here]) * slope_ref[:, there]
            up_bias_grad[:, there] += jnp.sum(upper_grad, 0, keepdims=True)
            upper_grad = upper_grad.astype(HALF)
            ugrad[:, here] = upper_grad
            normed_grad += outer_cols(upper_grad, ou[:, pl.ds(width + c * chunk, chunk)])
    first = norm_back(normed_grad, normal_1, inverse_1, gain_1)
    first_half = first.astype(HALF)
    first_ref[...] = first_half
    mgrad_a[...] = matmul(first_half, ou_a[:, :width]).astype(HALF)
    mgrad_b[...] = matmul(first_half, ou_b[:, :width]).astype(HALF)
    sums = (first, second, normed_grad * normal_1, normed_grad, cot * normal_2, cot)
    for j, rows in enumerate(sums):
        vec_grad[j : j + 1, :] += jnp.sum(rows, 0, keepdims=True)


def close_kernel(first, grad_a, grad_b, qkv_a, qkv_b, out):
    total = first[...].astype(SINGLE) + outer_cols(grad_a[...], qkv_a[...])
    out[...] = (total + outer_cols(grad_b[...], qkv_b[...])).astype(HALF)


def by_rows(kernel, name, streamed, held, outs, totals=(), pieces=(), scratch=(), where=None):
    rows = streamed[0].shape[0]
    block = math.gcd(rows, BLOCK)
    stream = lambda columns: pl.BlockSpec((block, columns), lambda i, *_: (i, 0))
    shape = jax.ShapeDtypeStruct
    scalars = () if where is None else (where,)
    return pl.pallas_call(
        kernel,
        grid_spec=pltpu.PrefetchScalarGridSpec(
            num_scalar_prefetch=len(scalars),
            grid=(rows // block,),
            in_specs=[stream(a.shape[1]) for a in streamed]
            + [
                pl.BlockSpec(a.shape, lambda i, *_: (0, 0), pipeline_mode=pl.Buffered(1))
                for a in held
            ]
            + [pl.BlockSpec(memory_space=pl.ANY)] * len(pieces),
            out_specs=[stream(columns) for columns in outs]
            + [pl.BlockSpec(size, lambda i, *_: (0, 0)) for size in totals],
            scratch_shapes=scratch,
        ),
        out_shape=[shape((rows, columns), HALF) for columns in outs]
        + [shape(size, SINGLE) for size in totals],
        compiler_params=pltpu.CompilerParams(vmem_limit_bytes=60 << 20),
        cost_estimate=SHORT,
        name=name,
    )(*scalars, *streamed, *held, *pieces)


def middle(where, mixes, tokens, cotangent, gathered, up_bias, vectors):
    depth = tokens.shape[1]
    width = mixes[0].shape[1]
    units = up_bias.shape[1] // 2
    block = math.gcd(tokens.shape[0], BLOCK)
    pieces, plans = [], []
    for n, (parts, moves) in enumerate(gathered):
        names = []
        for part in parts:
            known = [j for j, piece in enumerate(pieces) if piece is part]
            names.append(known[0] if known else len(pieces))
            if not known:
                pieces.append(part)
        plans.append((names, moves, n % 2))
    most = max(len(moves) for _, moves in gathered)
    held = [pltpu.VMEM((depth, columns), HALF) for columns in (width + units, units) for _ in (0, 1)]
    return by_rows(
        functools.partial(middle_kernel, math.gcd(units, CHUNK), plans, len(pieces)),
        "middle",
        (*mixes, tokens, cotangent),
        (up_bias, vectors),
        [depth] + [units] * 4 + [depth] * 3 + [width] * 2,
        [(8, depth), (1, 2 * units)],
        pieces,
        [pltpu.VMEM((block, 2 * units), SINGLE), *held, pltpu.SemaphoreType.DMA((4, most))],
        where,
    )


def close(first, grads, qkv_halves):
    return by_rows(close_kernel, "close", (first, *grads), qkv_halves, [first.shape[1]])[0]


def swap(array):
    return lax.ppermute(array, "tensor", SWAP)


def hop(array, distance, size):
    return lax.ppermute(array, "batch", [(i, i ^ distance) for i in range(size)])


def pack_first_kernel(*refs):
    out = refs[-1]
    width = refs[0].shape[1]
    for j, ref in enumerate(refs[:-1]):
        out[:, j * width : (j + 1) * width] = ref[...].astype(HALF)


def pack_rest_kernel(o_ref, up_ref, down_ref, ou, down, pack):
    width = o_ref.shape[1]
    ou[:, :width] = o_ref[...].astype(HALF)
    ou[:, width:] = up_ref[...].astype(HALF)
    down[...] = down_ref[...].astype(HALF)
    pack[:, : ou.shape[1]] = ou[...]
    pack[:, ou.shape[1] :] = down[...]


def packed(size, qkv, o_turned, up_weight, down_turned):
    if size != 16:
        first = jnp.concatenate(qkv, 1).astype(HALF)
        ou = jnp.concatenate([o_turned, up_weight], 1).astype(HALF)
        return first, ou, down_turned.astype(HALF), None
    rows, units = up_weight.shape
    width = o_turned.shape[1]
    shape = lambda columns: jax.ShapeDtypeStruct((rows, columns), HALF)
    params = pltpu.CompilerParams(vmem_limit_bytes=60 << 20)
    first = pl.pallas_call(
        pack_first_kernel,
        out_shape=shape(3 * width),
        compiler_params=params,
        cost_estimate=SHORT,
        name="pack_first",
    )(*qkv)
    rest = pl.pallas_call(
        pack_rest_kernel,
        out_shape=[shape(width + units), shape(units), shape(width + 2 * units)],
        compiler_params=params,
        cost_estimate=SHORT,
        name="pack_rest",
    )(o_turned, up_weight, down_turned)
    return first, *rest


def join_kernel(where_ref, mine, theirs, out):
    is_mine = pl.program_id(0) * 2 // pl.num_programs(0) == where_ref[1]

    @pl.when(is_mine)
    def _():
        out[...] = mine[...]

    @pl.when(jnp.logical_not(is_mine))
    def _():
        out[...] = theirs[...]


def join(where, mine, theirs):
    rows, columns = mine.shape
    block = rows
    steps = 1

    def spec(other):
        first = lambda w: (w[1] ^ other) * steps
        return pl.BlockSpec(
            (block, columns), lambda i, w: (jnp.clip(i - first(w), 0, steps - 1), 0)
        )

    return pl.pallas_call(
        join_kernel,
        grid_spec=pltpu.PrefetchScalarGridSpec(
            num_scalar_prefetch=1,
            grid=(2 * steps,),
            in_specs=[spec(0), spec(1)],
            out_specs=pl.BlockSpec((block, columns), lambda i, w: (i, 0)),
        ),
        out_shape=jax.ShapeDtypeStruct((2 * rows, columns), HALF),
        compiler_params=pltpu.CompilerParams(vmem_limit_bytes=60 << 20),
        cost_estimate=SHORT,
        name="join",
    )(where, mine, theirs)


def after(array, *others):
    return lax.optimization_barrier((array, *others))[0]


def meet(*arrays):
    return lax.optimization_barrier(arrays)


def cross(array, turn, size):
    pairs = [(2 * i + c, 2 * (i ^ (1 + (c ^ turn))) + c) for i in range(size) for c in (0, 1)]
    return lax.ppermute(array, ("batch", "tensor"), pairs)


class Quad:
    def __init__(self, size, part):
        self.size, self.part = size, part
        self.one = self.two = None

    def first(self):
        if self.size == 16:
            self.one = cross(self.part, 0, self.size)

    def second(self):
        if self.size == 16:
            self.two = cross(jnp.stack([self.part, self.one]), 1, self.size)

    def pieces(self):
        return [self.part, self.one, self.two]

    def moves(self, source, left):
        places = ((0, None, (0, 0, 0)), (1, None, (0, 1, 0)), (2, 0, (0, 0, 1)), (2, 1, (0, 1, 1)))
        return [(source + n, index, left, place) for n, index, place in places]


class Gather:
    def __init__(self, where, size, part, quad=None, left=0):
        self.where, self.size, self.part = where, size, part
        self.quad, self.left = quad, left
        self.came = []

    def over_z(self, *steps):
        if self.size == 16:
            self.came = [*self.came, *(hop(self.part, 4 * z, self.size) for z in steps)]

    def first(self):
        if self.size != 16:
            return self.part
        self.column = jnp.stack(self.came if self.quad else [self.part, *self.came])
        self.came = cross(self.column, 0, self.size)
        return self.column

    def second(self):
        if self.size != 16:
            return self.part
        self.pair = jnp.concatenate([self.column, self.came])
        self.came = cross(self.pair, 1, self.size)
        return self.pair

    def pieces(self):
        if self.size != 16:
            return [lax.all_gather(self.part, "batch", axis=0, tiled=True)]
        return [self.pair, self.came]

    def moves(self):
        if self.size != 16:
            return [(0, None, 0, None)]
        count = self.column.shape[0]
        moves = [
            (n, count * f + j, 0, (j + 4 - count, f, n))
            for n in (0, 1)
            for f in (0, 1)
            for j in range(count)
        ]
        return moves + (self.quad.moves(2, self.left) if self.quad else [])


def own_grad_kernel(counts, where_ref, *refs):
    n = len(counts)
    lefts, rights, received, outs, summed = (
        refs[:n],
        refs[n : 2 * n],
        refs[2 * n : 3 * n],
        refs[3 * n : -1],
        refs[-1],
    )
    step = pl.program_id(0)
    start = 0
    for left, right, got, count in zip(lefts, rights, received, counts):

        @pl.when((step >= start) & (step < start + count))
        def _(left=left, right=right, got=got):
            grads = inner_rows(left[...], right[...]) + got[...].astype(SINGLE)
            summed[...] = grads.astype(HALF)

        start += count
    rows = outs[0].shape[1]
    for j in range(16):
        at = pl.multiple_of(owner(where_ref, j % 4, j // 8, j // 4 % 2) * rows, rows)
        outs[1 - j // 8][j % 8] = summed[pl.ds(at, rows), :]


def own_grad(where, pairs, received):
    rows, depth = pairs[0][0].shape
    widths = [right.shape[1] for _, right in pairs]
    chunk = math.gcd(*widths, 768) if len(widths) == 1 else math.gcd(*widths)
    counts = [width // chunk for width in widths]
    starts = [sum(counts[:j]) for j in range(len(counts))]

    def spec(height, j):
        last = counts[j] - 1
        return pl.BlockSpec(
            (height, chunk), lambda c, m: (0, jnp.clip(c - starts[j], 0, last))
        )

    block = depth // 16
    return pl.pallas_call(
        functools.partial(own_grad_kernel, counts),
        grid_spec=pltpu.PrefetchScalarGridSpec(
            num_scalar_prefetch=1,
            grid=(sum(counts),),
            in_specs=[
                pl.BlockSpec((rows, depth), lambda c, m: (0, 0), pipeline_mode=pl.Buffered(1))
                for _ in pairs
            ]
            + [spec(rows, j) for j in range(len(pairs))]
            + [spec(depth, j) for j in range(len(pairs))],
            out_specs=[pl.BlockSpec((8, block, chunk), lambda c, m: (0, 0, c))] * 2,
            scratch_shapes=[pltpu.VMEM((depth, chunk), HALF)],
        ),
        out_shape=[jax.ShapeDtypeStruct((8, block, sum(widths)), HALF)] * 2,
        compiler_params=pltpu.CompilerParams(vmem_limit_bytes=60 << 20),
        cost_estimate=SHORT,
        name="own_grad",
    )(where, *[left for left, _ in pairs], *[right for _, right in pairs], *received)


class Scatter:
    def __init__(self, where, size, others):
        self.where, self.size = where, size
        self.sent = [inner_rows(left, right).astype(HALF) for left, right in others]
        self.came = [swap(grads) for grads in self.sent]

    def make(self, pairs):
        if self.size != 16:
            parts = [
                inner_rows(*pair) + part.astype(SINGLE) for pair, part in zip(pairs, self.came)
            ]
            self.made = [jnp.concatenate(parts, 1)]
        else:
            self.made = own_grad(self.where, pairs, self.came)
        return self.made

    def first(self):
        self.kept = self.made[-1]
        if self.size == 16:
            self.came = cross(self.made[0], 0, self.size)

    def second(self):
        if self.size != 16:
            return self.kept
        half = self.kept.shape[0] // 2
        sent = self.kept[half:] + self.came[half:]
        self.kept = self.kept[:half] + self.came[:half]
        self.came = cross(sent, 1, self.size)
        return sent

    def third(self):
        if self.size != 16:
            return self.kept
        total = self.kept + self.came
        self.kept = total[0]
        self.came = [hop(total[z], 4 * z, self.size) for z in (1, 2, 3)]
        return total

    def near_z(self):
        if self.size != 16:
            return self.kept
        sent = self.kept[1::2] + self.came[1::2]
        self.kept = self.kept[::2] + self.came[::2]
        self.came = hop(sent, 4, self.size)
        return sent

    def far_z(self):
        if self.size != 16:
            return self.kept
        sent = self.kept[1] + self.came[1]
        self.kept = self.kept[0] + self.came[0]
        self.came = [hop(sent, 8, self.size)]
        return sent

    def result(self):
        if self.size != 16:
            return lax.psum_scatter(self.kept, "batch", scatter_dimension=0, tiled=True)
        return sum((a.astype(SINGLE) for a in self.came), self.kept.astype(SINGLE))


class Total:
    def __init__(self, size, mine, theirs):
        self.size, self.sum, self.came = size, mine, swap(theirs)

    def over(self, distance):
        if self.size == 16:
            self.sum = self.sum + self.came
            self.came = hop(self.sum, distance, self.size)

    def over_z(self):
        if self.size == 16:
            self.sum = self.sum + self.came
            self.came = [hop(self.sum, 4 * z, self.size) for z in (1, 2, 3)]

    def result(self):
        if self.size != 16:
            return lax.psum(self.sum + self.came, "batch")
        one, two, three = self.came
        return (self.sum + one) + (two + three)


def per_device(
    size,
    tokens,
    lengths,
    q_weight,
    k_weight,
    v_weight,
    output_weight,
    up_weight,
    down_projection_weight,
    q_bias,
    v_bias,
    o_bias,
    up_bias,
    down_bias,
    gain_first,
    shift_first,
    gain_second,
    shift_second,
    out_grad,
):
    me = lax.axis_index("batch")
    core = lax.axis_index("tensor")
    depth = tokens.shape[1]
    width = q_weight.shape[1]
    units = up_weight.shape[1]
    rows = tokens.shape[0] // 2
    seqs = lengths.shape[0] // 2

    qkv_part, ou_part, down_part, pack = packed(
        size, (q_weight, k_weight, v_weight), output_weight.T, up_weight, down_projection_weight.T
    )
    tokens = lax.dynamic_slice_in_dim(tokens, core * rows, rows)
    cotangent = lax.dynamic_slice_in_dim(out_grad, core * rows, rows)
    lengths = lax.dynamic_slice_in_dim(lengths, core * seqs, seqs)
    biases = jnp.concatenate([q_bias, jnp.zeros_like(q_bias), v_bias, up_bias])
    other_biases = swap(biases)
    qkv_bias = [b[: 3 * width].reshape(1, -1) for b in (biases, other_biases)]
    up_biases = jnp.concatenate([b[3 * width :] for b in (biases, other_biases)]).reshape(1, -1)
    blank = jnp.zeros_like(o_bias)
    vectors = jnp.stack(
        [o_bias, down_bias, gain_first, shift_first, gain_second, shift_second, blank, blank]
    )

    where = jnp.stack([me, core]).astype(jnp.int32)

    quad = Quad(size, pack)
    qkv = Gather(where, size, qkv_part)
    ou = Gather(where, size, ou_part, quad, 0)
    down = Gather(where, size, down_part, quad, ou_part.shape[1])
    qkv.over_z(1, 2, 3)
    quad.first()
    qkv.came, quad.one, ou.part, down.part = meet(qkv.came, quad.one, ou.part, down.part)
    column = qkv.first()
    ou.part, quad.one = after((ou.part, quad.one), column)
    ou.over_z(1, 2, 3)
    quad.second()
    qkv.came, quad.two, ou.came, down.part, tokens, cotangent = meet(
        qkv.came, quad.two, ou.came, down.part, tokens, cotangent
    )
    down.over_z(1, 2, 3)
    pair = qkv.second()
    ou.came = after(ou.came, pair)
    ou.first()
    qkv.came, ou.came, down.came, *rest = meet(
        qkv.came, ou.came, down.came, vectors, qkv_bias, up_biases, where
    )
    vectors, qkv_bias, up_biases, where = rest
    swapped = lambda arrays: [swap(array) for array in arrays]
    qkv_own = qkv.pieces()
    qkv_other = swapped(qkv_own)
    shared = quad.pieces() if size == 16 else []
    shared_other = swapped(shared)
    pair = ou.second()
    column = down.first()
    front_own = attend(
        lengths, where, after(tokens, pair, column), (qkv_own, qkv.moves()), qkv_bias[0], 0
    )
    front_own, ou.came, down.came, qkv_other, shared_other = meet(
        front_own, ou.came, down.came, qkv_other, shared_other
    )
    pair = down.second()
    early = (ou.pair, down.pair) if size == 16 else ()
    early_other = swapped(early)
    front_other = attend(
        lengths, where, after(tokens, pair), (qkv_other, qkv.moves()), qkv_bias[1], 1
    )
    ou_late = [ou.came, swap(ou.came)] if size == 16 else []
    front_other, ou_late, down.came, early_other = meet(
        front_other, ou_late, down.came, early_other
    )
    if size == 16:
        down_late = [down.came, swap(down.came)]
        gathered = [
            ([pair, late, *pieces], moves)
            for lates, moves, pairs in (
                (ou_late, ou.moves(), (ou.pair, early_other[0])),
                (down_late, down.moves(), (down.pair, early_other[1])),
            )
            for pair, late, pieces in zip(pairs, lates, (shared, shared_other))
        ]
    else:
        gathered = []
        for weight in (ou, down):
            own = weight.pieces()
            gathered += [(own, weight.moves()), (swapped(own), weight.moves())]
    qkv_w = (front_own[3], front_other[3])
    mixes = (front_own[1], front_other[1])
    (
        output,
        *acts,
        ugrad_own,
        ugrad_other,
        normed,
        second,
        first,
        mgrad_own,
        mgrad_other,
        vec_sums,
        unit_sums,
    ) = middle(where, mixes, tokens, cotangent, gathered, up_biases, vectors)
    output_came = swap(output)
    down = Scatter(where, size, [(second, acts[1])])
    first = after(first, *down.sent)
    ou = Scatter(where, size, [(first, mixes[1]), (normed, ugrad_other)])
    down.came = after(down.came, *ou.sent)
    made = down.make([(second, acts[0])])
    down.first()
    back_other, bias_other, whole = attend_back(
        lengths, where, front_other[0], front_other[2], after(mgrad_other, *made), tokens
    )
    qkv = Scatter(where, size, [])
    down.came, whole = meet(down.came, whole)
    qkv.came = swap(whole)
    sent = down.second()
    ou.came = after(ou.came, sent)
    ou.make([(first, mixes[0]), (normed, ugrad_own)])
    down.came, ou.made = meet(down.came, ou.made)
    ou.first()
    sent = down.near_z()
    held = after(mgrad_own, sent, *ou.made)
    got = qkv.came if size == 16 else None
    back_own, bias_own, *qkv.made = attend_back(
        lengths, where, front_own[0], front_own[2], held, tokens, got
    )
    if size != 16:
        qkv.made = [qkv.made[0].astype(SINGLE) + qkv.came.astype(SINGLE)]
    shared = vec_sums[:6].reshape(-1)
    small = Total(
        size,
        jnp.concatenate([bias_own[0], unit_sums[0, :units], shared]),
        jnp.concatenate([bias_other[0], unit_sums[0, units:], shared]),
    )
    back_own, qkv.made, down.came, ou.came = meet(back_own, qkv.made, down.came, ou.came)
    qkv.first()
    ou_sent = ou.second()
    small.came = after(small.came, ou_sent)
    small.over(1)
    down_sent = down.far_z()
    tokens_grad = close(
        after(first, ou_sent, down_sent, small.sum), (back_own, back_other), qkv_w
    )
    tokens_grad_came = swap(tokens_grad)
    output = join(where, output, after(output_came, tokens_grad))
    output, qkv.came, ou.came, small.came = meet(output, qkv.came, ou.came, small.came)
    sent = qkv.second()
    small.came, ou.came = after((small.came, ou.came), sent)
    small.over(2)
    sent = ou.near_z()
    down.came = after(down.came, sent)
    down_sum = down.result()
    tokens_grad = after(tokens_grad, sent, small.sum)
    tokens_grad = join(where, tokens_grad, tokens_grad_came)
    qkv.came, down_sum, tokens_grad = meet(qkv.came, down_sum, tokens_grad)
    total = qkv.third()
    small.came, ou.came = after((small.came, ou.came), total)
    sent = ou.far_z()
    small.came = after(small.came, sent)
    small.over_z()
    small = small.result()
    ou.came = after(ou.came, small)
    ou_sum = ou.result()
    edge = 3 * width + units
    ready = (
        output,
        tokens_grad,
        ou_sum[:, :width].T,
        ou_sum[:, width:],
        down_sum.T,
        small[:width],
        small[2 * width : 3 * width],
        small[3 * width : edge],
        *jnp.split(small[edge:], 6),
    )
    qkv.came, ready = meet(qkv.came, ready)
    qkv_sum = qkv.result()
    output, tokens_grad, o_sum, up_sum, down_sum, q_bias_grad, v_bias_grad, up_bias_grad = ready[:8]
    o_bias_grad, down_bias_grad, gain_1, shift_1, gain_2, shift_2 = ready[8:]
    return (
        output,
        tokens_grad,
        qkv_sum[:, :width],
        qkv_sum[:, width : 2 * width],
        qkv_sum[:, 2 * width :],
        o_sum,
        up_sum,
        down_sum,
        q_bias_grad,
        v_bias_grad,
        o_bias_grad,
        up_bias_grad,
        down_bias_grad,
        gain_1,
        shift_1,
        gain_2,
        shift_2,
    )


def solution(mesh):
    in_specs = (
        P("batch", None),
        P("batch"),
        P("batch", "tensor"),
        P("batch", "tensor"),
        P("batch", "tensor"),
        P("tensor", "batch"),
        P("batch", "tensor"),
        P("tensor", "batch"),
        P("tensor"),
        P("tensor"),
        P(),
        P("tensor"),
        P(),
        P(),
        P(),
        P(),
        P(),
        P("batch", None),
    )
    out_specs = (
        P("batch", None),
        P("batch", None),
        P("batch", "tensor"),
        P("batch", "tensor"),
        P("batch", "tensor"),
        P("tensor", "batch"),
        P("batch", "tensor"),
        P("tensor", "batch"),
        P("tensor"),
        P("tensor"),
        P(),
        P("tensor"),
        P(),
        P(),
        P(),
        P(),
        P(),
    )
    return jax.shard_map(
        functools.partial(per_device, mesh.shape["batch"]),
        mesh=mesh,
        in_specs=in_specs,
        out_specs=out_specs,
        check_vma=False,
    )
```

```python
import functools
import math

import jax
import jax.numpy as jnp
from jax import lax
from jax.experimental import pallas as pl
from jax.experimental.pallas import tpu as pltpu
from jax.sharding import PartitionSpec as P

HEAD_DIM = 64
LANES = 128
BLOCK = 256
CHUNK = 768
EPSILON = 1e-12
NEGATIVE = -1000000000.0
HALF = jnp.bfloat16
SINGLE = jnp.float32
SWAP = ((0, 1), (1, 0))


def matmul(left, right):
    return jnp.dot(left, right, preferred_element_type=SINGLE)


def inner_rows(left, right):
    return lax.dot_general(left, right, (((0,), (0,)), ((), ())), preferred_element_type=SINGLE)


def outer_cols(left, right):
    return lax.dot_general(left, right, (((1,), (1,)), ((), ())), preferred_element_type=SINGLE)


def layer_norm(values, gain, shift):
    center = values - jnp.mean(values, -1, keepdims=True)
    inverse = lax.rsqrt(jnp.mean(center * center, -1, keepdims=True) + EPSILON)
    normal = center * inverse
    return (normal * gain + shift, normal, inverse)


def norm_back(grad, normal, inverse, gain):
    scaled = grad * gain
    inner = (
        scaled
        - jnp.mean(scaled, -1, keepdims=True)
        - normal * jnp.mean(scaled * normal, -1, keepdims=True)
    )
    return inner * inverse


def gelu_parts(upper):
    cdf = 0.5 * (1.0 + lax.erf(upper * (1.0 / math.sqrt(2.0))))
    density = jnp.exp(-0.5 * upper * upper) * (1.0 / math.sqrt(2.0 * math.pi))
    return (upper * cdf, cdf + upper * density)


def clear_at_start(*refs):
    @pl.when(pl.program_id(0) == 0)
    def _():
        for ref in refs:
            ref[...] = jnp.zeros_like(ref)


SHORT = pl.CostEstimate(flops=1000, bytes_accessed=1000, transcendentals=0)


def owner(where_ref, z, first, second, other=0):
    core = where_ref[1] ^ other
    return where_ref[0] ^ (4 * z) ^ (first * (1 + core)) ^ (second * (2 - core))


def bring(where_ref, moves, pieces, out, sems, other):
    rows = out.shape[0] // 16
    copies = []
    for j, (source, index, column, relative) in enumerate(moves):
        piece = pieces[source] if index is None else pieces[source].at[index]
        target = out
        if relative is not None:
            piece = piece.at[:, pl.ds(column, out.shape[1])]
            at = pl.multiple_of(owner(where_ref, *relative, other) * rows, rows)
            target = out.at[pl.ds(at, rows), :]
        copies.append(pltpu.make_async_copy(piece, target, sems.at[j]))
    return copies


def head_sides():
    lane = lax.broadcasted_iota(jnp.int32, (1, LANES), 1)
    first = (lane < HEAD_DIM).astype(SINGLE)
    return (first.astype(HALF), (1.0 - first).astype(HALF))


def attend_kernel(moves, other, len_ref, where_ref, tok_ref, b_ref, *refs):
    pieces, (qkv_ref, mixed_ref, lse_ref, w_ref, sems) = refs[:-5], refs[-5:]

    @pl.when(pl.program_id(0) == 0)
    def _():
        copies = bring(where_ref, moves, pieces, w_ref, sems, other)
        for copy in copies:
            copy.start()
        for copy in copies:
            copy.wait()

    span = tok_ref.shape[0]
    width = mixed_ref.shape[1]
    length = len_ref[pl.program_id(0)]
    qkv_ref[...] = (matmul(tok_ref[...], w_ref[...]) + b_ref[...]).astype(HALF)
    sides = head_sides()
    keep = lax.broadcasted_iota(jnp.int32, (span, span), 0) < length
    upper = lax.broadcasted_iota(jnp.int32, (LANES, 1), 0) < HEAD_DIM
    for pair in range(width // LANES):
        at = LANES * pair
        query = qkv_ref[:, pl.ds(at, LANES)] * HALF(HEAD_DIM**-0.5)
        keys = qkv_ref[:, pl.ds(width + at, LANES)]
        values = qkv_ref[:, pl.ds(2 * width + at, LANES)]
        both = outer_cols(jnp.concatenate([keys * side for side in sides]), query)
        expos, totals = [], []
        for h in range(2):
            scores = jnp.where(keep, both[h * span : (h + 1) * span], NEGATIVE)
            top = jnp.max(scores, 0, keepdims=True)
            expo = jnp.exp(scores - top)
            total = jnp.sum(expo, 0, keepdims=True)
            lse_ref[0, 2 * pair + h : 2 * pair + h + 1, :] = top + jnp.log(total)
            expos.append(expo.astype(HALF))
            totals.append(1.0 / total)
        mixed = inner_rows(
            jnp.concatenate([values * side for side in sides]), jnp.concatenate(expos)
        )
        mixed *= jnp.where(upper, totals[0], totals[1])
        mixed_ref[:, pl.ds(at, LANES)] = mixed.T.astype(HALF)


def attend(lengths, where, tokens, gathered, bias, other):
    pieces, moves = gathered
    rows, depth = tokens.shape
    seqs = lengths.shape[0]
    span = rows // seqs
    width = bias.shape[1] // 3
    heads = width // HEAD_DIM
    return pl.pallas_call(
        functools.partial(attend_kernel, moves, other),
        grid_spec=pltpu.PrefetchScalarGridSpec(
            num_scalar_prefetch=2,
            grid=(seqs,),
            in_specs=[
                pl.BlockSpec((span, depth), lambda i, *_: (i, 0)),
                pl.BlockSpec((1, 3 * width), lambda i, *_: (0, 0)),
            ]
            + [pl.BlockSpec(memory_space=pl.ANY)] * len(pieces),
            out_specs=[
                pl.BlockSpec((span, 3 * width), lambda i, *_: (i, 0)),
                pl.BlockSpec((span, width), lambda i, *_: (i, 0)),
                pl.BlockSpec((1, heads, span), lambda i, *_: (i, 0, 0)),
                pl.BlockSpec((depth, 3 * width), lambda i, *_: (0, 0)),
            ],
            scratch_shapes=[pltpu.SemaphoreType.DMA((len(moves),))],
        ),
        out_shape=[
            jax.ShapeDtypeStruct((rows, 3 * width), HALF),
            jax.ShapeDtypeStruct((rows, width), HALF),
            jax.ShapeDtypeStruct((seqs, heads, span), SINGLE),
            jax.ShapeDtypeStruct((depth, 3 * width), HALF),
        ],
        compiler_params=pltpu.CompilerParams(vmem_limit_bytes=60 << 20),
        cost_estimate=SHORT,
        name="attend",
    )(lengths, where, tokens, bias, *pieces)


WHOLE, BLOCKS = 0, 1


def attend_back_kernel(kind, len_ref, where_ref, qkv_ref, lse_ref, grad_ref, tok_ref, *refs):
    if kind == BLOCKS:
        got_ref, out_ref, bias_ref, sent_ref, kept_ref, summed = refs
    else:
        out_ref, bias_ref, whole_ref, summed = refs
    span, width = grad_ref.shape
    step = pl.program_id(0)
    length = len_ref[step]
    sides = head_sides()
    keep = lax.broadcasted_iota(jnp.int32, (span, span), 0) < length

    clear_at_start(bias_ref, summed)
    for pair in range(width // LANES):
        at = LANES * pair
        query = qkv_ref[:, pl.ds(at, LANES)] * HALF(HEAD_DIM**-0.5)
        keys = qkv_ref[:, pl.ds(width + at, LANES)]
        values = qkv_ref[:, pl.ds(2 * width + at, LANES)]
        grad = grad_ref[:, pl.ds(at, LANES)]
        side_keys = jnp.concatenate([keys * side for side in sides])
        both = outer_cols(side_keys, query)
        both_grads = outer_cols(jnp.concatenate([values * side for side in sides]), grad)
        key_grad = value_grad = 0.0
        score_grads = []
        for h in range(2):
            here = slice(h * span, (h + 1) * span)
            scores = jnp.where(keep, both[here], NEGATIVE)
            probs = jnp.exp(scores - lse_ref[0, 2 * pair + h : 2 * pair + h + 1, :])
            value_grad += matmul(probs.astype(HALF), grad * sides[h])
            prob_grad = both_grads[here]
            delta = jnp.sum(probs * prob_grad, 0, keepdims=True)
            score_grad = (probs * (prob_grad - delta)).astype(HALF)
            key_grad += matmul(score_grad, query * sides[h])
            score_grads.append(score_grad)
        query_grad = inner_rows(side_keys, jnp.concatenate(score_grads))
        query_grad = (query_grad * HEAD_DIM**-0.5).T
        for j, grads in enumerate((query_grad, key_grad, value_grad)):
            out_ref[:, pl.ds(j * width + at, LANES)] = grads.astype(HALF)
            if j != 1:
                bias_ref[:, pl.ds(j * width + at, LANES)] += jnp.sum(grads, 0, keepdims=True)
    for j in range(3):
        here = pl.ds(j * width, width)
        summed[:, here] += inner_rows(tok_ref[...], out_ref[:, here])

    @pl.when(step == pl.num_programs(0) - 1)
    def _():
        if kind == WHOLE:
            whole_ref[...] = summed[...].astype(HALF)
        else:
            summed[...] += got_ref[...].astype(SINGLE)
            rows = sent_ref.shape[1]
            for j in range(16):
                at = pl.multiple_of(owner(where_ref, j % 4, j // 8, j // 4 % 2) * rows, rows)
                target = sent_ref if j >= 8 else kept_ref
                target[j % 8] = summed[pl.ds(at, rows), :].astype(HALF)


def attend_back(lengths, where, qkv, lse, grad, tokens, got=None):
    rows, width = grad.shape
    depth = tokens.shape[1]
    seqs = lengths.shape[0]
    span = rows // seqs
    heads = width // HEAD_DIM
    stay = lambda size: pl.BlockSpec(size, lambda i, *_: (0,) * len(size))
    whole = (depth, 3 * width)
    blocks = (8, depth // 16, 3 * width)
    kind = WHOLE if got is None else BLOCKS
    shapes = [whole] if got is None else [blocks] * 2
    more = () if got is None else (got,)
    return pl.pallas_call(
        functools.partial(attend_back_kernel, kind),
        grid_spec=pltpu.PrefetchScalarGridSpec(
            num_scalar_prefetch=2,
            grid=(seqs,),
            in_specs=[
                pl.BlockSpec((span, 3 * width), lambda i, *_: (i, 0)),
                pl.BlockSpec((1, heads, span), lambda i, *_: (i, 0, 0)),
                pl.BlockSpec((span, width), lambda i, *_: (i, 0)),
                pl.BlockSpec((span, depth), lambda i, *_: (i, 0)),
            ]
            + [stay(whole) for _ in more],
            out_specs=[
                pl.BlockSpec((span, 3 * width), lambda i, *_: (i, 0)),
                stay((1, 3 * width)),
            ]
            + [stay(size) for size in shapes],
            scratch_shapes=[pltpu.VMEM(whole, SINGLE)],
        ),
        out_shape=[
            jax.ShapeDtypeStruct((rows, 3 * width), HALF),
            jax.ShapeDtypeStruct((1, 3 * width), SINGLE),
        ]
        + [jax.ShapeDtypeStruct(size, HALF) for size in shapes],
        compiler_params=pltpu.CompilerParams(vmem_limit_bytes=60 << 20),
        cost_estimate=SHORT,
        name="attend_back",
    )(lengths, where, qkv, lse, grad, tokens, *more)


def middle_kernel(chunk, plans, count, where_ref, mix_a, mix_b, tok_ref, cot_ref, up_bias, vec_ref, *refs):
    pieces, outs, scratch = refs[:count], refs[count:-6], refs[-6:]
    out_ref, act_a, act_b, ugrad_a, ugrad_b, normed_ref, second_ref = outs[:7]
    first_ref, mgrad_a, mgrad_b, vec_grad, up_bias_grad = outs[7:]
    slope_ref, *weights, sems = scratch
    ou_a, ou_b, down_a, down_b = weights
    step = pl.program_id(0)

    def copies(n):
        names, moves, other = plans[n]
        chosen = [pieces[j] for j in names]
        return bring(where_ref, moves, chosen, weights[n], sems.at[n], other)

    def wait_for(*which):
        @pl.when(step == 0)
        def _():
            for n in which:
                for copy in copies(n):
                    copy.wait()

    def start(*which):
        @pl.when(step == 0)
        def _():
            for n in which:
                for copy in copies(n):
                    copy.start()

    start(0, 1)
    clear_at_start(vec_grad, up_bias_grad)
    width = mix_a.shape[1]
    o_bias, down_bias, gain_1, shift_1, gain_2, shift_2 = (
        vec_ref[j : j + 1, :] for j in range(6)
    )
    start(2, 3)
    wait_for(0, 1, 2, 3)
    attention = outer_cols(mix_a[...], ou_a[:, :width])
    attention += outer_cols(mix_b[...], ou_b[:, :width])
    normed, normal_1, inverse_1 = layer_norm(
        tok_ref[...].astype(SINGLE) + attention + o_bias, gain_1, shift_1
    )
    normed_half = normed.astype(HALF)
    normed_ref[...] = normed_half
    units = down_a.shape[1]
    branch = 0.0
    for half, (ou, down, act) in enumerate(((ou_a, down_a, act_a), (ou_b, down_b, act_b))):
        for c in range(units // chunk):
            here = pl.ds(c * chunk, chunk)
            there = pl.ds(half * units + c * chunk, chunk)
            upper = matmul(normed_half, ou[:, pl.ds(width + c * chunk, chunk)])
            active, slope = gelu_parts(upper + up_bias[:, there])
            active = active.astype(HALF)
            act[:, here] = active
            slope_ref[:, there] = slope
            branch += outer_cols(active, down[:, here])
    output, normal_2, inverse_2 = layer_norm(normed + branch + down_bias, gain_2, shift_2)
    out_ref[...] = output.astype(HALF)
    cot = cot_ref[...].astype(SINGLE)
    second = norm_back(cot, normal_2, inverse_2, gain_2)
    second_half = second.astype(HALF)
    second_ref[...] = second_half
    normed_grad = second
    for half, (ou, down, ugrad) in enumerate(((ou_a, down_a, ugrad_a), (ou_b, down_b, ugrad_b))):
        for c in range(units // chunk):
            here = pl.ds(c * chunk, chunk)
            there = pl.ds(half * units + c * chunk, chunk)
            upper_grad = matmul(second_half, down[:, here]) * slope_ref[:, there]
            up_bias_grad[:, there] += jnp.sum(upper_grad, 0, keepdims=True)
            upper_grad = upper_grad.astype(HALF)
            ugrad[:, here] = upper_grad
            normed_grad += outer_cols(upper_grad, ou[:, pl.ds(width + c * chunk, chunk)])
    first = norm_back(normed_grad, normal_1, inverse_1, gain_1)
    first_half = first.astype(HALF)
    first_ref[...] = first_half
    mgrad_a[...] = matmul(first_half, ou_a[:, :width]).astype(HALF)
    mgrad_b[...] = matmul(first_half, ou_b[:, :width]).astype(HALF)
    sums = (first, second, normed_grad * normal_1, normed_grad, cot * normal_2, cot)
    for j, rows in enumerate(sums):
        vec_grad[j : j + 1, :] += jnp.sum(rows, 0, keepdims=True)


def close_kernel(first, grad_a, grad_b, qkv_a, qkv_b, out):
    total = first[...].astype(SINGLE) + outer_cols(grad_a[...], qkv_a[...])
    out[...] = (total + outer_cols(grad_b[...], qkv_b[...])).astype(HALF)


def by_rows(kernel, name, streamed, held, outs, totals=(), pieces=(), scratch=(), where=None):
    rows = streamed[0].shape[0]
    block = math.gcd(rows, BLOCK)
    stream = lambda columns: pl.BlockSpec((block, columns), lambda i, *_: (i, 0))
    shape = jax.ShapeDtypeStruct
    scalars = () if where is None else (where,)
    return pl.pallas_call(
        kernel,
        grid_spec=pltpu.PrefetchScalarGridSpec(
            num_scalar_prefetch=len(scalars),
            grid=(rows // block,),
            in_specs=[stream(a.shape[1]) for a in streamed]
            + [
                pl.BlockSpec(a.shape, lambda i, *_: (0, 0), pipeline_mode=pl.Buffered(1))
                for a in held
            ]
            + [pl.BlockSpec(memory_space=pl.ANY)] * len(pieces),
            out_specs=[stream(columns) for columns in outs]
            + [pl.BlockSpec(size, lambda i, *_: (0, 0)) for size in totals],
            scratch_shapes=scratch,
        ),
        out_shape=[shape((rows, columns), HALF) for columns in outs]
        + [shape(size, SINGLE) for size in totals],
        compiler_params=pltpu.CompilerParams(vmem_limit_bytes=60 << 20),
        cost_estimate=SHORT,
        name=name,
    )(*scalars, *streamed, *held, *pieces)


def middle(where, mixes, tokens, cotangent, gathered, up_bias, vectors):
    depth = tokens.shape[1]
    width = mixes[0].shape[1]
    units = up_bias.shape[1] // 2
    block = math.gcd(tokens.shape[0], BLOCK)
    pieces, plans = [], []
    for n, (parts, moves) in enumerate(gathered):
        names = []
        for part in parts:
            known = [j for j, piece in enumerate(pieces) if piece is part]
            names.append(known[0] if known else len(pieces))
            if not known:
                pieces.append(part)
        plans.append((names, moves, n % 2))
    most = max(len(moves) for _, moves in gathered)
    held = [pltpu.VMEM((depth, columns), HALF) for columns in (width + units, units) for _ in (0, 1)]
    return by_rows(
        functools.partial(middle_kernel, math.gcd(units, CHUNK), plans, len(pieces)),
        "middle",
        (*mixes, tokens, cotangent),
        (up_bias, vectors),
        [depth] + [units] * 4 + [depth] * 3 + [width] * 2,
        [(8, depth), (1, 2 * units)],
        pieces,
        [pltpu.VMEM((block, 2 * units), SINGLE), *held, pltpu.SemaphoreType.DMA((4, most))],
        where,
    )


def close(first, grads, qkv_halves):
    return by_rows(close_kernel, "close", (first, *grads), qkv_halves, [first.shape[1]])[0]


def swap(array):
    return lax.ppermute(array, "tensor", SWAP)


def hop(array, distance, size):
    return lax.ppermute(array, "batch", [(i, i ^ distance) for i in range(size)])


def pack_first_kernel(*refs):
    out = refs[-1]
    width = refs[0].shape[1]
    for j, ref in enumerate(refs[:-1]):
        out[:, j * width : (j + 1) * width] = ref[...].astype(HALF)


def pack_rest_kernel(o_ref, up_ref, down_ref, ou, down, pack):
    width = o_ref.shape[1]
    ou[:, :width] = o_ref[...].astype(HALF)
    ou[:, width:] = up_ref[...].astype(HALF)
    down[...] = down_ref[...].astype(HALF)
    pack[:, : ou.shape[1]] = ou[...]
    pack[:, ou.shape[1] :] = down[...]


def packed(size, qkv, o_turned, up_weight, down_turned):
    if size != 16:
        first = jnp.concatenate(qkv, 1).astype(HALF)
        ou = jnp.concatenate([o_turned, up_weight], 1).astype(HALF)
        return first, ou, down_turned.astype(HALF), None
    rows, units = up_weight.shape
    width = o_turned.shape[1]
    shape = lambda columns: jax.ShapeDtypeStruct((rows, columns), HALF)
    params = pltpu.CompilerParams(vmem_limit_bytes=60 << 20)
    first = pl.pallas_call(
        pack_first_kernel,
        out_shape=shape(3 * width),
        compiler_params=params,
        cost_estimate=SHORT,
        name="pack_first",
    )(*qkv)
    rest = pl.pallas_call(
        pack_rest_kernel,
        out_shape=[shape(width + units), shape(units), shape(width + 2 * units)],
        compiler_params=params,
        cost_estimate=SHORT,
        name="pack_rest",
    )(o_turned, up_weight, down_turned)
    return first, *rest


def join_kernel(where_ref, mine, theirs, out):
    is_mine = pl.program_id(0) * 2 // pl.num_programs(0) == where_ref[1]

    @pl.when(is_mine)
    def _():
        out[...] = mine[...]

    @pl.when(jnp.logical_not(is_mine))
    def _():
        out[...] = theirs[...]


def join(where, mine, theirs):
    rows, columns = mine.shape
    block = rows
    steps = 1

    def spec(other):
        first = lambda w: (w[1] ^ other) * steps
        return pl.BlockSpec(
            (block, columns), lambda i, w: (jnp.clip(i - first(w), 0, steps - 1), 0)
        )

    return pl.pallas_call(
        join_kernel,
        grid_spec=pltpu.PrefetchScalarGridSpec(
            num_scalar_prefetch=1,
            grid=(2 * steps,),
            in_specs=[spec(0), spec(1)],
            out_specs=pl.BlockSpec((block, columns), lambda i, w: (i, 0)),
        ),
        out_shape=jax.ShapeDtypeStruct((2 * rows, columns), HALF),
        compiler_params=pltpu.CompilerParams(vmem_limit_bytes=60 << 20),
        cost_estimate=SHORT,
        name="join",
    )(where, mine, theirs)


def after(array, *others):
    return lax.optimization_barrier((array, *others))[0]


def meet(*arrays):
    return lax.optimization_barrier(arrays)


def cross(array, turn, size):
    pairs = [(2 * i + c, 2 * (i ^ (1 + (c ^ turn))) + c) for i in range(size) for c in (0, 1)]
    return lax.ppermute(array, ("batch", "tensor"), pairs)


class Quad:
    def __init__(self, size, part):
        self.size, self.part = size, part
        self.one = self.two = None

    def first(self):
        if self.size == 16:
            self.one = cross(self.part, 0, self.size)

    def second(self):
        if self.size == 16:
            self.two = cross(jnp.stack([self.part, self.one]), 1, self.size)

    def pieces(self):
        return [self.part, self.one, self.two]

    def moves(self, source, left):
        places = ((0, None, (0, 0, 0)), (1, None, (0, 1, 0)), (2, 0, (0, 0, 1)), (2, 1, (0, 1, 1)))
        return [(source + n, index, left, place) for n, index, place in places]


class Gather:
    def __init__(self, where, size, part, quad=None, left=0):
        self.where, self.size, self.part = where, size, part
        self.quad, self.left = quad, left
        self.came = []

    def over_z(self, *steps):
        if self.size == 16:
            self.came = [*self.came, *(hop(self.part, 4 * z, self.size) for z in steps)]

    def first(self):
        if self.size != 16:
            return self.part
        self.column = jnp.stack(self.came if self.quad else [self.part, *self.came])
        self.came = cross(self.column, 0, self.size)
        return self.column

    def second(self):
        if self.size != 16:
            return self.part
        self.pair = jnp.concatenate([self.column, self.came])
        self.came = cross(self.pair, 1, self.size)
        return self.pair

    def pieces(self):
        if self.size != 16:
            return [lax.all_gather(self.part, "batch", axis=0, tiled=True)]
        return [self.pair, self.came]

    def moves(self):
        if self.size != 16:
            return [(0, None, 0, None)]
        count = self.column.shape[0]
        moves = [
            (n, count * f + j, 0, (j + 4 - count, f, n))
            for n in (0, 1)
            for f in (0, 1)
            for j in range(count)
        ]
        return moves + (self.quad.moves(2, self.left) if self.quad else [])


def own_grad_kernel(counts, where_ref, *refs):
    n = len(counts)
    lefts, rights, received, outs, summed = (
        refs[:n],
        refs[n : 2 * n],
        refs[2 * n : 3 * n],
        refs[3 * n : -1],
        refs[-1],
    )
    step = pl.program_id(0)
    start = 0
    for left, right, got, count in zip(lefts, rights, received, counts):

        @pl.when((step >= start) & (step < start + count))
        def _(left=left, right=right, got=got):
            grads = inner_rows(left[...], right[...]) + got[...].astype(SINGLE)
            summed[...] = grads.astype(HALF)

        start += count
    rows = outs[0].shape[1]
    for j in range(16):
        at = pl.multiple_of(owner(where_ref, j % 4, j // 8, j // 4 % 2) * rows, rows)
        outs[1 - j // 8][j % 8] = summed[pl.ds(at, rows), :]


def own_grad(where, pairs, received):
    rows, depth = pairs[0][0].shape
    widths = [right.shape[1] for _, right in pairs]
    chunk = math.gcd(*widths, 768) if len(widths) == 1 else math.gcd(*widths)
    counts = [width // chunk for width in widths]
    starts = [sum(counts[:j]) for j in range(len(counts))]

    def spec(height, j):
        last = counts[j] - 1
        return pl.BlockSpec(
            (height, chunk), lambda c, m: (0, jnp.clip(c - starts[j], 0, last))
        )

    block = depth // 16
    return pl.pallas_call(
        functools.partial(own_grad_kernel, counts),
        grid_spec=pltpu.PrefetchScalarGridSpec(
            num_scalar_prefetch=1,
            grid=(sum(counts),),
            in_specs=[
                pl.BlockSpec((rows, depth), lambda c, m: (0, 0), pipeline_mode=pl.Buffered(1))
                for _ in pairs
            ]
            + [spec(rows, j) for j in range(len(pairs))]
            + [spec(depth, j) for j in range(len(pairs))],
            out_specs=[pl.BlockSpec((8, block, chunk), lambda c, m: (0, 0, c))] * 2,
            scratch_shapes=[pltpu.VMEM((depth, chunk), HALF)],
        ),
        out_shape=[jax.ShapeDtypeStruct((8, block, sum(widths)), HALF)] * 2,
        compiler_params=pltpu.CompilerParams(vmem_limit_bytes=60 << 20),
        cost_estimate=SHORT,
        name="own_grad",
    )(where, *[left for left, _ in pairs], *[right for _, right in pairs], *received)


class Scatter:
    def __init__(self, where, size, others):
        self.where, self.size = where, size
        self.sent = [inner_rows(left, right).astype(HALF) for left, right in others]
        self.came = [swap(grads) for grads in self.sent]

    def make(self, pairs):
        if self.size != 16:
            parts = [
                inner_rows(*pair) + part.astype(SINGLE) for pair, part in zip(pairs, self.came)
            ]
            self.made = [jnp.concatenate(parts, 1)]
        else:
            self.made = own_grad(self.where, pairs, self.came)
        return self.made

    def first(self):
        self.kept = self.made[-1]
        if self.size == 16:
            self.came = cross(self.made[0], 0, self.size)

    def second(self):
        if self.size != 16:
            return self.kept
        half = self.kept.shape[0] // 2
        sent = self.kept[half:] + self.came[half:]
        self.kept = self.kept[:half] + self.came[:half]
        self.came = cross(sent, 1, self.size)
        return sent

    def near_z(self):
        if self.size != 16:
            return self.kept
        sent = self.kept[1::2] + self.came[1::2]
        self.kept = self.kept[::2] + self.came[::2]
        self.came = hop(sent, 4, self.size)
        return sent

    def far_z(self):
        if self.size != 16:
            return self.kept
        sent = self.kept[1] + self.came[1]
        self.kept = self.kept[0] + self.came[0]
        self.came = [hop(sent, 8, self.size)]
        return sent

    def result(self):
        if self.size != 16:
            return lax.psum_scatter(self.kept, "batch", scatter_dimension=0, tiled=True)
        return sum((a.astype(SINGLE) for a in self.came), self.kept.astype(SINGLE))


class Total:
    def __init__(self, size, mine, theirs):
        self.size, self.sum, self.came = size, mine, swap(theirs)

    def over(self, distance):
        if self.size == 16:
            self.sum = self.sum + self.came
            self.came = hop(self.sum, distance, self.size)

    def over_z(self):
        if self.size == 16:
            self.sum = self.sum + self.came
            self.came = [hop(self.sum, 4 * z, self.size) for z in (1, 2, 3)]

    def result(self):
        if self.size != 16:
            return lax.psum(self.sum + self.came, "batch")
        one, two, three = self.came
        return (self.sum + one) + (two + three)


def per_device(
    size,
    tokens,
    lengths,
    q_weight,
    k_weight,
    v_weight,
    output_weight,
    up_weight,
    down_projection_weight,
    q_bias,
    v_bias,
    o_bias,
    up_bias,
    down_bias,
    gain_first,
    shift_first,
    gain_second,
    shift_second,
    out_grad,
):
    me = lax.axis_index("batch")
    core = lax.axis_index("tensor")
    depth = tokens.shape[1]
    width = q_weight.shape[1]
    units = up_weight.shape[1]
    rows = tokens.shape[0] // 2
    seqs = lengths.shape[0] // 2

    qkv_part, ou_part, down_part, pack = packed(
        size, (q_weight, k_weight, v_weight), output_weight.T, up_weight, down_projection_weight.T
    )
    tokens = lax.dynamic_slice_in_dim(tokens, core * rows, rows)
    cotangent = lax.dynamic_slice_in_dim(out_grad, core * rows, rows)
    lengths = lax.dynamic_slice_in_dim(lengths, core * seqs, seqs)
    biases = jnp.concatenate([q_bias, jnp.zeros_like(q_bias), v_bias, up_bias])
    other_biases = swap(biases)
    qkv_bias = [b[: 3 * width].reshape(1, -1) for b in (biases, other_biases)]
    up_biases = jnp.concatenate([b[3 * width :] for b in (biases, other_biases)]).reshape(1, -1)
    blank = jnp.zeros_like(o_bias)
    vectors = jnp.stack(
        [o_bias, down_bias, gain_first, shift_first, gain_second, shift_second, blank, blank]
    )

    where = jnp.stack([me, core]).astype(jnp.int32)

    quad = Quad(size, pack)
    qkv = Gather(where, size, qkv_part)
    ou = Gather(where, size, ou_part, quad, 0)
    down = Gather(where, size, down_part, quad, ou_part.shape[1])
    qkv.over_z(1, 2, 3)
    quad.first()
    qkv.came, quad.one, ou.part, down.part = meet(qkv.came, quad.one, ou.part, down.part)
    column = qkv.first()
    ou.part, quad.one = after((ou.part, quad.one), column)
    ou.over_z(1, 2, 3)
    quad.second()
    qkv.came, quad.two, ou.came, down.part, tokens, cotangent = meet(
        qkv.came, quad.two, ou.came, down.part, tokens, cotangent
    )
    down.over_z(1, 2, 3)
    pair = qkv.second()
    ou.came = after(ou.came, pair)
    ou.first()
    qkv.came, ou.came, down.came, *rest = meet(
        qkv.came, ou.came, down.came, vectors, qkv_bias, up_biases, where
    )
    vectors, qkv_bias, up_biases, where = rest
    swapped = lambda arrays: [swap(array) for array in arrays]
    qkv_own = qkv.pieces()
    qkv_other = swapped(qkv_own)
    shared = quad.pieces() if size == 16 else []
    shared_other = swapped(shared)
    pair = ou.second()
    column = down.first()
    front_own = attend(
        lengths, where, after(tokens, pair, column), (qkv_own, qkv.moves()), qkv_bias[0], 0
    )
    front_own, ou.came, down.came, qkv_other, shared_other = meet(
        front_own, ou.came, down.came, qkv_other, shared_other
    )
    pair = down.second()
    early = (ou.pair, down.pair) if size == 16 else ()
    early_other = swapped(early)
    front_other = attend(
        lengths, where, after(tokens, pair), (qkv_other, qkv.moves()), qkv_bias[1], 1
    )
    ou_late = [ou.came, swap(ou.came)] if size == 16 else []
    front_other, ou_late, down.came, early_other = meet(
        front_other, ou_late, down.came, early_other
    )
    if size == 16:
        down_late = [down.came, swap(down.came)]
        gathered = [
            ([pair, late, *pieces], moves)
            for lates, moves, pairs in (
                (ou_late, ou.moves(), (ou.pair, early_other[0])),
                (down_late, down.moves(), (down.pair, early_other[1])),
            )
            for pair, late, pieces in zip(pairs, lates, (shared, shared_other))
        ]
    else:
        gathered = []
        for weight in (ou, down):
            own = weight.pieces()
            gathered += [(own, weight.moves()), (swapped(own), weight.moves())]
    qkv_w = (front_own[3], front_other[3])
    mixes = (front_own[1], front_other[1])
    (
        output,
        *acts,
        ugrad_own,
        ugrad_other,
        normed,
        second,
        first,
        mgrad_own,
        mgrad_other,
        vec_sums,
        unit_sums,
    ) = middle(where, mixes, tokens, cotangent, gathered, up_biases, vectors)
    output_came = swap(output)
    down = Scatter(where, size, [(second, acts[1])])
    first = after(first, *down.sent)
    ou = Scatter(where, size, [(first, mixes[1]), (normed, ugrad_other)])
    down.came = after(down.came, *ou.sent)
    made = down.make([(second, acts[0])])
    down.first()
    back_other, bias_other, whole = attend_back(
        lengths, where, front_other[0], front_other[2], after(mgrad_other, *made), tokens
    )
    qkv = Scatter(where, size, [])
    down.came, whole = meet(down.came, whole)
    qkv.came = swap(whole)
    sent = down.second()
    ou.came = after(ou.came, sent)
    ou.make([(first, mixes[0]), (normed, ugrad_own)])
    down.came, ou.made = meet(down.came, ou.made)
    ou.first()
    sent = down.near_z()
    held = after(mgrad_own, sent, *ou.made)
    got = qkv.came if size == 16 else None
    back_own, bias_own, *qkv.made = attend_back(
        lengths, where, front_own[0], front_own[2], held, tokens, got
    )
    if size != 16:
        qkv.made = [qkv.made[0].astype(SINGLE) + qkv.came.astype(SINGLE)]
    shared = vec_sums[:6].reshape(-1)
    small = Total(
        size,
        jnp.concatenate([bias_own[0], unit_sums[0, :units], shared]),
        jnp.concatenate([bias_other[0], unit_sums[0, units:], shared]),
    )
    back_own, qkv.made, down.came, ou.came = meet(back_own, qkv.made, down.came, ou.came)
    qkv.first()
    ou_sent = ou.second()
    small.came = after(small.came, ou_sent)
    small.over(1)
    down_sent = down.far_z()
    tokens_grad = close(
        after(first, ou_sent, down_sent, small.sum), (back_own, back_other), qkv_w
    )
    tokens_grad_came = swap(tokens_grad)
    output = join(where, output, after(output_came, tokens_grad))
    output, qkv.came, ou.came, small.came = meet(output, qkv.came, ou.came, small.came)
    sent = qkv.second()
    small.came, ou.came = after((small.came, ou.came), sent)
    small.over(2)
    sent = ou.near_z()
    down.came = after(down.came, sent)
    down_sum = down.result()
    tokens_grad = after(tokens_grad, sent, small.sum)
    tokens_grad = join(where, tokens_grad, tokens_grad_came)
    qkv.came, down_sum, tokens_grad = meet(qkv.came, down_sum, tokens_grad)
    total = qkv.near_z()
    ou.came = after(ou.came, total)
    sent = ou.far_z()
    small.came = after(small.came, sent)
    small.over_z()
    qkv.came = after(qkv.came, small.sum)
    sent = qkv.far_z()
    small.came = after(small.came, sent)
    small = small.result()
    ou.came = after(ou.came, small)
    ou_sum = ou.result()
    edge = 3 * width + units
    ready = (
        output,
        tokens_grad,
        ou_sum[:, :width].T,
        ou_sum[:, width:],
        down_sum.T,
        small[:width],
        small[2 * width : 3 * width],
        small[3 * width : edge],
        *jnp.split(small[edge:], 6),
    )
    qkv.came, ready = meet(qkv.came, ready)
    qkv_sum = qkv.result()
    output, tokens_grad, o_sum, up_sum, down_sum, q_bias_grad, v_bias_grad, up_bias_grad = ready[:8]
    o_bias_grad, down_bias_grad, gain_1, shift_1, gain_2, shift_2 = ready[8:]
    return (
        output,
        tokens_grad,
        qkv_sum[:, :width],
        qkv_sum[:, width : 2 * width],
        qkv_sum[:, 2 * width :],
        o_sum,
        up_sum,
        down_sum,
        q_bias_grad,
        v_bias_grad,
        o_bias_grad,
        up_bias_grad,
        down_bias_grad,
        gain_1,
        shift_1,
        gain_2,
        shift_2,
    )


def solution(mesh):
    in_specs = (
        P("batch", None),
        P("batch"),
        P("batch", "tensor"),
        P("batch", "tensor"),
        P("batch", "tensor"),
        P("tensor", "batch"),
        P("batch", "tensor"),
        P("tensor", "batch"),
        P("tensor"),
        P("tensor"),
        P(),
        P("tensor"),
        P(),
        P(),
        P(),
        P(),
        P(),
        P("batch", None),
    )
    out_specs = (
        P("batch", None),
        P("batch", None),
        P("batch", "tensor"),
        P("batch", "tensor"),
        P("batch", "tensor"),
        P("tensor", "batch"),
        P("batch", "tensor"),
        P("tensor", "batch"),
        P("tensor"),
        P("tensor"),
        P(),
        P("tensor"),
        P(),
        P(),
        P(),
        P(),
        P(),
    )
    return jax.shard_map(
        functools.partial(per_device, mesh.shape["batch"]),
        mesh=mesh,
        in_specs=in_specs,
        out_specs=out_specs,
        check_vma=False,
    )
```

```python
import functools
import math

import jax
import jax.numpy as jnp
from jax import lax
from jax.experimental import pallas as pl
from jax.experimental.pallas import tpu as pltpu
from jax.sharding import PartitionSpec as P

HEAD_DIM = 64
LANES = 128
BLOCK = 256
CHUNK = 768
EPSILON = 1e-12
NEGATIVE = -1000000000.0
HALF = jnp.bfloat16
SINGLE = jnp.float32
SWAP = ((0, 1), (1, 0))


def matmul(left, right):
    return jnp.dot(left, right, preferred_element_type=SINGLE)


def inner_rows(left, right):
    return lax.dot_general(left, right, (((0,), (0,)), ((), ())), preferred_element_type=SINGLE)


def outer_cols(left, right):
    return lax.dot_general(left, right, (((1,), (1,)), ((), ())), preferred_element_type=SINGLE)


def layer_norm(values, gain, shift):
    center = values - jnp.mean(values, -1, keepdims=True)
    inverse = lax.rsqrt(jnp.mean(center * center, -1, keepdims=True) + EPSILON)
    normal = center * inverse
    return (normal * gain + shift, normal, inverse)


def norm_back(grad, normal, inverse, gain):
    scaled = grad * gain
    inner = (
        scaled
        - jnp.mean(scaled, -1, keepdims=True)
        - normal * jnp.mean(scaled * normal, -1, keepdims=True)
    )
    return inner * inverse


def gelu_parts(upper):
    cdf = 0.5 * (1.0 + lax.erf(upper * (1.0 / math.sqrt(2.0))))
    density = jnp.exp(-0.5 * upper * upper) * (1.0 / math.sqrt(2.0 * math.pi))
    return (upper * cdf, cdf + upper * density)


def clear_at_start(*refs):
    @pl.when(pl.program_id(0) == 0)
    def _():
        for ref in refs:
            ref[...] = jnp.zeros_like(ref)


SHORT = pl.CostEstimate(flops=1000, bytes_accessed=1000, transcendentals=0)


def owner(where_ref, z, first, second, other=0):
    core = where_ref[1] ^ other
    return where_ref[0] ^ (4 * z) ^ (first * (1 + core)) ^ (second * (2 - core))


def bring(where_ref, moves, pieces, out, sems, other):
    rows = out.shape[0] // 16
    copies = []
    for j, (source, index, column, relative) in enumerate(moves):
        piece = pieces[source] if index is None else pieces[source].at[index]
        target = out
        if relative is not None:
            piece = piece.at[:, pl.ds(column, out.shape[1])]
            at = pl.multiple_of(owner(where_ref, *relative, other) * rows, rows)
            target = out.at[pl.ds(at, rows), :]
        copies.append(pltpu.make_async_copy(piece, target, sems.at[j]))
    return copies


def head_sides():
    lane = lax.broadcasted_iota(jnp.int32, (1, LANES), 1)
    first = (lane < HEAD_DIM).astype(SINGLE)
    return (first.astype(HALF), (1.0 - first).astype(HALF))


def attend_kernel(moves, other, len_ref, where_ref, tok_ref, b_ref, *refs):
    pieces, (qkv_ref, mixed_ref, lse_ref, w_ref, sems) = refs[:-5], refs[-5:]

    @pl.when(pl.program_id(0) == 0)
    def _():
        copies = bring(where_ref, moves, pieces, w_ref, sems, other)
        for copy in copies:
            copy.start()
        for copy in copies:
            copy.wait()

    span = tok_ref.shape[0]
    width = mixed_ref.shape[1]
    length = len_ref[pl.program_id(0)]
    qkv_ref[...] = (matmul(tok_ref[...], w_ref[...]) + b_ref[...]).astype(HALF)
    sides = head_sides()
    keep = lax.broadcasted_iota(jnp.int32, (span, span), 0) < length
    upper = lax.broadcasted_iota(jnp.int32, (LANES, 1), 0) < HEAD_DIM
    for pair in range(width // LANES):
        at = LANES * pair
        query = qkv_ref[:, pl.ds(at, LANES)] * HALF(HEAD_DIM**-0.5)
        keys = qkv_ref[:, pl.ds(width + at, LANES)]
        values = qkv_ref[:, pl.ds(2 * width + at, LANES)]
        both = outer_cols(jnp.concatenate([keys * side for side in sides]), query)
        expos, totals = [], []
        for h in range(2):
            scores = jnp.where(keep, both[h * span : (h + 1) * span], NEGATIVE)
            top = jnp.max(scores, 0, keepdims=True)
            expo = jnp.exp(scores - top)
            total = jnp.sum(expo, 0, keepdims=True)
            lse_ref[0, 2 * pair + h : 2 * pair + h + 1, :] = top + jnp.log(total)
            expos.append(expo.astype(HALF))
            totals.append(1.0 / total)
        mixed = inner_rows(
            jnp.concatenate([values * side for side in sides]), jnp.concatenate(expos)
        )
        mixed *= jnp.where(upper, totals[0], totals[1])
        mixed_ref[:, pl.ds(at, LANES)] = mixed.T.astype(HALF)


def attend(lengths, where, tokens, gathered, bias, other):
    pieces, moves = gathered
    rows, depth = tokens.shape
    seqs = lengths.shape[0]
    span = rows // seqs
    width = bias.shape[1] // 3
    heads = width // HEAD_DIM
    return pl.pallas_call(
        functools.partial(attend_kernel, moves, other),
        grid_spec=pltpu.PrefetchScalarGridSpec(
            num_scalar_prefetch=2,
            grid=(seqs,),
            in_specs=[
                pl.BlockSpec((span, depth), lambda i, *_: (i, 0)),
                pl.BlockSpec((1, 3 * width), lambda i, *_: (0, 0)),
            ]
            + [pl.BlockSpec(memory_space=pl.ANY)] * len(pieces),
            out_specs=[
                pl.BlockSpec((span, 3 * width), lambda i, *_: (i, 0)),
                pl.BlockSpec((span, width), lambda i, *_: (i, 0)),
                pl.BlockSpec((1, heads, span), lambda i, *_: (i, 0, 0)),
                pl.BlockSpec((depth, 3 * width), lambda i, *_: (0, 0)),
            ],
            scratch_shapes=[pltpu.SemaphoreType.DMA((len(moves),))],
        ),
        out_shape=[
            jax.ShapeDtypeStruct((rows, 3 * width), HALF),
            jax.ShapeDtypeStruct((rows, width), HALF),
            jax.ShapeDtypeStruct((seqs, heads, span), SINGLE),
            jax.ShapeDtypeStruct((depth, 3 * width), HALF),
        ],
        compiler_params=pltpu.CompilerParams(vmem_limit_bytes=60 << 20),
        cost_estimate=SHORT,
        name="attend",
    )(lengths, where, tokens, bias, *pieces)


WHOLE, BLOCKS = 0, 1


def attend_back_kernel(kind, len_ref, where_ref, qkv_ref, lse_ref, grad_ref, tok_ref, *refs):
    if kind == BLOCKS:
        got_ref, out_ref, bias_ref, sent_ref, kept_ref, summed = refs
    else:
        out_ref, bias_ref, whole_ref, summed = refs
    span, width = grad_ref.shape
    step = pl.program_id(0)
    length = len_ref[step]
    sides = head_sides()
    keep = lax.broadcasted_iota(jnp.int32, (span, span), 0) < length

    clear_at_start(bias_ref, summed)
    for pair in range(width // LANES):
        at = LANES * pair
        query = qkv_ref[:, pl.ds(at, LANES)] * HALF(HEAD_DIM**-0.5)
        keys = qkv_ref[:, pl.ds(width + at, LANES)]
        values = qkv_ref[:, pl.ds(2 * width + at, LANES)]
        grad = grad_ref[:, pl.ds(at, LANES)]
        side_keys = jnp.concatenate([keys * side for side in sides])
        both = outer_cols(side_keys, query)
        both_grads = outer_cols(jnp.concatenate([values * side for side in sides]), grad)
        key_grad = value_grad = 0.0
        score_grads = []
        for h in range(2):
            here = slice(h * span, (h + 1) * span)
            scores = jnp.where(keep, both[here], NEGATIVE)
            probs = jnp.exp(scores - lse_ref[0, 2 * pair + h : 2 * pair + h + 1, :])
            value_grad += matmul(probs.astype(HALF), grad * sides[h])
            prob_grad = both_grads[here]
            delta = jnp.sum(probs * prob_grad, 0, keepdims=True)
            score_grad = (probs * (prob_grad - delta)).astype(HALF)
            key_grad += matmul(score_grad, query * sides[h])
            score_grads.append(score_grad)
        query_grad = inner_rows(side_keys, jnp.concatenate(score_grads))
        query_grad = (query_grad * HEAD_DIM**-0.5).T
        for j, grads in enumerate((query_grad, key_grad, value_grad)):
            out_ref[:, pl.ds(j * width + at, LANES)] = grads.astype(HALF)
            if j != 1:
                bias_ref[:, pl.ds(j * width + at, LANES)] += jnp.sum(grads, 0, keepdims=True)
    for j in range(3):
        here = pl.ds(j * width, width)
        summed[:, here] += inner_rows(tok_ref[...], out_ref[:, here])

    @pl.when(step == pl.num_programs(0) - 1)
    def _():
        if kind == WHOLE:
            whole_ref[...] = summed[...].astype(HALF)
        else:
            summed[...] += got_ref[...].astype(SINGLE)
            rows = sent_ref.shape[1]
            for j in range(16):
                at = pl.multiple_of(owner(where_ref, j % 4, j // 8, j // 4 % 2) * rows, rows)
                target = sent_ref if j >= 8 else kept_ref
                target[j % 8] = summed[pl.ds(at, rows), :].astype(HALF)


def attend_back(lengths, where, qkv, lse, grad, tokens, got=None):
    rows, width = grad.shape
    depth = tokens.shape[1]
    seqs = lengths.shape[0]
    span = rows // seqs
    heads = width // HEAD_DIM
    stay = lambda size: pl.BlockSpec(size, lambda i, *_: (0,) * len(size))
    whole = (depth, 3 * width)
    blocks = (8, depth // 16, 3 * width)
    kind = WHOLE if got is None else BLOCKS
    shapes = [whole] if got is None else [blocks] * 2
    more = () if got is None else (got,)
    return pl.pallas_call(
        functools.partial(attend_back_kernel, kind),
        grid_spec=pltpu.PrefetchScalarGridSpec(
            num_scalar_prefetch=2,
            grid=(seqs,),
            in_specs=[
                pl.BlockSpec((span, 3 * width), lambda i, *_: (i, 0)),
                pl.BlockSpec((1, heads, span), lambda i, *_: (i, 0, 0)),
                pl.BlockSpec((span, width), lambda i, *_: (i, 0)),
                pl.BlockSpec((span, depth), lambda i, *_: (i, 0)),
            ]
            + [stay(whole) for _ in more],
            out_specs=[
                pl.BlockSpec((span, 3 * width), lambda i, *_: (i, 0)),
                stay((1, 3 * width)),
            ]
            + [stay(size) for size in shapes],
            scratch_shapes=[pltpu.VMEM(whole, SINGLE)],
        ),
        out_shape=[
            jax.ShapeDtypeStruct((rows, 3 * width), HALF),
            jax.ShapeDtypeStruct((1, 3 * width), SINGLE),
        ]
        + [jax.ShapeDtypeStruct(size, HALF) for size in shapes],
        compiler_params=pltpu.CompilerParams(vmem_limit_bytes=60 << 20),
        cost_estimate=SHORT,
        name="attend_back",
    )(lengths, where, qkv, lse, grad, tokens, *more)


def middle_kernel(chunk, plans, count, where_ref, mix_a, mix_b, tok_ref, cot_ref, up_bias, vec_ref, *refs):
    pieces, outs, scratch = refs[:count], refs[count:-6], refs[-6:]
    out_ref, act_a, act_b, ugrad_a, ugrad_b, normed_ref, second_ref = outs[:7]
    first_ref, mgrad_a, mgrad_b, vec_grad, up_bias_grad = outs[7:]
    slope_ref, *weights, sems = scratch
    ou_a, ou_b, down_a, down_b = weights
    step = pl.program_id(0)

    def copies(n):
        names, moves, other = plans[n]
        chosen = [pieces[j] for j in names]
        return bring(where_ref, moves, chosen, weights[n], sems.at[n], other)

    def wait_for(*which):
        @pl.when(step == 0)
        def _():
            for n in which:
                for copy in copies(n):
                    copy.wait()

    def start(*which):
        @pl.when(step == 0)
        def _():
            for n in which:
                for copy in copies(n):
                    copy.start()

    start(0, 1)
    clear_at_start(vec_grad, up_bias_grad)
    width = mix_a.shape[1]
    o_bias, down_bias, gain_1, shift_1, gain_2, shift_2 = (
        vec_ref[j : j + 1, :] for j in range(6)
    )
    start(2, 3)
    wait_for(0, 1, 2, 3)
    attention = outer_cols(mix_a[...], ou_a[:, :width])
    attention += outer_cols(mix_b[...], ou_b[:, :width])
    normed, normal_1, inverse_1 = layer_norm(
        tok_ref[...].astype(SINGLE) + attention + o_bias, gain_1, shift_1
    )
    normed_half = normed.astype(HALF)
    normed_ref[...] = normed_half
    units = down_a.shape[1]
    branch = 0.0
    for half, (ou, down, act) in enumerate(((ou_a, down_a, act_a), (ou_b, down_b, act_b))):
        for c in range(units // chunk):
            here = pl.ds(c * chunk, chunk)
            there = pl.ds(half * units + c * chunk, chunk)
            upper = matmul(normed_half, ou[:, pl.ds(width + c * chunk, chunk)])
            active, slope = gelu_parts(upper + up_bias[:, there])
            active = active.astype(HALF)
            act[:, here] = active
            slope_ref[:, there] = slope
            branch += outer_cols(active, down[:, here])
    output, normal_2, inverse_2 = layer_norm(normed + branch + down_bias, gain_2, shift_2)
    out_ref[...] = output.astype(HALF)
    cot = cot_ref[...].astype(SINGLE)
    second = norm_back(cot, normal_2, inverse_2, gain_2)
    second_half = second.astype(HALF)
    second_ref[...] = second_half
    normed_grad = second
    for half, (ou, down, ugrad) in enumerate(((ou_a, down_a, ugrad_a), (ou_b, down_b, ugrad_b))):
        for c in range(units // chunk):
            here = pl.ds(c * chunk, chunk)
            there = pl.ds(half * units + c * chunk, chunk)
            upper_grad = matmul(second_half, down[:, here]) * slope_ref[:, there]
            up_bias_grad[:, there] += jnp.sum(upper_grad, 0, keepdims=True)
            upper_grad = upper_grad.astype(HALF)
            ugrad[:, here] = upper_grad
            normed_grad += outer_cols(upper_grad, ou[:, pl.ds(width + c * chunk, chunk)])
    first = norm_back(normed_grad, normal_1, inverse_1, gain_1)
    first_half = first.astype(HALF)
    first_ref[...] = first_half
    mgrad_a[...] = matmul(first_half, ou_a[:, :width]).astype(HALF)
    mgrad_b[...] = matmul(first_half, ou_b[:, :width]).astype(HALF)
    sums = (first, second, normed_grad * normal_1, normed_grad, cot * normal_2, cot)
    for j, rows in enumerate(sums):
        vec_grad[j : j + 1, :] += jnp.sum(rows, 0, keepdims=True)


def close_kernel(first, grad_a, grad_b, qkv_a, qkv_b, out):
    total = first[...].astype(SINGLE) + outer_cols(grad_a[...], qkv_a[...])
    out[...] = (total + outer_cols(grad_b[...], qkv_b[...])).astype(HALF)


def by_rows(kernel, name, streamed, held, outs, totals=(), pieces=(), scratch=(), where=None):
    rows = streamed[0].shape[0]
    block = math.gcd(rows, BLOCK if not pieces else 2 * BLOCK)
    stream = lambda columns: pl.BlockSpec((block, columns), lambda i, *_: (i, 0))
    shape = jax.ShapeDtypeStruct
    scalars = () if where is None else (where,)
    return pl.pallas_call(
        kernel,
        grid_spec=pltpu.PrefetchScalarGridSpec(
            num_scalar_prefetch=len(scalars),
            grid=(rows // block,),
            in_specs=[stream(a.shape[1]) for a in streamed]
            + [
                pl.BlockSpec(a.shape, lambda i, *_: (0, 0), pipeline_mode=pl.Buffered(1))
                for a in held
            ]
            + [pl.BlockSpec(memory_space=pl.ANY)] * len(pieces),
            out_specs=[stream(columns) for columns in outs]
            + [pl.BlockSpec(size, lambda i, *_: (0, 0)) for size in totals],
            scratch_shapes=scratch,
        ),
        out_shape=[shape((rows, columns), HALF) for columns in outs]
        + [shape(size, SINGLE) for size in totals],
        compiler_params=pltpu.CompilerParams(vmem_limit_bytes=60 << 20),
        cost_estimate=SHORT,
        name=name,
    )(*scalars, *streamed, *held, *pieces)


def middle(where, mixes, tokens, cotangent, gathered, up_bias, vectors):
    depth = tokens.shape[1]
    width = mixes[0].shape[1]
    units = up_bias.shape[1] // 2
    block = math.gcd(tokens.shape[0], 2 * BLOCK)
    pieces, plans = [], []
    for n, (parts, moves) in enumerate(gathered):
        names = []
        for part in parts:
            known = [j for j, piece in enumerate(pieces) if piece is part]
            names.append(known[0] if known else len(pieces))
            if not known:
                pieces.append(part)
        plans.append((names, moves, n % 2))
    most = max(len(moves) for _, moves in gathered)
    held = [pltpu.VMEM((depth, columns), HALF) for columns in (width + units, units) for _ in (0, 1)]
    return by_rows(
        functools.partial(middle_kernel, math.gcd(units, CHUNK), plans, len(pieces)),
        "middle",
        (*mixes, tokens, cotangent),
        (up_bias, vectors),
        [depth] + [units] * 4 + [depth] * 3 + [width] * 2,
        [(8, depth), (1, 2 * units)],
        pieces,
        [pltpu.VMEM((block, 2 * units), SINGLE), *held, pltpu.SemaphoreType.DMA((4, most))],
        where,
    )


def close(first, grads, qkv_halves):
    return by_rows(close_kernel, "close", (first, *grads), qkv_halves, [first.shape[1]])[0]


def swap(array):
    return lax.ppermute(array, "tensor", SWAP)


def hop(array, distance, size):
    return lax.ppermute(array, "batch", [(i, i ^ distance) for i in range(size)])


def pack_first_kernel(*refs):
    out = refs[-1]
    width = refs[0].shape[1]
    for j, ref in enumerate(refs[:-1]):
        out[:, j * width : (j + 1) * width] = ref[...].astype(HALF)


def pack_rest_kernel(o_ref, up_ref, down_ref, ou, down, pack):
    width = o_ref.shape[1]
    ou[:, :width] = o_ref[...].astype(HALF)
    ou[:, width:] = up_ref[...].astype(HALF)
    down[...] = down_ref[...].astype(HALF)
    pack[:, : ou.shape[1]] = ou[...]
    pack[:, ou.shape[1] :] = down[...]


def packed(size, qkv, o_turned, up_weight, down_turned):
    if size != 16:
        first = jnp.concatenate(qkv, 1).astype(HALF)
        ou = jnp.concatenate([o_turned, up_weight], 1).astype(HALF)
        return first, ou, down_turned.astype(HALF), None
    rows, units = up_weight.shape
    width = o_turned.shape[1]
    shape = lambda columns: jax.ShapeDtypeStruct((rows, columns), HALF)
    params = pltpu.CompilerParams(vmem_limit_bytes=60 << 20)
    first = pl.pallas_call(
        pack_first_kernel,
        out_shape=shape(3 * width),
        compiler_params=params,
        cost_estimate=SHORT,
        name="pack_first",
    )(*qkv)
    rest = pl.pallas_call(
        pack_rest_kernel,
        out_shape=[shape(width + units), shape(units), shape(width + 2 * units)],
        compiler_params=params,
        cost_estimate=SHORT,
        name="pack_rest",
    )(o_turned, up_weight, down_turned)
    return first, *rest


def join_kernel(where_ref, mine, theirs, out):
    is_mine = pl.program_id(0) * 2 // pl.num_programs(0) == where_ref[1]

    @pl.when(is_mine)
    def _():
        out[...] = mine[...]

    @pl.when(jnp.logical_not(is_mine))
    def _():
        out[...] = theirs[...]


def join(where, mine, theirs):
    rows, columns = mine.shape
    block = rows
    steps = 1

    def spec(other):
        first = lambda w: (w[1] ^ other) * steps
        return pl.BlockSpec(
            (block, columns), lambda i, w: (jnp.clip(i - first(w), 0, steps - 1), 0)
        )

    return pl.pallas_call(
        join_kernel,
        grid_spec=pltpu.PrefetchScalarGridSpec(
            num_scalar_prefetch=1,
            grid=(2 * steps,),
            in_specs=[spec(0), spec(1)],
            out_specs=pl.BlockSpec((block, columns), lambda i, w: (i, 0)),
        ),
        out_shape=jax.ShapeDtypeStruct((2 * rows, columns), HALF),
        compiler_params=pltpu.CompilerParams(vmem_limit_bytes=60 << 20),
        cost_estimate=SHORT,
        name="join",
    )(where, mine, theirs)


def after(array, *others):
    return lax.optimization_barrier((array, *others))[0]


def meet(*arrays):
    return lax.optimization_barrier(arrays)


def cross(array, turn, size):
    pairs = [(2 * i + c, 2 * (i ^ (1 + (c ^ turn))) + c) for i in range(size) for c in (0, 1)]
    return lax.ppermute(array, ("batch", "tensor"), pairs)


class Quad:
    def __init__(self, size, part):
        self.size, self.part = size, part
        self.one = self.two = None

    def first(self):
        if self.size == 16:
            self.one = cross(self.part, 0, self.size)

    def second(self):
        if self.size == 16:
            self.two = cross(jnp.stack([self.part, self.one]), 1, self.size)

    def pieces(self):
        return [self.part, self.one, self.two]

    def moves(self, source, left):
        places = ((0, None, (0, 0, 0)), (1, None, (0, 1, 0)), (2, 0, (0, 0, 1)), (2, 1, (0, 1, 1)))
        return [(source + n, index, left, place) for n, index, place in places]


class Gather:
    def __init__(self, where, size, part, quad=None, left=0):
        self.where, self.size, self.part = where, size, part
        self.quad, self.left = quad, left
        self.came = []

    def over_z(self, *steps):
        if self.size == 16:
            self.came = [*self.came, *(hop(self.part, 4 * z, self.size) for z in steps)]

    def first(self):
        if self.size != 16:
            return self.part
        self.column = jnp.stack(self.came if self.quad else [self.part, *self.came])
        self.came = cross(self.column, 0, self.size)
        return self.column

    def second(self):
        if self.size != 16:
            return self.part
        self.pair = jnp.concatenate([self.column, self.came])
        self.came = cross(self.pair, 1, self.size)
        return self.pair

    def pieces(self):
        if self.size != 16:
            return [lax.all_gather(self.part, "batch", axis=0, tiled=True)]
        return [self.pair, self.came]

    def moves(self):
        if self.size != 16:
            return [(0, None, 0, None)]
        count = self.column.shape[0]
        moves = [
            (n, count * f + j, 0, (j + 4 - count, f, n))
            for n in (0, 1)
            for f in (0, 1)
            for j in range(count)
        ]
        return moves + (self.quad.moves(2, self.left) if self.quad else [])


def own_grad_kernel(counts, where_ref, *refs):
    n = len(counts)
    lefts, rights, received, outs, summed = (
        refs[:n],
        refs[n : 2 * n],
        refs[2 * n : 3 * n],
        refs[3 * n : -1],
        refs[-1],
    )
    step = pl.program_id(0)
    start = 0
    for left, right, got, count in zip(lefts, rights, received, counts):

        @pl.when((step >= start) & (step < start + count))
        def _(left=left, right=right, got=got):
            grads = inner_rows(left[...], right[...]) + got[...].astype(SINGLE)
            summed[...] = grads.astype(HALF)

        start += count
    rows = outs[0].shape[1]
    for j in range(16):
        at = pl.multiple_of(owner(where_ref, j % 4, j // 8, j // 4 % 2) * rows, rows)
        outs[1 - j // 8][j % 8] = summed[pl.ds(at, rows), :]


def own_grad(where, pairs, received):
    rows, depth = pairs[0][0].shape
    widths = [right.shape[1] for _, right in pairs]
    chunk = math.gcd(*widths, 768) if len(widths) == 1 else math.gcd(*widths)
    counts = [width // chunk for width in widths]
    starts = [sum(counts[:j]) for j in range(len(counts))]

    def spec(height, j):
        last = counts[j] - 1
        return pl.BlockSpec(
            (height, chunk), lambda c, m: (0, jnp.clip(c - starts[j], 0, last))
        )

    block = depth // 16
    return pl.pallas_call(
        functools.partial(own_grad_kernel, counts),
        grid_spec=pltpu.PrefetchScalarGridSpec(
            num_scalar_prefetch=1,
            grid=(sum(counts),),
            in_specs=[
                pl.BlockSpec((rows, depth), lambda c, m: (0, 0), pipeline_mode=pl.Buffered(1))
                for _ in pairs
            ]
            + [spec(rows, j) for j in range(len(pairs))]
            + [spec(depth, j) for j in range(len(pairs))],
            out_specs=[pl.BlockSpec((8, block, chunk), lambda c, m: (0, 0, c))] * 2,
            scratch_shapes=[pltpu.VMEM((depth, chunk), HALF)],
        ),
        out_shape=[jax.ShapeDtypeStruct((8, block, sum(widths)), HALF)] * 2,
        compiler_params=pltpu.CompilerParams(vmem_limit_bytes=60 << 20),
        cost_estimate=SHORT,
        name="own_grad",
    )(where, *[left for left, _ in pairs], *[right for _, right in pairs], *received)


class Scatter:
    def __init__(self, where, size, others):
        self.where, self.size = where, size
        self.sent = [inner_rows(left, right).astype(HALF) for left, right in others]
        self.came = [swap(grads) for grads in self.sent]

    def make(self, pairs):
        if self.size != 16:
            parts = [
                inner_rows(*pair) + part.astype(SINGLE) for pair, part in zip(pairs, self.came)
            ]
            self.made = [jnp.concatenate(parts, 1)]
        else:
            self.made = own_grad(self.where, pairs, self.came)
        return self.made

    def first(self):
        self.kept = self.made[-1]
        if self.size == 16:
            self.came = cross(self.made[0], 0, self.size)

    def second(self):
        if self.size != 16:
            return self.kept
        half = self.kept.shape[0] // 2
        sent = self.kept[half:] + self.came[half:]
        self.kept = self.kept[:half] + self.came[:half]
        self.came = cross(sent, 1, self.size)
        return sent

    def near_z(self):
        if self.size != 16:
            return self.kept
        sent = self.kept[1::2] + self.came[1::2]
        self.kept = self.kept[::2] + self.came[::2]
        self.came = hop(sent, 4, self.size)
        return sent

    def far_z(self):
        if self.size != 16:
            return self.kept
        sent = self.kept[1] + self.came[1]
        self.kept = self.kept[0] + self.came[0]
        self.came = [hop(sent, 8, self.size)]
        return sent

    def result(self):
        if self.size != 16:
            return lax.psum_scatter(self.kept, "batch", scatter_dimension=0, tiled=True)
        return sum((a.astype(SINGLE) for a in self.came), self.kept.astype(SINGLE))


class Total:
    def __init__(self, size, mine, theirs):
        self.size, self.sum, self.came = size, mine, swap(theirs)

    def over(self, distance):
        if self.size == 16:
            self.sum = self.sum + self.came
            self.came = hop(self.sum, distance, self.size)

    def over_z(self):
        if self.size == 16:
            self.sum = self.sum + self.came
            self.came = [hop(self.sum, 4 * z, self.size) for z in (1, 2, 3)]

    def result(self):
        if self.size != 16:
            return lax.psum(self.sum + self.came, "batch")
        one, two, three = self.came
        return (self.sum + one) + (two + three)


def per_device(
    size,
    tokens,
    lengths,
    q_weight,
    k_weight,
    v_weight,
    output_weight,
    up_weight,
    down_projection_weight,
    q_bias,
    v_bias,
    o_bias,
    up_bias,
    down_bias,
    gain_first,
    shift_first,
    gain_second,
    shift_second,
    out_grad,
):
    me = lax.axis_index("batch")
    core = lax.axis_index("tensor")
    depth = tokens.shape[1]
    width = q_weight.shape[1]
    units = up_weight.shape[1]
    rows = tokens.shape[0] // 2
    seqs = lengths.shape[0] // 2

    qkv_part, ou_part, down_part, pack = packed(
        size, (q_weight, k_weight, v_weight), output_weight.T, up_weight, down_projection_weight.T
    )
    tokens = lax.dynamic_slice_in_dim(tokens, core * rows, rows)
    cotangent = lax.dynamic_slice_in_dim(out_grad, core * rows, rows)
    lengths = lax.dynamic_slice_in_dim(lengths, core * seqs, seqs)
    biases = jnp.concatenate([q_bias, jnp.zeros_like(q_bias), v_bias, up_bias])
    other_biases = swap(biases)
    qkv_bias = [b[: 3 * width].reshape(1, -1) for b in (biases, other_biases)]
    up_biases = jnp.concatenate([b[3 * width :] for b in (biases, other_biases)]).reshape(1, -1)
    blank = jnp.zeros_like(o_bias)
    vectors = jnp.stack(
        [o_bias, down_bias, gain_first, shift_first, gain_second, shift_second, blank, blank]
    )

    where = jnp.stack([me, core]).astype(jnp.int32)

    quad = Quad(size, pack)
    qkv = Gather(where, size, qkv_part)
    ou = Gather(where, size, ou_part, quad, 0)
    down = Gather(where, size, down_part, quad, ou_part.shape[1])
    qkv.over_z(1, 2, 3)
    quad.first()
    qkv.came, quad.one, ou.part, down.part = meet(qkv.came, quad.one, ou.part, down.part)
    column = qkv.first()
    ou.part, quad.one = after((ou.part, quad.one), column)
    ou.over_z(1, 2, 3)
    quad.second()
    qkv.came, quad.two, ou.came, down.part, tokens, cotangent = meet(
        qkv.came, quad.two, ou.came, down.part, tokens, cotangent
    )
    down.over_z(1, 2, 3)
    pair = qkv.second()
    ou.came = after(ou.came, pair)
    ou.first()
    qkv.came, ou.came, down.came, *rest = meet(
        qkv.came, ou.came, down.came, vectors, qkv_bias, up_biases, where
    )
    vectors, qkv_bias, up_biases, where = rest
    swapped = lambda arrays: [swap(array) for array in arrays]
    qkv_own = qkv.pieces()
    qkv_other = swapped(qkv_own)
    shared = quad.pieces() if size == 16 else []
    shared_other = swapped(shared)
    pair = ou.second()
    column = down.first()
    front_own = attend(
        lengths, where, after(tokens, pair, column), (qkv_own, qkv.moves()), qkv_bias[0], 0
    )
    front_own, ou.came, down.came, qkv_other, shared_other = meet(
        front_own, ou.came, down.came, qkv_other, shared_other
    )
    pair = down.second()
    early = (ou.pair, down.pair) if size == 16 else ()
    early_other = swapped(early)
    front_other = attend(
        lengths, where, after(tokens, pair), (qkv_other, qkv.moves()), qkv_bias[1], 1
    )
    ou_late = [ou.came, swap(ou.came)] if size == 16 else []
    front_other, ou_late, down.came, early_other = meet(
        front_other, ou_late, down.came, early_other
    )
    if size == 16:
        down_late = [down.came, swap(down.came)]
        gathered = [
            ([pair, late, *pieces], moves)
            for lates, moves, pairs in (
                (ou_late, ou.moves(), (ou.pair, early_other[0])),
                (down_late, down.moves(), (down.pair, early_other[1])),
            )
            for pair, late, pieces in zip(pairs, lates, (shared, shared_other))
        ]
    else:
        gathered = []
        for weight in (ou, down):
            own = weight.pieces()
            gathered += [(own, weight.moves()), (swapped(own), weight.moves())]
    qkv_w = (front_own[3], front_other[3])
    mixes = (front_own[1], front_other[1])
    (
        output,
        *acts,
        ugrad_own,
        ugrad_other,
        normed,
        second,
        first,
        mgrad_own,
        mgrad_other,
        vec_sums,
        unit_sums,
    ) = middle(where, mixes, tokens, cotangent, gathered, up_biases, vectors)
    output_came = swap(output)
    down = Scatter(where, size, [(second, acts[1])])
    first = after(first, *down.sent)
    ou = Scatter(where, size, [(first, mixes[1]), (normed, ugrad_other)])
    down.came = after(down.came, *ou.sent)
    made = down.make([(second, acts[0])])
    down.first()
    back_other, bias_other, whole = attend_back(
        lengths, where, front_other[0], front_other[2], after(mgrad_other, *made), tokens
    )
    qkv = Scatter(where, size, [])
    down.came, whole = meet(down.came, whole)
    qkv.came = swap(whole)
    sent = down.second()
    ou.came = after(ou.came, sent)
    ou.make([(first, mixes[0]), (normed, ugrad_own)])
    down.came, ou.made = meet(down.came, ou.made)
    ou.first()
    sent = down.near_z()
    held = after(mgrad_own, sent, *ou.made)
    got = qkv.came if size == 16 else None
    back_own, bias_own, *qkv.made = attend_back(
        lengths, where, front_own[0], front_own[2], held, tokens, got
    )
    if size != 16:
        qkv.made = [qkv.made[0].astype(SINGLE) + qkv.came.astype(SINGLE)]
    shared = vec_sums[:6].reshape(-1)
    small = Total(
        size,
        jnp.concatenate([bias_own[0], unit_sums[0, :units], shared]),
        jnp.concatenate([bias_other[0], unit_sums[0, units:], shared]),
    )
    back_own, qkv.made, down.came, ou.came = meet(back_own, qkv.made, down.came, ou.came)
    qkv.first()
    ou_sent = ou.second()
    small.came = after(small.came, ou_sent)
    small.over(1)
    down_sent = down.far_z()
    tokens_grad = close(
        after(first, ou_sent, down_sent, small.sum), (back_own, back_other), qkv_w
    )
    tokens_grad_came = swap(tokens_grad)
    output = join(where, output, after(output_came, tokens_grad))
    output, qkv.came, ou.came, small.came = meet(output, qkv.came, ou.came, small.came)
    sent = qkv.second()
    small.came, ou.came = after((small.came, ou.came), sent)
    small.over(2)
    sent = ou.near_z()
    down.came = after(down.came, sent)
    down_sum = down.result()
    tokens_grad = after(tokens_grad, sent, small.sum)
    tokens_grad = join(where, tokens_grad, tokens_grad_came)
    qkv.came, down_sum, tokens_grad = meet(qkv.came, down_sum, tokens_grad)
    total = qkv.near_z()
    ou.came = after(ou.came, total)
    sent = ou.far_z()
    small.came = after(small.came, sent)
    small.over_z()
    qkv.came = after(qkv.came, small.sum)
    sent = qkv.far_z()
    small.came = after(small.came, sent)
    small = small.result()
    ou.came = after(ou.came, small)
    ou_sum = ou.result()
    edge = 3 * width + units
    ready = (
        output,
        tokens_grad,
        ou_sum[:, :width].T,
        ou_sum[:, width:],
        down_sum.T,
        small[:width],
        small[2 * width : 3 * width],
        small[3 * width : edge],
        *jnp.split(small[edge:], 6),
    )
    qkv.came, ready = meet(qkv.came, ready)
    qkv_sum = qkv.result()
    output, tokens_grad, o_sum, up_sum, down_sum, q_bias_grad, v_bias_grad, up_bias_grad = ready[:8]
    o_bias_grad, down_bias_grad, gain_1, shift_1, gain_2, shift_2 = ready[8:]
    return (
        output,
        tokens_grad,
        qkv_sum[:, :width],
        qkv_sum[:, width : 2 * width],
        qkv_sum[:, 2 * width :],
        o_sum,
        up_sum,
        down_sum,
        q_bias_grad,
        v_bias_grad,
        o_bias_grad,
        up_bias_grad,
        down_bias_grad,
        gain_1,
        shift_1,
        gain_2,
        shift_2,
    )


def solution(mesh):
    in_specs = (
        P("batch", None),
        P("batch"),
        P("batch", "tensor"),
        P("batch", "tensor"),
        P("batch", "tensor"),
        P("tensor", "batch"),
        P("batch", "tensor"),
        P("tensor", "batch"),
        P("tensor"),
        P("tensor"),
        P(),
        P("tensor"),
        P(),
        P(),
        P(),
        P(),
        P(),
        P("batch", None),
    )
    out_specs = (
        P("batch", None),
        P("batch", None),
        P("batch", "tensor"),
        P("batch", "tensor"),
        P("batch", "tensor"),
        P("tensor", "batch"),
        P("batch", "tensor"),
        P("tensor", "batch"),
        P("tensor"),
        P("tensor"),
        P(),
        P("tensor"),
        P(),
        P(),
        P(),
        P(),
        P(),
    )
    return jax.shard_map(
        functools.partial(per_device, mesh.shape["batch"]),
        mesh=mesh,
        in_specs=in_specs,
        out_specs=out_specs,
        check_vma=False,
    )
```
